128 devices in a mesh: fsdp: 32 (over y, z, core), dp: 4 (over x).
Axes of the slice: x: 4, y: 4, z: 4, core: 2. Of those that a mesh axis runs over, the one named last changes fastest.
Arguments:
- tokens: bfloat16 [512, 202, 768], P(('fsdp', 'dp')), may hold values from -6 to 6
- lengths: int32 [512], P(('fsdp', 'dp')), may hold values from 10 to 202, as said below
- feature_proj: bfloat16 [64, 32], replicated, may hold values from -0.75 to 0.75
- ln1_gain: bfloat16 [768], P('fsdp'), may hold values from 0.5 to 1.5
- ln1_bias: bfloat16 [768], P('fsdp'), may hold values from -1 to 1
- w_query: bfloat16 [768, 768], P('fsdp'), may hold values from -0.21875 to 0.21875
- b_query: bfloat16 [768], P('fsdp'), may hold values from -1 to 1
- w_key: bfloat16 [768, 768], P('fsdp'), may hold values from -0.21875 to 0.21875
- b_key: bfloat16 [768], P('fsdp'), may hold values from -1 to 1
- w_value: bfloat16 [768, 768], P('fsdp'), may hold values from -0.21875 to 0.21875
- b_value: bfloat16 [768], P('fsdp'), may hold values from -1 to 1
- w_out: bfloat16 [768, 768], P('fsdp'), may hold values from -1.75 to 1.75
- b_out: bfloat16 [768], P('fsdp'), may hold values from -1 to 1
- ln2_gain: bfloat16 [768], P('fsdp'), may hold values from 0.5 to 1.5
- ln2_bias: bfloat16 [768], P('fsdp'), may hold values from -1 to 1
- w_up: bfloat16 [768, 3072], P('fsdp'), may hold values from -0.21875 to 0.21875
- b_up: bfloat16 [3072], P('fsdp'), may hold values from -1 to 1
- w_down: bfloat16 [3072, 768], P('fsdp'), may hold values from -0.109375 to 0.109375
- b_down: bfloat16 [768], P('fsdp'), may hold values from -1 to 1
- cotangent: bfloat16 [512, 202, 768], P(('fsdp', 'dp')), may hold values from -24 to 24
Outputs:
- layer_out: bfloat16 [512, 202, 768], P(('fsdp', 'dp'))
- grad_tokens: bfloat16 [512, 202, 768], P(('fsdp', 'dp'))
- grad_ln1_gain: float32 [768], P('fsdp')
- grad_ln1_bias: float32 [768], P('fsdp')
- grad_w_query: float32 [768, 768], P('fsdp')
- grad_b_query: float32 [768], P('fsdp')
- grad_w_key: float32 [768, 768], P('fsdp')
- grad_b_key: float32 [768], P('fsdp')
- grad_w_value: float32 [768, 768], P('fsdp')
- grad_b_value: float32 [768], P('fsdp')
- grad_w_out: float32 [768, 768], P('fsdp')
- grad_b_out: float32 [768], P('fsdp')
- grad_ln2_gain: float32 [768], P('fsdp')
- grad_ln2_bias: float32 [768], P('fsdp')
- grad_w_up: float32 [768, 3072], P('fsdp')
- grad_b_up: float32 [3072], P('fsdp')
- grad_w_down: float32 [3072, 768], P('fsdp')
- grad_b_down: float32 [768], P('fsdp')
The draws below stay inside these ranges and needn't reach their ends.
Inputs may be any that keep to these rules, and one draw needn't show every extreme that they name: `lengths`: every molecule has 10 to 202 tokens, and at least one has exactly 202.
All inputs are finite; a program needn't handle non-finite values.
Results may differ from the reference program's by a relative error of at most 0.024.
Values may be sent and summed in bfloat16 or wider, within the bound.
A program may use at most 192 MiB of HBM per device.

```python
import jax
import jax.numpy as jnp
from jax import lax

D = 768
HEADS = 12
HEAD = 64
FF = 3072
FEATS = 32
MAXLEN = 202
MINLEN = 10
MOLS_DEV = 4
MOLS = 512


def draw_lengths(key, part):
    key = jax.random.fold_in(key, 7)
    first_key, second_key = jax.random.split(key)
    drawn_lengths = jax.random.randint(first_key, (MOLS,), MINLEN, MAXLEN + 1, dtype=jnp.int32)
    chosen = jax.random.randint(second_key, (), 0, MOLS, dtype=jnp.int32)
    return jnp.where(jnp.arange(MOLS, dtype=jnp.int32) == chosen, MAXLEN, drawn_lengths).astype(jnp.int32)


def strengthened(drawn, own_key, source, target, blocks, factor):
    owner, partner = [(jnp.arange(drawn.shape[axis_at]) // (drawn.shape[axis_at] // blocks)).reshape([-1 if axis == axis_at else 1 for axis in range(drawn.ndim)]) for axis_at in (source, target)]
    chosen = jax.random.permutation(own_key, blocks)[partner]
    strong = (owner == chosen) | (owner == (partner + blocks // 2) % blocks)
    return jnp.where(strong, factor * drawn, drawn)


def block_levels(stream_key, extent, shards, smallest, largest):
    factor_of = 1.0
    for position, blocks in shards:
        heights = jax.random.uniform(jax.random.fold_in(jax.random.fold_in(stream_key, 6), position), (blocks,), jnp.float32, smallest / len(shards), largest / len(shards))
        factor_of = factor_of * jnp.repeat(jnp.exp(heights), extent[position] // blocks).reshape((-1,) + (1,) * (len(extent) - 1 - position))
    return factor_of


def gaussian(key, shape, width, reach, shards=(), held_as=jnp.bfloat16):
    level = block_levels(key, shape, shards, -0.22, 0.18) if shards else 1.0
    values = jax.random.normal(key, shape, jnp.float32) * width * level
    return jnp.minimum(jnp.maximum(values, -reach), reach).astype(held_as)


def heavy_noise(key, dims, scale, reach, cuts, heavy, kind=jnp.bfloat16):
    drawn = scale * jax.random.normal(key, dims, jnp.float32)
    if cuts:
        drawn = drawn * block_levels(key, dims, cuts, -0.22, 0.18)
    return jnp.clip(strengthened(drawn, jax.random.fold_in(key, 3), *heavy), -reach, reach).astype(kind)


def setup_inputs(seed: int = 0) -> dict:
    streams_of = jax.random.split(jax.random.key(seed), 21)
    tokens = gaussian(streams_of[0], (MOLS, MAXLEN, D), 1.0, 6.0, ((0, 128),))
    lengths = draw_lengths(jax.random.fold_in(streams_of[20], 71), 0)
    feature_proj = gaussian(streams_of[2], (HEAD, FEATS), HEAD ** -0.5, 0.75)
    ln1_gain = jnp.clip(1.0 + 0.1 * jax.random.normal(streams_of[3], (D,), jnp.float32), 0.5, 1.5).astype(jnp.bfloat16)
    ln1_bias = gaussian(streams_of[4], (D,), 0.2, 1.0, ((0, 32),))
    w_query = gaussian(streams_of[5], (D, D), D ** -0.5, 0.21875, ((0, 32),))
    b_query = gaussian(streams_of[6], (D,), 0.2, 1.0, ((0, 32),))
    w_key = gaussian(streams_of[7], (D, D), D ** -0.5, 0.21875, ((0, 32),))
    b_key = gaussian(streams_of[8], (D,), 0.2, 1.0, ((0, 32),))
    w_value = gaussian(streams_of[9], (D, D), D ** -0.5, 0.21875, ((0, 32),))
    b_value = gaussian(streams_of[10], (D,), 0.2, 1.0, ((0, 32),))
    w_out = gaussian(streams_of[11], (D, D), (D // 64) ** -0.5, 1.75, ((0, 32),))
    b_out = gaussian(streams_of[12], (D,), 0.2, 1.0, ((0, 32),))
    ln2_gain = jnp.clip(1.0 + 0.1 * jax.random.normal(streams_of[13], (D,), jnp.float32), 0.5, 1.5).astype(jnp.bfloat16)
    ln2_bias = gaussian(streams_of[14], (D,), 0.2, 1.0, ((0, 32),))
    w_up = gaussian(streams_of[15], (D, FF), D ** -0.5, 0.21875, ((0, 32),))
    b_up = gaussian(streams_of[16], (FF,), 0.2, 1.0, ((0, 32),))
    w_down = gaussian(streams_of[17], (FF, D), FF ** -0.5, 0.109375, ((0, 32),))
    b_down = gaussian(streams_of[18], (D,), 0.2, 1.0, ((0, 32),))
    cotangent = heavy_noise(streams_of[19], (MOLS, MAXLEN, D), 1.0, 24.0, ((0, 128),), (0, 2, 128, 5.5))
    return {"tokens": tokens, "lengths": lengths, "feature_proj": feature_proj, "ln1_gain": ln1_gain, "ln1_bias": ln1_bias, "w_query": w_query, "b_query": b_query, "w_key": w_key, "b_key": b_key, "w_value": w_value, "b_value": b_value, "w_out": w_out, "b_out": b_out, "ln2_gain": ln2_gain, "ln2_bias": ln2_bias, "w_up": w_up, "b_up": b_up, "w_down": w_down, "b_down": b_down, "cotangent": cotangent}


@jax.custom_vjp
def low(v):
    return lax.optimization_barrier(v.astype(jnp.bfloat16)).astype(jnp.float32)

@jax.custom_vjp
def low_back(v):
    return v

def low_keep(v):
    return (low(v), None)

def low_pass(kept, grad):
    return (grad,)

def back_keep(v):
    return (v, None)

def back_low(kept, grad):
    return (low(grad),)
low.defvjp(low_keep, low_pass)
low_back.defvjp(back_keep, back_low)
EPS_NORM = 1e-05
EPS_ATTN = 1e-06
HIGH = lax.Precision.HIGHEST

def normalize(inputs, gain, shift):
    centre = inputs - lax.optimization_barrier(jnp.mean(inputs, axis=-1, keepdims=True))
    scale = lax.rsqrt(lax.optimization_barrier(jnp.mean(centre * centre, axis=-1, keepdims=True)) + EPS_NORM)
    return centre * scale * gain + shift

def attend(query, key_rows, value_rows, projection, key_mask):
    mol_count, slot_count = key_mask.shape
    model_width = query.shape[-1]
    head_size = model_width // HEADS
    half_size = head_size // 2
    positions = jnp.arange(slot_count).astype(jnp.float32)
    frequency = 10000.0 ** (jnp.arange(half_size).astype(jnp.float32) * (-2.0 / head_size))
    angles = positions[:, None] * frequency[None, :]
    cosines = jnp.cos(angles)[None, :, None, :]
    sines = jnp.sin(angles)[None, :, None, :]

    def turned(rows_in):
        heads_in = rows_in.reshape(mol_count, slot_count, HEADS, head_size)
        low_half = heads_in[..., :half_size]
        high_half = heads_in[..., half_size:]
        return jnp.concatenate([low_half * cosines - high_half * sines, high_half * cosines + low_half * sines], axis=-1)
    feat_query = jax.nn.softplus(jnp.einsum('gshd,df->gshf', turned(query), projection, precision=HIGH))
    feat_key = jax.nn.softplus(jnp.einsum('gshd,df->gshf', turned(key_rows), projection, precision=HIGH))
    feat_key = feat_key * key_mask[:, :, None, None]
    value_heads = value_rows.reshape(mol_count, slot_count, HEADS, head_size)
    kv_state = jnp.einsum('gshf,gshd->ghfd', feat_key, value_heads, precision=HIGH)
    feature_sum = lax.optimization_barrier(jnp.sum(feat_key, axis=1))
    numerator = jnp.einsum('gshf,ghfd->gshd', feat_query, kv_state, precision=HIGH)
    denominator = jnp.einsum('gshf,ghf->gsh', feat_query, feature_sum, precision=HIGH) + EPS_ATTN
    return (numerator / denominator[..., None]).reshape(mol_count * slot_count, model_width)

def gelu_tanh(values):
    return jax.nn.gelu(values, approximate=True)

def layer(params, inputs, key_mask, row_mask, projection):
    ln1_gain, ln1_bias, w_query, b_query, w_key, b_key, w_value, b_value, w_out, b_out, ln2_gain, ln2_bias, w_up, b_up, w_down, b_down = params
    mol_count, slot_count, model_width = inputs.shape
    flat_rows = inputs.reshape(mol_count * slot_count, model_width)
    normed_one = low(normalize(flat_rows, ln1_gain, ln1_bias))
    query = low_back(jnp.dot(normed_one, w_query, precision=HIGH) + b_query)
    key_rows = low_back(jnp.dot(normed_one, w_key, precision=HIGH) + b_key)
    value_rows = low_back(jnp.dot(normed_one, w_value, precision=HIGH) + b_value)
    mixed = low(attend(query, key_rows, value_rows, projection, key_mask))
    branch = low_back(jnp.dot(mixed, w_out, precision=HIGH) + b_out)
    middle = flat_rows + branch
    normed_two = low(normalize(middle, ln2_gain, ln2_bias))
    pre_act = low_back(jnp.dot(normed_two, w_up, precision=HIGH) + b_up)
    hidden = low(gelu_tanh(pre_act))
    branch_two = low_back(jnp.dot(hidden, w_down, precision=HIGH) + b_down)
    result = (middle + branch_two) * row_mask.reshape(-1, 1)
    return result.reshape(mol_count, slot_count, model_width)

def to_float(array_in):
    return array_in.astype(jnp.float32)

def reference(tokens, lengths, feature_proj, ln1_gain, ln1_bias, w_query, b_query, w_key, b_key, w_value, b_value, w_out, b_out, ln2_gain, ln2_bias, w_up, b_up, w_down, b_down, cotangent):
    params = jax.tree.map(to_float, (ln1_gain, ln1_bias, w_query, b_query, w_key, b_key, w_value, b_value, w_out, b_out, ln2_gain, ln2_bias, w_up, b_up, w_down, b_down))
    projection = feature_proj.astype(jnp.float32)
    positions = jnp.arange(MAXLEN, dtype=jnp.int32)
    batch_most = lax.optimization_barrier(jnp.max(lengths.reshape(MOLS // MOLS_DEV, MOLS_DEV), axis=1))
    padded = jnp.repeat(batch_most, MOLS_DEV)
    key_mask = (positions[None, :] < lengths[:, None]).astype(jnp.float32)
    row_mask = (positions[None, :] < padded[:, None]).astype(jnp.float32)
    per_block = 16
    block_count = MOLS // per_block

    def split(array_in):
        return array_in.reshape((block_count, per_block) + array_in.shape[1:])
    zero_grads = jax.tree.map(jnp.zeros_like, params)

    def step(carry, block):
        inputs, key_block, row_block, grad_block = block

        def forward(weights_all, inputs_all):
            return layer(weights_all, inputs_all, key_block, row_block, projection)
        outputs, pullback = jax.vjp(forward, params, inputs)
        grad_params, grad_inputs = pullback(grad_block)
        return (jax.tree.map(jnp.add, carry, grad_params), (outputs, grad_inputs))
    grads, (outputs, grad_inputs) = lax.scan(step, zero_grads, (split(tokens.astype(jnp.float32)), split(key_mask), split(row_mask), split(cotangent.astype(jnp.float32))))
    layer_out = outputs.reshape(MOLS, MAXLEN, D).astype(jnp.bfloat16)
    grad_tokens = grad_inputs.reshape(MOLS, MAXLEN, D).astype(jnp.bfloat16)
    return (layer_out, grad_tokens, grads[0], grads[1], grads[2], grads[3], grads[4], grads[5], grads[6], grads[7], grads[8], grads[9], grads[10], grads[11], grads[12], grads[13], grads[14], grads[15])
```

```python
from functools import partial

import jax
import jax.numpy as jnp
from jax import lax
from jax.experimental import pallas as pl
from jax.experimental.pallas import tpu as pltpu
from jax.sharding import PartitionSpec as P

HEADS = 12


MESH = pl.DeviceIdType.MESH
RING = 4
BLK = 48
WID = 768
HALF = 384
ALL = pl.ds(0, RING)


def rounded(value):
    return value.astype(jnp.bfloat16)


def wide(value):
    return value.astype(jnp.float32)


class Net:
    def __init__(self, send_sems, recv_sems):
        self.send_sems, self.recv_sems, self.count, self.open = send_sems, recv_sems, 0, []
        index = lax.axis_index("fsdp")
        self.x = lax.axis_index("dp")
        self.y = index // (2 * RING)
        self.z = (index // 2) % RING
        self.c = index % 2

    def at(self, y, z, c):
        return {"fsdp": ((y + RING) % RING) * (2 * RING) + ((z + RING) % RING) * 2 + c}

    def sibling(self):
        return self.at(self.y, self.z, 1 - self.c)

    def along(self, axis, step):
        if axis == "y":
            return self.at(self.y + step, self.z, self.c)
        if axis == "z":
            return self.at(self.y, self.z + step, self.c)
        return {"dp": (self.x + step) % RING}

    def greet(self):
        barrier = pltpu.get_barrier_semaphore()
        peers = [self.sibling()] + [
            self.along(axis, step) for axis in ("x", "y", "z") for step in (1, 2, 3)
        ]
        for peer in peers:
            pl.semaphore_signal(barrier, inc=1, device_id=peer, device_id_type=MESH)
        pl.semaphore_wait(barrier, len(peers))

    def send(self, src, dst, device):
        slot = self.count
        self.count += 1
        copy = pltpu.make_async_remote_copy(
            src_ref=src,
            dst_ref=dst,
            send_sem=self.send_sems.at[slot],
            recv_sem=self.recv_sems.at[slot],
            device_id=device,
            device_id_type=MESH,
        )
        copy.start()
        self.open.append(copy)
        return slot

    def arrived(self, slot, land):
        pltpu.make_async_remote_copy(
            src_ref=land,
            dst_ref=land,
            send_sem=self.send_sems.at[slot],
            recv_sem=self.recv_sems.at[slot],
            device_id=self.sibling(),
            device_id_type=MESH,
        ).wait_recv()

    def settle(self):
        for copy in self.open:
            copy.wait_send()
        self.open = []

    def axes(self, way):
        return ("y", "z") if way == 0 else ("z", "y")

    def place(self, way):
        return (self.y, self.z) if way == 0 else (self.z, self.y)


def wrap(index):
    return (index + RING) % RING


def slot_of(ref, part, way, core, first, second):
    y, z = (first, second) if way == 0 else (second, first)
    piece = 2 * core + way
    if part < 2:
        return ref.at[4 * part + piece, y, z]
    if not isinstance(y, pl.Slice):
        return ref.at[8 + y, z, piece]
    return ref.at[pl.ds(8, RING), z, piece]


def half(ref, side):
    lead = (slice(None),) * (len(ref.shape) - 1)
    return ref.at[lead + (pl.ds(side * HALF, HALF),)]


def gather_steps(net, weights, part):
    ways = (0, 1)
    sent = {}

    def slot(way, first, second, core=None):
        return slot_of(weights, part, way, net.c if core is None else core, first, second)

    for way in ways:
        p, q = net.place(way)
        axis = net.axes(way)[0]
        own = slot(way, p, q)
        sent[way, "r"] = net.send(own, own, net.along(axis, 1))
        sent[way, "l"] = net.send(own, own, net.along(axis, -1))
    yield
    for way in ways:
        p, q = net.place(way)
        axis = net.axes(way)[0]
        left = slot(way, wrap(p - 1), q)
        net.arrived(sent[way, "r"], left)
        sent[way, "fr"] = net.send(half(left, 0), half(left, 0), net.along(axis, 1))
        right = slot(way, wrap(p + 1), q)
        net.arrived(sent[way, "l"], right)
        sent[way, "fl"] = net.send(half(right, 1), half(right, 1), net.along(axis, -1))
    yield
    for way in ways:
        p, q = net.place(way)
        axis = net.axes(way)[1]
        far = slot(way, wrap(p + 2), q)
        net.arrived(sent[way, "fr"], half(far, 0))
        net.arrived(sent[way, "fl"], half(far, 1))
        row = slot(way, ALL, q)
        sent[way, "r2"] = net.send(row, row, net.along(axis, 1))
        sent[way, "l2"] = net.send(row, row, net.along(axis, -1))
        sent[way, "s0"] = net.send(row, row, net.sibling())
    yield
    for way in ways:
        p, q = net.place(way)
        axis = net.axes(way)[1]
        left = slot(way, ALL, wrap(q - 1))
        net.arrived(sent[way, "r2"], left)
        sent[way, "fr2"] = net.send(half(left, 0), half(left, 0), net.along(axis, 1))
        sent[way, "s1"] = net.send(left, left, net.sibling())
        right = slot(way, ALL, wrap(q + 1))
        net.arrived(sent[way, "l2"], right)
        sent[way, "fl2"] = net.send(half(right, 1), half(right, 1), net.along(axis, -1))
        sent[way, "s2"] = net.send(right, right, net.sibling())
    yield
    for way in ways:
        p, q = net.place(way)
        far = slot(way, ALL, wrap(q + 2))
        net.arrived(sent[way, "fr2"], half(far, 0))
        net.arrived(sent[way, "fl2"], half(far, 1))
        sent[way, "s3"] = net.send(far, far, net.sibling())
    yield
    for way in ways:
        p, q = net.place(way)
        other = 1 - net.c
        for name, step in (("s0", 0), ("s1", -1), ("s2", 1), ("s3", 2)):
            net.arrived(sent[way, name], slot(way, ALL, wrap(q + step), other))


def gather_small(net, small):
    own = small.at[net.y, net.z]
    sent = [net.send(own, own, net.along("y", step)) for step in (1, 2, 3)]
    yield
    for slot, step in zip(sent, (1, 2, 3)):
        net.arrived(slot, small.at[wrap(net.y - step), net.z])
    row = small.at[ALL, net.z]
    sent = [net.send(row, row, net.along("z", step)) for step in (1, 2, 3)]
    yield
    for slot, step in zip(sent, (1, 2, 3)):
        net.arrived(slot, small.at[ALL, wrap(net.z - step)])


def load_shards(net, weights, small, mine, theirs, small_mine, shards):
    queries, keys, values, outs, ups, downs, packed = shards
    first = net.c == 0
    rows = pl.ds(pl.multiple_of(24 * net.c, 8), 24)

    def lane(piece):
        return pl.ds(pl.multiple_of(WID * piece, WID), WID)

    for way in (0, 1):
        early, late = ((queries, values), (keys, outs))[way]
        early, late = wide(early[...]), wide(late[...])
        mine[way, rows] = jnp.where(first, early, late)
        theirs[way] = jnp.where(first, late, early)
        mine[2 + way, rows] = wide(ups[:, lane(2 * net.c + way)])
        theirs[2 + way] = wide(ups[:, lane(2 - 2 * net.c + way)])
    small_mine[rows] = wide(packed[...])
    sent = net.send(theirs, mine.at[ALL, rows], net.sibling())
    sent_small = net.send(small_mine.at[rows], small_mine.at[rows], net.sibling())
    for way in (0, 1):
        weights[8 + net.y, net.z, 2 * net.c + way] = downs[pl.ds(BLK * way, BLK)]
    others = pl.ds(pl.multiple_of(24 - 24 * net.c, 8), 24)
    net.arrived(sent_small, small_mine.at[others])
    small[net.y, net.z] = rounded(small_mine[...])
    net.arrived(sent, mine.at[ALL, others])
    for part in (0, 1):
        for way in (0, 1):
            weights[4 * part + 2 * net.c + way, net.y, net.z] = rounded(mine[2 * part + way])


def add_blocks(target, source):
    if len(target.shape) == 2:
        target[...] = rounded(wide(target[...]) + wide(source[...]))
        return
    for index in range(target.shape[0]):
        add_blocks(target.at[index], source.at[index])


def add_two(target, one, two):
    if len(target.shape) == 2:
        target[...] = rounded(wide(target[...]) + wide(one[...]) + wide(two[...]))
        return
    for index in range(target.shape[0]):
        add_two(target.at[index], one.at[index], two.at[index])


def ring_reduce(net, group, land, axis, me):
    ahead, behind, far = wrap(me + 1), wrap(me - 1), wrap(me + 2)
    right, left = net.along(axis, 1), net.along(axis, -1)
    one_r = net.send(half(group(far), 0), land.at[0], right)
    one_l = net.send(half(group(far), 1), land.at[1], left)
    two_r = net.send(half(group(ahead), 1), land.at[2], right)
    two_l = net.send(half(group(behind), 0), land.at[3], left)
    yield
    net.arrived(one_r, land.at[0])
    add_blocks(half(group(ahead), 0), land.at[0])
    three_r = net.send(half(group(ahead), 0), land.at[4], right)
    net.arrived(one_l, land.at[1])
    add_blocks(half(group(behind), 1), land.at[1])
    three_l = net.send(half(group(behind), 1), land.at[5], left)
    yield
    net.arrived(two_r, land.at[2])
    net.arrived(three_l, land.at[5])
    add_two(half(group(me), 1), land.at[2], land.at[5])
    net.arrived(two_l, land.at[3])
    net.arrived(three_r, land.at[4])
    add_two(half(group(me), 0), land.at[3], land.at[4])


def together(*steps):
    steps = list(steps)
    while steps:
        steps = [step for step in steps if next(step, steps) is not steps]
        if steps:
            yield


def reduce_steps(net, grads, part, pair, big, little, cross, total, result):
    ways = (0, 1)

    def slot(way, first, second):
        return slot_of(grads, part, way, net.c, first, second)

    def whole(way, core):
        if part < 2:
            return grads.at[4 * part + 2 * core + way]
        return grads.at[pl.ds(8, RING), ALL, 2 * core + way]

    sent = [net.send(whole(way, 1 - net.c), pair.at[way], net.sibling()) for way in ways]
    yield
    for way in ways:
        net.arrived(sent[way], pair.at[way])
        for index in range(RING):
            add_blocks(whole(way, net.c).at[index], pair.at[way, index])
    yield from together(
        *[
            ring_reduce(
                net,
                lambda at, way=way: slot(way, ALL, at),
                big.at[way],
                net.axes(way)[1],
                net.place(way)[1],
            )
            for way in ways
        ]
    )
    yield
    yield from together(
        *[
            ring_reduce(
                net,
                lambda at, way=way: slot(way, at, net.place(way)[1]),
                little.at[way],
                net.axes(way)[0],
                net.place(way)[0],
            )
            for way in ways
        ]
    )
    sent = {}
    for way in ways:
        cross[way, net.x] = slot(way, *net.place(way))[...]
        for step in (1, 2, 3):
            mine = cross.at[way, net.x]
            sent[way, step] = net.send(mine, mine, net.along("x", step))
    yield
    for way in ways:
        for step in (1, 2, 3):
            net.arrived(sent[way, step], cross.at[way, wrap(net.x - step)])
        total[way] = (
            (wide(cross[way, 0]) + wide(cross[way, 1])) + wide(cross[way, 2])
        ) + wide(cross[way, 3])
    if part == 2:
        for way in ways:
            result[pl.ds(BLK * way, BLK)] = total[way]
        return
    sent = []
    for way in ways:
        mine = result.at[2 * net.c + way]
        result[2 * net.c + way] = total[way, pl.ds(pl.multiple_of(24 * net.c, 8), 24)]
        sent.append(
            net.send(
                total.at[way, pl.ds(pl.multiple_of(24 - 24 * net.c, 8), 24)], mine, net.sibling()
            )
        )
    yield
    for way in ways:
        net.arrived(sent[way], result.at[2 - 2 * net.c + way])


def vector_steps(net, vectors, land):
    sent = net.send(vectors, land.at[0, 0], net.sibling())
    yield
    net.arrived(sent, land.at[0, 0])
    value = vectors[...] + land[0, 0]
    for stage, axis, me in ((1, "z", net.z), (2, "y", net.y), (3, "x", net.x)):
        land[stage, me] = value
        mine = land.at[stage, me]
        sent = [net.send(mine, mine, net.along(axis, step)) for step in (1, 2, 3)]
        yield
        for step in (1, 2, 3):
            net.arrived(sent[step - 1], land.at[stage, wrap(me - step)])
        value = ((land[stage, 0] + land[stage, 1]) + land[stage, 2]) + land[stage, 3]
    land[0, 1] = value

VMEM = pl.BlockSpec(memory_space=pltpu.VMEM)
ANY = pl.BlockSpec(memory_space=pl.ANY)


def gather_kernel(
    queries, keys, values, outs, ups, downs, packed, weights_out, small_out,
    weights, small, mine, theirs, small_mine, send_sems, recv_sems, local_sem,
):
    net = Net(send_sems, recv_sems)
    net.greet()
    load_shards(net, weights, small, mine, theirs, small_mine, (queries, keys, values, outs, ups, downs, packed))
    steps = together(gather_small(net, small), *[gather_steps(net, weights, part) for part in (0, 1, 2)])
    for _ in steps:
        pass
    net.settle()
    copy = pltpu.make_async_copy(weights, weights_out, local_sem.at[0])
    copy.start()
    copy_small = pltpu.make_async_copy(small, small_out, local_sem.at[1])
    copy_small.start()
    copy.wait()
    copy_small.wait()


def gather_call(*shards):
    bf = jnp.bfloat16
    return pl.pallas_call(
        gather_kernel,
        out_shape=(
            jax.ShapeDtypeStruct((12, 4, 4, 48, 768), bf),
            jax.ShapeDtypeStruct((4, 4, 48, 128), bf),
        ),
        in_specs=[VMEM] * 7,
        out_specs=(ANY, ANY),
        scratch_shapes=[
            pltpu.VMEM((12, 4, 4, 48, 768), bf),
            pltpu.VMEM((4, 4, 48, 128), bf),
            pltpu.VMEM((4, 48, 768), jnp.float32),
            pltpu.VMEM((4, 24, 768), jnp.float32),
            pltpu.VMEM((48, 128), jnp.float32),
            pltpu.SemaphoreType.DMA((128,)),
            pltpu.SemaphoreType.DMA((128,)),
            pltpu.SemaphoreType.DMA((2,)),
        ],
        compiler_params=pltpu.CompilerParams(
            collective_id=0, has_side_effects=True, vmem_limit_bytes=60 * 2**20
        ),
    )(*shards)


def reduce_kernel(
    terms, vectors_in, out_square, out_up, out_down, out_vectors,
    grads, vectors, pair, big, little, cross, total, land, square, up, down,
    send_sems, recv_sems, local_sem,
):
    net = Net(send_sems, recv_sems)
    copy = pltpu.make_async_copy(terms, grads, local_sem.at[0])
    copy.start()
    vectors[...] = vectors_in[...]
    net.greet()
    copy.wait()
    steps = [
        reduce_steps(net, grads, part, pair.at[part], big.at[part], little.at[part], cross.at[part], total.at[part], result)
        for part, result in ((2, down), (1, up), (0, square))
    ]
    for _ in together(vector_steps(net, vectors, land), *steps):
        pass
    net.settle()
    out_square[...] = square[...]
    out_up[...] = up[...]
    out_down[...] = down[...]
    out_vectors[...] = land[0, 1]


def reduce_call(terms, vectors):
    bf, ff = jnp.bfloat16, jnp.float32
    return pl.pallas_call(
        reduce_kernel,
        out_shape=(
            jax.ShapeDtypeStruct((4, 24, 768), ff),
            jax.ShapeDtypeStruct((4, 24, 768), ff),
            jax.ShapeDtypeStruct((96, 768), ff),
            jax.ShapeDtypeStruct((16, 768), ff),
        ),
        in_specs=[ANY, VMEM],
        out_specs=(VMEM, VMEM, VMEM, VMEM),
        scratch_shapes=[
            pltpu.VMEM((12, 4, 4, 48, 768), bf),
            pltpu.VMEM((16, 768), ff),
            pltpu.VMEM((3, 2, 4, 4, 48, 768), bf),
            pltpu.VMEM((3, 2, 6, 4, 48, 384), bf),
            pltpu.VMEM((3, 2, 6, 48, 384), bf),
            pltpu.VMEM((3, 2, 4, 48, 768), bf),
            pltpu.VMEM((3, 2, 48, 768), ff),
            pltpu.VMEM((4, 4, 16, 768), ff),
            pltpu.VMEM((4, 24, 768), ff),
            pltpu.VMEM((4, 24, 768), ff),
            pltpu.VMEM((96, 768), ff),
            pltpu.SemaphoreType.DMA((128,)),
            pltpu.SemaphoreType.DMA((128,)),
            pltpu.SemaphoreType.DMA((2,)),
        ],
        compiler_params=pltpu.CompilerParams(
            collective_id=1, has_side_effects=True, vmem_limit_bytes=60 * 2**20
        ),
    )(terms, vectors)


EPS_NORM = 1e-05
EPS_ATTN = 1e-06
HIGH = lax.Precision.HIGHEST


def normalize(inputs, gain, shift):
    centre = inputs - jnp.mean(inputs, axis=-1, keepdims=True)
    scale = lax.rsqrt(jnp.mean(centre * centre, axis=-1, keepdims=True) + EPS_NORM)
    return centre * scale * gain + shift


def attend(query, key_rows, value_rows, projection, key_mask):
    mol_count, slot_count = key_mask.shape
    model_width = query.shape[-1]
    head_size = model_width // HEADS
    half_size = head_size // 2
    positions = jnp.arange(slot_count).astype(jnp.float32)
    frequency = 10000.0 ** (jnp.arange(half_size).astype(jnp.float32) * (-2.0 / head_size))
    angles = positions[:, None] * frequency[None, :]
    cosines = jnp.cos(angles)[None, :, None, :]
    sines = jnp.sin(angles)[None, :, None, :]

    def turned(rows_in):
        heads_in = rows_in.reshape(mol_count, slot_count, HEADS, head_size)
        low_half = heads_in[..., :half_size]
        high_half = heads_in[..., half_size:]
        return jnp.concatenate(
            [low_half * cosines - high_half * sines, high_half * cosines + low_half * sines],
            axis=-1,
        )

    feat_query = jax.nn.softplus(
        jnp.einsum("gshd,df->gshf", turned(query), projection, precision=HIGH)
    )
    feat_key = jax.nn.softplus(
        jnp.einsum("gshd,df->gshf", turned(key_rows), projection, precision=HIGH)
    )
    feat_key = feat_key * key_mask[:, :, None, None]
    value_heads = value_rows.reshape(mol_count, slot_count, HEADS, head_size)
    kv_state = jnp.einsum("gshf,gshd->ghfd", feat_key, value_heads, precision=HIGH)
    feature_sum = jnp.sum(feat_key, axis=1)
    numerator = jnp.einsum("gshf,ghfd->gshd", feat_query, kv_state, precision=HIGH)
    denominator = jnp.einsum("gshf,ghf->gsh", feat_query, feature_sum, precision=HIGH) + EPS_ATTN
    return (numerator / denominator[..., None]).reshape(mol_count * slot_count, model_width)


def gelu_tanh(values):
    return jax.nn.gelu(values, approximate=True)


def matmul(left, right):
    return jnp.dot(left, right, preferred_element_type=jnp.float32)


def outer_product(left, right):
    return lax.dot_general(
        left, right, (((0,), (0,)), ((), ())), preferred_element_type=jnp.float32
    )


def times_transpose(left, right):
    return lax.dot_general(
        left, right, (((1,), (1,)), ((), ())), preferred_element_type=jnp.float32
    )


def column_sums(rows_in):
    return jnp.sum(rows_in.astype(jnp.float32), axis=0)


def body(
    tokens,
    lengths,
    feature_proj,
    ln1_gain,
    ln1_bias,
    w_query,
    b_query,
    w_key,
    b_key,
    w_value,
    b_value,
    w_out,
    b_out,
    ln2_gain,
    ln2_bias,
    w_up,
    b_up,
    w_down,
    b_down,
    cotangent,
):
    packed = jnp.stack(
        [ln1_gain, ln1_bias, b_query, b_key, b_value, b_out, ln2_gain, ln2_bias, b_down]
        + [b_up[24 * k : 24 * k + 24] for k in range(4)],
        axis=1,
    )
    packed = jnp.pad(packed, ((0, 0), (0, 128 - 13)))
    weights, small = gather_call(w_query, w_key, w_value, w_out, w_up, w_down, packed)
    small = small.reshape(768, 128)
    squares = weights.reshape(12, 768, 768)
    full_up = jnp.concatenate([squares[4], squares[5], squares[6], squares[7]], axis=1)
    full_down = squares[8:].reshape(3072, 768)
    full_b_up = small[:, 9:13].reshape(32, 24, 4).transpose(0, 2, 1).reshape(3072)
    gathered = regathered = (
        small[:, 0], small[:, 1], squares[0], small[:, 2], squares[1], small[:, 3], squares[2], small[:, 4],
        squares[3], small[:, 5], small[:, 6], small[:, 7], full_up, full_b_up, full_down, small[:, 8],
    )
    mol_count, slot_count, model_width = tokens.shape
    projection = feature_proj.astype(jnp.float32)
    positions = jnp.arange(slot_count, dtype=jnp.int32)
    batch_most = jnp.max(lengths)
    key_mask = (positions[None, :] < lengths[:, None]).astype(jnp.float32)
    row_flat = jnp.broadcast_to(
        (positions < batch_most).astype(jnp.float32)[None, :], (mol_count, slot_count)
    ).reshape(-1)
    gain_one = gathered[0].astype(jnp.float32)
    shift_one = gathered[1].astype(jnp.float32)
    gain_two = gathered[10].astype(jnp.float32)
    shift_two = gathered[11].astype(jnp.float32)
    flat_rows = tokens.reshape(-1, model_width).astype(jnp.float32)
    normed_one, pull_one = jax.vjp(normalize, flat_rows, gain_one, shift_one)
    lowered_one = normed_one.astype(jnp.bfloat16)
    query = matmul(lowered_one, gathered[2]) + gathered[3].astype(jnp.float32)
    key_rows = matmul(lowered_one, gathered[4]) + gathered[5].astype(jnp.float32)
    value_rows = matmul(lowered_one, gathered[6]) + gathered[7].astype(jnp.float32)
    mixed, pull_attn = jax.vjp(
        partial(attend, projection=projection, key_mask=key_mask), query, key_rows, value_rows
    )
    mixed_low = mixed.astype(jnp.bfloat16)
    middle = flat_rows + matmul(mixed_low, gathered[8]) + gathered[9].astype(jnp.float32)
    normed_two, pull_two = jax.vjp(normalize, middle, gain_two, shift_two)
    lowered_two = normed_two.astype(jnp.bfloat16)
    pre_act = matmul(lowered_two, gathered[12]) + gathered[13].astype(jnp.float32)
    activated, pull_gelu = jax.vjp(gelu_tanh, pre_act)
    hidden = activated.astype(jnp.bfloat16)
    result = (middle + matmul(hidden, gathered[14]) + gathered[15].astype(jnp.float32)) * row_flat[
        :, None
    ]
    layer_out = result.astype(jnp.bfloat16).reshape(tokens.shape)
    grad_out = cotangent.reshape(-1, model_width).astype(jnp.float32) * row_flat[:, None]
    grad_down = grad_out.astype(jnp.bfloat16)
    term_w_down = outer_product(hidden, grad_down)
    term_b_down = column_sums(grad_down)
    grad_hidden = times_transpose(grad_down, regathered[14])
    (grad_pre,) = pull_gelu(grad_hidden)
    grad_pre_low = grad_pre.astype(jnp.bfloat16)
    term_w_up = outer_product(lowered_two, grad_pre_low)
    term_b_up = column_sums(grad_pre_low)
    grad_two = times_transpose(grad_pre_low, regathered[12])
    grad_mid_norm, term_ln2_gain, term_ln2_bias = pull_two(grad_two)
    grad_middle = grad_out + grad_mid_norm
    grad_branch = grad_middle.astype(jnp.bfloat16)
    term_w_out = outer_product(mixed_low, grad_branch)
    term_b_out = column_sums(grad_branch)
    grad_mixed = times_transpose(grad_branch, regathered[8])
    grad_query, grad_key, grad_value = pull_attn(grad_mixed)
    query_low = grad_query.astype(jnp.bfloat16)
    key_low = grad_key.astype(jnp.bfloat16)
    value_low = grad_value.astype(jnp.bfloat16)
    term_w_query = outer_product(lowered_one, query_low)
    term_b_query = column_sums(query_low)
    term_w_key = outer_product(lowered_one, key_low)
    term_b_key = column_sums(key_low)
    term_w_value = outer_product(lowered_one, value_low)
    term_b_value = column_sums(value_low)
    grad_one = (
        times_transpose(query_low, regathered[2])
        + times_transpose(key_low, regathered[4])
        + times_transpose(value_low, regathered[6])
    )
    grad_in_norm, term_ln1_gain, term_ln1_bias = pull_one(grad_one)
    grad_tokens = (grad_middle + grad_in_norm).astype(jnp.bfloat16).reshape(tokens.shape)
    low = lambda v: v.astype(jnp.bfloat16)
    terms = jnp.concatenate(
        [low(term_w_query)[None], low(term_w_key)[None], low(term_w_value)[None], low(term_w_out)[None]]
        + [low(term_w_up[:, 768 * j : 768 * j + 768])[None] for j in range(4)]
        + [low(term_w_down).reshape(4, 768, 768)],
        axis=0,
    ).reshape(12, 4, 4, 48, 768)
    vectors = jnp.stack(
        [term_ln1_gain, term_ln1_bias, term_b_query, term_b_key, term_b_value, term_b_out,
         term_ln2_gain, term_ln2_bias, term_b_down]
        + [term_b_up[768 * j : 768 * j + 768] for j in range(4)]
        + [jnp.zeros_like(term_b_out)] * 3
    )
    square, up, down, vectors = reduce_call(terms, vectors)
    index = lax.axis_index("fsdp")
    narrow = lax.dynamic_slice(vectors, (0, 24 * index), (9, 24))
    grad_b_up = lax.dynamic_slice(vectors[9:13].reshape(3072), (96 * index,), (96,))
    return (
        layer_out, grad_tokens, narrow[0], narrow[1], square[0], narrow[2], square[1], narrow[3], square[2], narrow[4],
        square[3], narrow[5], narrow[6], narrow[7], up.transpose(1, 0, 2).reshape(24, 3072), grad_b_up, down, narrow[8],
    )


def solution(mesh):
    placed = (
        P(("fsdp", "dp"), None, None),
        P(("fsdp", "dp")),
        P(),
        P("fsdp"),
        P("fsdp"),
        P("fsdp", None),
        P("fsdp"),
        P("fsdp", None),
        P("fsdp"),
        P("fsdp", None),
        P("fsdp"),
        P("fsdp", None),
        P("fsdp"),
        P("fsdp"),
        P("fsdp"),
        P("fsdp", None),
        P("fsdp"),
        P("fsdp", None),
        P("fsdp"),
        P(("fsdp", "dp"), None, None),
    )
    return jax.shard_map(
        body,
        mesh=mesh,
        in_specs=placed,
        out_specs=(
            P(("fsdp", "dp"), None, None),
            P(("fsdp", "dp"), None, None),
            P("fsdp"),
            P("fsdp"),
            P("fsdp", None),
            P("fsdp"),
            P("fsdp", None),
            P("fsdp"),
            P("fsdp", None),
            P("fsdp"),
            P("fsdp", None),
            P("fsdp"),
            P("fsdp"),
            P("fsdp"),
            P("fsdp", None),
            P("fsdp"),
            P("fsdp", None),
            P("fsdp"),
        ),
        check_vma=False,
    )
```

```python
import jax
import jax.numpy as jnp
import numpy as np
from jax import lax
from jax.experimental import pallas as pl
from jax.experimental.pallas import tpu as pltpu
from jax.sharding import PartitionSpec as P


MESH = pl.DeviceIdType.MESH
RING = 4
BLK = 48
WID = 768
HALF = 384
ALL = pl.ds(0, RING)


def rounded(value):
    return value.astype(jnp.bfloat16)


def wide(value):
    return value.astype(jnp.float32)


class Net:
    def __init__(self, send_sems, recv_sems):
        self.marks = {}
        self.send_sems, self.recv_sems, self.count, self.open = send_sems, recv_sems, 0, []
        index = lax.axis_index("fsdp")
        self.x = lax.axis_index("dp")
        self.y = index // (2 * RING)
        self.z = (index // 2) % RING
        self.c = index % 2

    def at(self, y, z, c):
        return {"fsdp": ((y + RING) % RING) * (2 * RING) + ((z + RING) % RING) * 2 + c}

    def sibling(self):
        return self.at(self.y, self.z, 1 - self.c)

    def along(self, axis, step):
        if axis == "y":
            return self.at(self.y + step, self.z, self.c)
        if axis == "z":
            return self.at(self.y, self.z + step, self.c)
        return {"dp": (self.x + step) % RING}

    def greet(self):
        barrier = pltpu.get_barrier_semaphore()
        peers = [self.sibling()] + [
            self.along(axis, step) for axis in ("x", "y", "z") for step in (1, 2, 3)
        ]
        for peer in peers:
            pl.semaphore_signal(barrier, inc=1, device_id=peer, device_id_type=MESH)
        pl.semaphore_wait(barrier, len(peers))

    def send(self, src, dst, device):
        slot = self.count
        self.count += 1
        copy = pltpu.make_async_remote_copy(
            src_ref=src,
            dst_ref=dst,
            send_sem=self.send_sems.at[slot],
            recv_sem=self.recv_sems.at[slot],
            device_id=device,
            device_id_type=MESH,
        )
        copy.start()
        self.open.append(copy)
        return slot

    def arrived(self, slot, land):
        pltpu.make_async_remote_copy(
            src_ref=land,
            dst_ref=land,
            send_sem=self.send_sems.at[slot],
            recv_sem=self.recv_sems.at[slot],
            device_id=self.sibling(),
            device_id_type=MESH,
        ).wait_recv()

    def settle(self):
        for copy in self.open:
            copy.wait_send()
        self.open = []

    def partners(self):
        near = [self.along(axis, step) for axis in ("y", "z") for step in (1, -1)]
        return [self.sibling()] + near + [self.along("x", step) for step in (1, 2, 3)]

    def axes(self, way):
        return ("y", "z") if way == 0 else ("z", "y")

    def place(self, way):
        return (self.y, self.z) if way == 0 else (self.z, self.y)


def wrap(index):
    return (index + RING) % RING


def base_of(ref, part):
    return 4 * part if ref.shape[0] == 12 else 4 * (part % 2)


def slot_of(ref, part, way, core, first, second):
    y, z = (first, second) if way == 0 else (second, first)
    piece = 2 * core + way
    base = base_of(ref, part)
    if part < 2:
        return ref.at[base + piece, y, z]
    if not isinstance(y, pl.Slice):
        return ref.at[base + y, z, piece]
    return ref.at[pl.ds(base, RING), z, piece]


def half(ref, side):
    lead = (slice(None),) * (len(ref.shape) - 1)
    return ref.at[lead + (pl.ds(side * HALF, HALF),)]


def gather_steps(net, weights, part):
    ways = (0, 1)
    sent = {}

    def slot(way, first, second, core=None):
        return slot_of(weights, part, way, net.c if core is None else core, first, second)

    for way in ways:
        p, q = net.place(way)
        axis = net.axes(way)[0]
        own = slot(way, p, q)
        sent[way, "r"] = net.send(own, own, net.along(axis, 1))
        sent[way, "l"] = net.send(own, own, net.along(axis, -1))
    yield
    for way in ways:
        p, q = net.place(way)
        axis = net.axes(way)[0]
        left = slot(way, wrap(p - 1), q)
        net.arrived(sent[way, "r"], left)
        sent[way, "fr"] = net.send(half(left, 0), half(left, 0), net.along(axis, 1))
        right = slot(way, wrap(p + 1), q)
        net.arrived(sent[way, "l"], right)
        sent[way, "fl"] = net.send(half(right, 1), half(right, 1), net.along(axis, -1))
    yield
    for way in ways:
        p, q = net.place(way)
        axis = net.axes(way)[1]
        far = slot(way, wrap(p + 2), q)
        net.arrived(sent[way, "fr"], half(far, 0))
        net.arrived(sent[way, "fl"], half(far, 1))
        row = slot(way, ALL, q)
        sent[way, "r2"] = net.send(row, row, net.along(axis, 1))
        sent[way, "l2"] = net.send(row, row, net.along(axis, -1))
        sent[way, "s0"] = net.send(row, row, net.sibling())
    yield
    for way in ways:
        p, q = net.place(way)
        axis = net.axes(way)[1]
        left = slot(way, ALL, wrap(q - 1))
        net.arrived(sent[way, "r2"], left)
        sent[way, "fr2"] = net.send(half(left, 0), half(left, 0), net.along(axis, 1))
        sent[way, "s1"] = net.send(left, left, net.sibling())
        right = slot(way, ALL, wrap(q + 1))
        net.arrived(sent[way, "l2"], right)
        sent[way, "fl2"] = net.send(half(right, 1), half(right, 1), net.along(axis, -1))
        sent[way, "s2"] = net.send(right, right, net.sibling())
    yield
    for way in ways:
        p, q = net.place(way)
        far = slot(way, ALL, wrap(q + 2))
        net.arrived(sent[way, "fr2"], half(far, 0))
        net.arrived(sent[way, "fl2"], half(far, 1))
        sent[way, "s3"] = net.send(far, far, net.sibling())
    yield
    for way in ways:
        p, q = net.place(way)
        other = 1 - net.c
        for name, step in (("s0", 0), ("s1", -1), ("s2", 1), ("s3", 2)):
            net.arrived(sent[way, name], slot(way, ALL, wrap(q + step), other))


def gather_small(net, small):
    own = small.at[net.y, net.z]
    sent = [net.send(own, own, net.along("y", step)) for step in (1, 2, 3)]
    yield
    for slot, step in zip(sent, (1, 2, 3)):
        net.arrived(slot, small.at[wrap(net.y - step), net.z])
    row = small.at[ALL, net.z]
    sent = [net.send(row, row, net.along("z", step)) for step in (1, 2, 3)]
    yield
    for slot, step in zip(sent, (1, 2, 3)):
        net.arrived(slot, small.at[ALL, wrap(net.z - step)])


def load_shards(net, weights, small, stage, small_mine, shards):
    queries, keys, values, outs, ups, downs, packed = shards
    first = net.c == 0

    def rows(slot, core):
        return pl.ds(pl.multiple_of(BLK * slot + 24 * core, 8), 24)

    def lane(piece):
        return pl.ds(pl.multiple_of(WID * piece, WID), WID)

    def exchange(slot, mine, theirs):
        outgoing = pl.ds(4 * BLK + 24 * slot, 24)
        stage[rows(slot, net.c)] = mine
        stage[outgoing] = theirs
        return net.send(stage.at[outgoing], stage.at[rows(slot, net.c)], net.sibling())

    source, target = iota((24, HALF), 1), iota((24, HALF), 0)
    spread = jnp.broadcast_to(wide(packed[...]), (24, HALF)) * flag(source % 24 == target)
    pick = rounded(flag(iota((HALF, 128), 0) // 24 == iota((HALF, 128), 1)))
    small_mine[rows(0, net.c)] = dot(rounded(spread), pick)
    sent_small = net.send(small_mine.at[rows(0, net.c)], small_mine.at[rows(0, net.c)], net.sibling())
    sent = []
    for way in (0, 1):
        early, late = ((queries, values), (keys, outs))[way]
        early, late = wide(early[...]), wide(late[...])
        sent.append(exchange(way, jnp.where(first, early, late), jnp.where(first, late, early)))
    for way in (0, 1):
        near, away = 2 * net.c + way, 2 - 2 * net.c + way
        sent.append(exchange(2 + way, wide(ups[:, lane(near)]), wide(ups[:, lane(away)])))
    for way in (0, 1):
        weights[8 + net.y, net.z, 2 * net.c + way] = downs[pl.ds(BLK * way, BLK)]
    yield
    net.arrived(sent_small, small_mine.at[rows(0, 1 - net.c)])
    small[net.y, net.z] = rounded(small_mine[...])
    for slot in (0, 1, 2, 3):
        if slot == 2:
            yield
        net.arrived(sent[slot], stage.at[rows(slot, 1 - net.c)])
        piece = 4 * (slot // 2) + 2 * net.c + slot % 2
        weights[piece, net.y, net.z] = rounded(stage[pl.ds(BLK * slot, BLK)])


def add_blocks(target, source):
    if len(target.shape) == 2:
        target[...] = rounded(wide(target[...]) + wide(source[...]))
        return
    for index in range(target.shape[0]):
        add_blocks(target.at[index], source.at[index])


def add_two(target, one, two):
    if len(target.shape) == 2:
        target[...] = rounded(wide(target[...]) + wide(one[...]) + wide(two[...]))
        return
    for index in range(target.shape[0]):
        add_two(target.at[index], one.at[index], two.at[index])


def ring_reduce(net, group, land, axis, me):
    ahead, behind, far = wrap(me + 1), wrap(me - 1), wrap(me + 2)
    right, left = net.along(axis, 1), net.along(axis, -1)
    one_r = net.send(half(group(far), 0), land.at[0], right)
    one_l = net.send(half(group(far), 1), land.at[1], left)
    two_r = net.send(half(group(ahead), 1), land.at[2], right)
    two_l = net.send(half(group(behind), 0), land.at[3], left)
    yield
    net.arrived(one_r, land.at[0])
    add_blocks(half(group(ahead), 0), land.at[0])
    three_r = net.send(half(group(ahead), 0), land.at[4], right)
    net.arrived(one_l, land.at[1])
    add_blocks(half(group(behind), 1), land.at[1])
    three_l = net.send(half(group(behind), 1), land.at[5], left)
    yield
    net.arrived(two_r, land.at[2])
    net.arrived(three_l, land.at[5])
    add_two(half(group(me), 1), land.at[2], land.at[5])
    net.arrived(two_l, land.at[3])
    net.arrived(three_r, land.at[4])
    add_two(half(group(me), 0), land.at[3], land.at[4])


def together(*steps):
    steps = list(steps)
    while steps:
        steps = [step for step in steps if next(step, steps) is not steps]
        if steps:
            yield


def strip(result, part, piece):
    if part == 0:
        return result.at[piece]
    return result.at[:, pl.ds(pl.multiple_of(WID * piece, WID), WID)]


def reduce_steps(net, grads, part, pair, pair_credit, big, little, cross, total, result):
    ways = (0, 1)

    def slot(way, first, second):
        return slot_of(grads, part, way, net.c, first, second)

    def whole(way, core):
        if part < 2:
            return grads.at[base_of(grads, part) + 2 * core + way]
        return grads.at[pl.ds(base_of(grads, part), RING), ALL, 2 * core + way]

    if part != 2:
        pl.semaphore_wait(pair_credit, 1)
    sent = [net.send(whole(way, 1 - net.c), pair.at[way], net.sibling()) for way in ways]
    yield
    for way in ways:
        net.arrived(sent[way], pair.at[way])
        for index in range(RING):
            add_blocks(whole(way, net.c).at[index], pair.at[way, index])
    if part != 0:
        pl.semaphore_signal(pair_credit, inc=1, device_id=net.sibling(), device_id_type=MESH)
    yield from together(
        *[
            ring_reduce(
                net,
                lambda at, way=way: slot(way, ALL, at),
                big.at[way],
                net.axes(way)[1],
                net.place(way)[1],
            )
            for way in ways
        ]
    )
    yield
    yield from together(
        *[
            ring_reduce(
                net,
                lambda at, way=way: slot(way, at, net.place(way)[1]),
                little.at[way],
                net.axes(way)[0],
                net.place(way)[0],
            )
            for way in ways
        ]
    )
    sent = {}
    for way in ways:
        cross[way, net.x] = slot(way, *net.place(way))[...]
        for step in (1, 2, 3):
            mine = cross.at[way, net.x]
            sent[way, step] = net.send(mine, mine, net.along("x", step))
    yield
    for way in ways:
        for step in (1, 2, 3):
            net.arrived(sent[way, step], cross.at[way, wrap(net.x - step)])
        target = result.at[pl.ds(BLK * way, BLK)] if part == 2 else total.at[way]
        target[...] = (
            (wide(cross[way, 0]) + wide(cross[way, 1])) + wide(cross[way, 2])
        ) + wide(cross[way, 3])
    if part == 2:
        return
    sent = []
    for way in ways:
        mine = strip(result, part, 2 * net.c + way)
        mine[...] = total[way, pl.ds(pl.multiple_of(24 * net.c, 8), 24)]
        sent.append(
            net.send(
                total.at[way, pl.ds(pl.multiple_of(24 - 24 * net.c, 8), 24)], mine, net.sibling()
            )
        )
    yield
    for way in ways:
        net.arrived(sent[way], strip(result, part, 2 - 2 * net.c + way))


def vector_steps(net, vectors, land):
    sent = net.send(vectors, land.at[0, 0], net.sibling())
    yield
    net.arrived(sent, land.at[0, 0])
    value = vectors[...] + land[0, 0]
    for stage, axis, me in ((1, "z", net.z), (2, "y", net.y), (3, "x", net.x)):
        land[stage, me] = value
        mine = land.at[stage, me]
        sent = [net.send(mine, mine, net.along(axis, step)) for step in (1, 2, 3)]
        yield
        for step in (1, 2, 3):
            net.arrived(sent[step - 1], land.at[stage, wrap(me - step)])
        value = ((land[stage, 0] + land[stage, 1]) + land[stage, 2]) + land[stage, 3]
    land[0, 1] = value

ROWS = 202
PAD = 208
MOLS = 4
TOTAL = MOLS * PAD
GROUPS = 3
LANES = 256
FEAT = 128
EPS_NORM = 1e-05
EPS_ATTN = 1e-06
GELU_SCALE = 0.7978845608028654
GELU_CUBIC = 0.044715


def dot(left, right):
    return jnp.dot(left, right, preferred_element_type=jnp.float32)


def dot_nt(left, right):
    return lax.dot_general(left, right, (((1,), (1,)), ((), ())), preferred_element_type=jnp.float32)


def dot_tn(left, right):
    return lax.dot_general(left, right, (((0,), (0,)), ((), ())), preferred_element_type=jnp.float32)


def square(ref, index):
    return ref[index].reshape(WID, WID)


def iota(shape, axis):
    return lax.broadcasted_iota(jnp.int32, shape, axis)


def flag(condition):
    return jnp.where(condition, 1.0, 0.0)


def softplus(value):
    small = jnp.exp(-jnp.abs(value))
    tail = jnp.where(small < 1e-3, small * (1.0 - 0.5 * small), jnp.log(1.0 + small))
    return jnp.maximum(value, 0.0) + tail


def softplus_slope(feature):
    return jnp.where(feature < 1e-3, feature * (1.0 - 0.5 * feature), 1.0 - jnp.exp(-feature))


def centred(value):
    centre = value - jnp.mean(value, axis=-1, keepdims=True)
    scale = lax.rsqrt(jnp.mean(centre * centre, axis=-1, keepdims=True) + EPS_NORM)
    return centre * scale, scale


def rows_of(molecule):
    return pl.ds(pl.multiple_of(molecule * PAD, 16), PAD)


def column_sum(value):
    return jnp.sum(value, axis=0, keepdims=True)


GAIN1, BIAS1, B_QUERY, B_KEY, B_VALUE, B_OUT, GAIN2, BIAS2, B_DOWN, B_UP = range(10)


class Layer:
    def __init__(self, **refs):
        self.__dict__.update(refs)

    def row(self, index):
        return self.params[pl.ds(index, 1)]

    def add_row(self, index, value):
        self.vectors[pl.ds(index, 1)] += value

    def block_mask(self):
        shape = (FEAT, LANES)
        return flag(iota(shape, 0) // 32 == iota(shape, 1) // 64)

    def prepare_features(self):
        proj = self.feature_ref[...]
        pick_rows = iota((LANES, 64), 0) % 64
        swap = iota((LANES, 64), 1)
        same = rounded(flag(pick_rows == swap))
        turned = rounded(flag(pick_rows + 32 == swap) - flag(pick_rows == swap + 32))
        spread = rounded(flag(iota((32, FEAT), 1) % 32 == iota((32, FEAT), 0)))
        mask = flag(iota((LANES, FEAT), 0) // 64 == iota((LANES, FEAT), 1) // 32)
        for index, pick in ((0, same), (1, turned)):
            tall = rounded(dot(pick, proj))
            self.features[index] = rounded(dot(tall, spread) * mask)

    def prepare_tokens(self):
        zero = jnp.zeros((16, WID), jnp.bfloat16)
        for molecule in range(MOLS):
            start = molecule * PAD
            self.tokens[pl.ds(start + PAD - 16, 16)] = zero
            self.tokens[pl.ds(start, ROWS)] = self.raw[molecule]

    def prepare_cotangent(self):
        most = jnp.maximum(
            jnp.maximum(self.lengths[0], self.lengths[1]), jnp.maximum(self.lengths[2], self.lengths[3])
        )
        zero = jnp.zeros((16, WID), jnp.bfloat16)
        keep = iota((ROWS, WID), 0) < most
        for molecule in range(MOLS):
            start = molecule * PAD
            self.grad_down[pl.ds(start + PAD - 16, 16)] = zero
            masked = jnp.where(keep, wide(self.raw[molecule]), 0.0)
            self.grad_down[pl.ds(start, ROWS)] = rounded(masked)
            self.add_row(B_DOWN, column_sum(masked))

    def prepare_params(self):
        columns = wide(self.small[...].reshape(WID, 128))
        rows = columns.T
        self.params[pl.ds(0, 16)] = rows[0:16]
        lanes = iota((8, WID), 1)
        owner = flag(lanes // 192 == iota((8, WID), 0))
        stacked = jnp.concatenate(
            [jnp.broadcast_to(rows[B_UP + k : B_UP + k + 1], (8, WID)) * owner for k in range(4)], axis=0
        )
        source = iota((WID, WID), 0)
        pick = rounded(flag(96 * ((source // 24) % 8) + source % 24 == iota((WID, WID), 1)))
        spread = dot(rounded(stacked), pick)
        total = spread[0:8]
        for k in range(1, 4):
            total = total + pltpu.roll(spread[8 * k : 8 * k + 8], 24 * k, 1)
        self.params[pl.ds(16, 8)] = total

    def norm_one(self):
        gain, bias = self.row(GAIN1), self.row(BIAS1)
        for molecule in range(MOLS):
            rows = pl.ds(molecule * PAD, PAD)
            normed, _ = centred(wide(self.tokens[rows]))
            self.normed_one[rows] = rounded(normed * gain + bias)

    def turn(self, value, group):
        both = value[:, group * LANES : (group + 1) * LANES]
        cosines = jnp.concatenate([self.cosines[...]] * 2, axis=1)
        sines = jnp.concatenate([self.sines[...]] * 2, axis=1)
        return rounded(both * cosines), rounded(both * sines)

    def state(self, molecule, group, mask):
        rows, ones = rows_of(molecule), jnp.ones((PAD, LANES), jnp.bfloat16)
        keys = self.feat_key[rows, group * FEAT : (group + 1) * FEAT]
        values = self.values[rows, group * LANES : (group + 1) * LANES]
        return jnp.concatenate(
            [rounded(dot_tn(keys, values) * mask), rounded(dot_tn(keys, ones) * mask)], axis=1
        )

    def attend(self, molecule):
        rows = rows_of(molecule)
        normed = self.normed_one[rows]
        query = dot(normed, square(self.weights, 0)) + self.row(B_QUERY)
        key = dot(normed, square(self.weights, 1)) + self.row(B_KEY)
        value = dot(normed, square(self.weights, 2)) + self.row(B_VALUE)
        length = self.lengths[molecule]
        valid = jnp.where(iota((PAD, WID), 0) < length, value, 0.0)
        level = column_sum(valid) / wide(jnp.maximum(length, 1))
        self.levels[pl.ds(8 * molecule, 1)] = level
        self.values[rows] = rounded(value - level)
        keep = iota((PAD, FEAT), 0) < length
        mask = self.block_mask()
        for group in range(GROUPS):
            lanes = slice(group * FEAT, (group + 1) * FEAT)
            cos_part, sin_part = self.turn(query, group)
            feat = softplus(dot(cos_part, self.features[0]) + dot(sin_part, self.features[1]))
            feat_query = rounded(feat)
            self.feat_query[rows, lanes] = feat_query
            cos_part, sin_part = self.turn(key, group)
            feat = softplus(dot(cos_part, self.features[0]) + dot(sin_part, self.features[1]))
            self.feat_key[rows, lanes] = rounded(jnp.where(keep, feat, 0.0))
            state = self.state(molecule, group, mask)
            self.states[molecule, group] = state
            both = dot(feat_query, state)
            centre = level[:, group * LANES : (group + 1) * LANES]
            mixed = centre + (both[:, :LANES] - EPS_ATTN * centre) / (both[:, LANES:] + EPS_ATTN)
            self.mixed[rows, group * LANES : (group + 1) * LANES] = rounded(mixed)

    def middle_rows(self, molecule):
        rows = rows_of(molecule)
        middle = (
            wide(self.tokens[rows])
            + dot(self.mixed[rows], square(self.weights, 3))
            + self.row(B_OUT)
        )
        self.middle[rows] = middle
        normed, _ = centred(middle)
        self.normed_two[rows] = rounded(normed * self.row(GAIN2) + self.row(BIAS2))

    def up_rows(self, quarter, molecule):
        rows = rows_of(molecule)
        pre = dot(self.normed_two[rows], square(self.weights, 4 + quarter)) + self.row(16 + quarter)
        squared = pre * pre
        gate = 0.5 + 0.5 * jnp.tanh(pre * (GELU_SCALE + GELU_SCALE * GELU_CUBIC * squared))
        hidden = pre * gate
        slope = gate + (hidden - hidden * gate) * (
            2.0 * GELU_SCALE + 6.0 * GELU_SCALE * GELU_CUBIC * squared
        )
        self.hidden[quarter, rows] = rounded(hidden)
        self.slope[quarter, rows] = rounded(slope)

    def store_term(self, slot, value):
        self.grads[slot] = rounded(value).reshape(4, 4, BLK, WID)

    def term_down(self, quarter):
        self.store_term(quarter, dot_tn(self.hidden[quarter], self.grad_down[...]))

    def grad_pre_rows(self, quarter, molecule):
        rows = rows_of(molecule)
        grad_hidden = dot_nt(self.grad_down[rows], square(self.weights, 8 + quarter))
        grad_pre = rounded(grad_hidden * wide(self.slope[quarter, rows]))
        self.slope[quarter, rows] = grad_pre
        self.add_row(B_UP + quarter, column_sum(wide(grad_pre)))

    def term_up(self, quarter):
        self.store_term(4 + quarter, dot_tn(self.normed_two[...], self.slope[quarter]))

    def grad_middle_rows(self, molecule):
        rows = rows_of(molecule)
        grad_two = dot_nt(self.slope[0, rows], square(self.weights, 4))
        for quarter in range(1, 4):
            grad_two += dot_nt(self.slope[quarter, rows], square(self.weights, 4 + quarter))
        normed, scale = centred(self.middle[rows])
        self.add_row(GAIN2, column_sum(grad_two * normed))
        self.add_row(BIAS2, column_sum(grad_two))
        scaled = grad_two * self.row(GAIN2)
        first = jnp.mean(scaled, axis=-1, keepdims=True)
        second = jnp.mean(scaled * normed, axis=-1, keepdims=True)
        self.grad_middle[rows] = wide(self.grad_down[rows]) + scale * (scaled - first - normed * second)

    def branch_rows(self, molecule):
        rows = rows_of(molecule)
        low = rounded(self.grad_middle[rows])
        self.slope[3, rows] = low
        self.add_row(B_OUT, column_sum(wide(low)))

    def term_out(self):
        self.store_term(3, dot_tn(self.mixed[...], self.slope[3]))

    def attend_back(self, molecule):
        rows = rows_of(molecule)
        grad_mixed = dot_nt(self.slope[3, rows], square(self.weights, 3))
        mask = self.block_mask()
        both_mask = jnp.concatenate([mask, mask], axis=1)
        ones = jnp.ones((PAD, LANES), jnp.bfloat16)
        cosines = jnp.concatenate([self.cosines[...]] * 2, axis=1)
        sines = jnp.concatenate([self.sines[...]] * 2, axis=1)
        for group in range(GROUPS):
            thin = slice(group * FEAT, (group + 1) * FEAT)
            lanes = slice(group * LANES, (group + 1) * LANES)
            feat_query, feat_key = self.feat_query[rows, thin], self.feat_key[rows, thin]
            values, state = self.values[rows, lanes], self.states[molecule, group]
            both = dot(feat_query, state)
            inverse = 1.0 / (both[:, LANES:] + EPS_ATTN)
            grad_num = grad_mixed[:, lanes] * inverse
            offset = EPS_ATTN * self.levels[pl.ds(8 * molecule, 1), lanes]
            grad_den = -grad_num * ((both[:, :LANES] - offset) * inverse)
            grad_both = jnp.concatenate([rounded(grad_num), rounded(grad_den)], axis=1)
            grad_feat_query = dot_nt(grad_both, state)
            grad_state = rounded(dot_tn(feat_query, grad_both) * both_mask)
            grad_feat_key = dot_nt(jnp.concatenate([values, ones], axis=1), grad_state)
            grad_value = rounded(dot(feat_key, grad_state[:, :LANES]))
            self.slope[2, rows, lanes] = grad_value
            self.add_lanes(B_VALUE, group, grad_value)
            for slot, row, feat, grad in (
                (0, B_QUERY, feat_query, grad_feat_query),
                (1, B_KEY, feat_key, grad_feat_key),
            ):
                grad = rounded(grad * softplus_slope(wide(feat)))
                low = rounded(
                    cosines * dot_nt(grad, self.features[0]) + sines * dot_nt(grad, self.features[1])
                )
                self.slope[slot, rows, lanes] = low
                self.add_lanes(row, group, low)

    def add_lanes(self, row, group, value):
        self.vectors[pl.ds(row, 1), group * LANES : (group + 1) * LANES] += column_sum(wide(value))

    def term_square(self, index):
        self.store_term(index, dot_tn(self.normed_one[...], self.slope[index]))

    def grad_token_rows(self, molecule):
        rows = rows_of(molecule)
        grad_one = dot_nt(self.slope[0, rows], square(self.weights, 0))
        for index in (1, 2):
            grad_one += dot_nt(self.slope[index, rows], square(self.weights, index))
        normed, scale = centred(wide(self.tokens[rows]))
        self.add_row(GAIN1, column_sum(grad_one * normed))
        self.add_row(BIAS1, column_sum(grad_one))
        scaled = grad_one * self.row(GAIN1)
        first = jnp.mean(scaled, axis=-1, keepdims=True)
        second = jnp.mean(scaled * normed, axis=-1, keepdims=True)
        grad = self.grad_middle[rows] + scale * (scaled - first - normed * second)
        self.raw[molecule] = rounded(grad[:ROWS])

    def layer_out_rows(self, molecule):
        rows = rows_of(molecule)
        result = self.middle[rows] + self.row(B_DOWN)
        for quarter in range(4):
            result += dot(self.hidden[quarter, rows], square(self.weights, 8 + quarter))
        most = jnp.maximum(
            jnp.maximum(self.lengths[0], self.lengths[1]), jnp.maximum(self.lengths[2], self.lengths[3])
        )
        keep = iota((ROWS, WID), 0) < most
        self.raw[molecule] = rounded(jnp.where(keep, result[:ROWS], 0.0))


def each(work):
    def step(molecule, carry):
        work(molecule)
        return carry

    lax.fori_loop(0, MOLS, step, 0)


LAYER_SCRATCH = dict(
    raw=((MOLS, ROWS, WID), jnp.bfloat16),
    tokens=((TOTAL, WID), jnp.bfloat16),
    grad_down=((TOTAL, WID), jnp.bfloat16),
    normed_one=((TOTAL, WID), jnp.bfloat16),
    values=((TOTAL, WID), jnp.bfloat16),
    mixed=((TOTAL, WID), jnp.bfloat16),
    normed_two=((TOTAL, WID), jnp.bfloat16),
    feat_query=((TOTAL, HALF), jnp.bfloat16),
    feat_key=((TOTAL, HALF), jnp.bfloat16),
    levels=((8 * MOLS, WID), jnp.float32),
    states=((MOLS, GROUPS, FEAT, 2 * LANES), jnp.bfloat16),
    middle=((TOTAL, WID), jnp.float32),
    grad_middle=((TOTAL, WID), jnp.float32),
    hidden=((4, TOTAL, WID), jnp.bfloat16),
    slope=((4, TOTAL, WID), jnp.bfloat16),
    features=((2, LANES, FEAT), jnp.bfloat16),
    params=((24, WID), jnp.float32),
    vectors=((16, WID), jnp.float32),
    grads=((8, 4, 4, BLK, WID), jnp.bfloat16),
    weights=((12, 4, 4, BLK, WID), jnp.bfloat16),
    small=((4, 4, BLK, 128), jnp.bfloat16),
)


VMEM = pl.BlockSpec(memory_space=pltpu.VMEM)
SMEM = pl.BlockSpec(memory_space=pltpu.SMEM)
ANY = pl.BlockSpec(memory_space=pl.ANY)
SEMS = 224


def landing(name):
    bf = jnp.bfloat16
    return {
        name + "_big": ((2, 6, 4, BLK, HALF), bf),
        name + "_little": ((2, 6, BLK, HALF), bf),
        name + "_cross": ((2, 4, BLK, WID), bf),
    }


COMM_SCRATCH = dict(
    pair=((2, 4, 4, BLK, WID), jnp.bfloat16),
    **landing("odd"),
    **landing("even"),
    total_zero=((2, BLK, WID), jnp.float32),
    total_one=((2, BLK, WID), jnp.float32),
    square_sum=((4, 24, WID), jnp.float32),
    up_sum=((24, 4 * WID), jnp.float32),
    down_sum=((2 * BLK, WID), jnp.float32),
    vector_land=((4, 4, 16, WID), jnp.float32),
    narrow=((16, 128), jnp.float32),
    small_mine=((BLK, 128), jnp.float32),
)
LOADS = ("tokens", "cotangent")
OUTS = ("layer", "tokens", "square", "up", "down", "narrow")


def some(work, *molecules):
    def step(molecule, carry):
        work(molecule)
        return carry

    lax.fori_loop(molecules[0], molecules[-1] + 1, step, 0)


def layer_kernel(
    lengths, queries, keys, values, outs, ups, downs, packed, feature_ref, cosines, sines,
    tokens_in, cot_in, layer_out, tokens_out, square_out, up_out, down_out, narrow_out, *scratch,
):
    names = list(LAYER_SCRATCH) + list(COMM_SCRATCH)
    refs = dict(zip(names, scratch))
    send_sems, recv_sems, local_sems, credits, pair_credit = scratch[len(names):]
    net = Net(send_sems, recv_sems)
    work = Layer(
        lengths=lengths, feature_ref=feature_ref, cosines=cosines, sines=sines,
        **{name: refs[name] for name in LAYER_SCRATCH},
    )
    load_tokens = pltpu.make_async_copy(tokens_in, work.raw, local_sems.at[0])
    load_cot = pltpu.make_async_copy(cot_in, work.raw, local_sems.at[1])
    load_tokens.start()
    net.greet()

    shards = (queries, keys, values, outs, ups, downs, packed)
    load = load_shards(
        net, work.weights, work.small, work.grad_middle, refs["small_mine"], shards
    )
    small = gather_small(net, work.small)
    get = [gather_steps(net, work.weights, part) for part in (0, 1, 2)]

    def go(*steps):
        for step in steps:
            next(step, None)

    go(load)
    work.vectors[...] = jnp.zeros_like(work.vectors)
    work.prepare_features()
    go(load, small, get[0], load, get[1])
    load_tokens.wait()
    work.prepare_tokens()
    load_cot.start()
    go(get[0], small, get[0], get[1])
    load_cot.wait()
    work.prepare_cotangent()
    go(small)
    work.prepare_params()
    go(get[0], get[1])
    work.norm_one()
    go(get[0], get[2], get[0], get[2])
    some(work.attend, 0, 1)
    go(get[1], get[2])
    some(work.attend, 2, 3)
    some(work.middle_rows, 0, 3)
    go(get[1], get[1], get[2])
    for quarter in range(4):
        some(lambda molecule: work.up_rows(quarter, molecule), 0, 3)
        if quarter == 0:
            go(get[2])
    for quarter in range(4):
        work.term_down(quarter)
    go(get[2])
    net.settle()

    def reduce(part, name, total, result):
        return reduce_steps(
            net, work.grads, part, refs["pair"], pair_credit, refs[name + "_big"], refs[name + "_little"],
            refs[name + "_cross"], total, refs[result],
        )

    down = reduce(2, "even", None, "down_sum")
    up = reduce(1, "odd", refs["total_one"], "up_sum")
    squares = reduce(0, "even", refs["total_zero"], "square_sum")
    go(down)
    for quarter in range(4):
        some(lambda molecule: work.grad_pre_rows(quarter, molecule), 0, 3)
        go(*[down] * (quarter % 2))
    for quarter in range(4):
        work.term_up(quarter)
        go(*[down] * (quarter % 2))
    go(up)
    some(work.grad_middle_rows, 0, 1)
    go(down)
    some(work.grad_middle_rows, 2, 3)
    some(work.branch_rows, 0, 3)
    go(down, up, down)
    some(work.attend_back, 0, 0)
    go(up, down)
    some(work.attend_back, 1, 1)
    go(up, down)
    some(work.attend_back, 2, 2)
    go(up, down)
    some(work.attend_back, 3, 3)
    for _ in down:
        pass
    net.settle()
    for device in net.partners():
        pl.semaphore_signal(credits, inc=1, device_id=device, device_id_type=MESH)
    for index in range(3):
        work.term_square(index)
    work.term_out()
    pl.semaphore_wait(credits, 8)
    go(squares, up)
    some(work.grad_token_rows, 0, 3)
    write_tokens = pltpu.make_async_copy(work.raw, tokens_out, local_sems.at[0])
    write_tokens.start()
    vectors = vector_steps(net, work.vectors, refs["vector_land"])
    go(squares, vectors, up)
    write_tokens.wait()
    some(work.layer_out_rows, 0, 1)
    go(squares, vectors, up)
    some(work.layer_out_rows, 2, 3)
    write_layer = pltpu.make_async_copy(work.raw, layer_out, local_sems.at[1])
    write_layer.start()
    for _ in together(squares, vectors, up):
        pass
    total = refs["vector_land"][0, 1]
    place = net.y * 8 + net.z * 2 + net.c
    narrow = refs["narrow"]
    turned = pltpu.roll(total, WID - 24 * place, 1)
    narrow[...] = turned[:, :128]
    chosen = refs["vector_land"][0, 1, pl.ds(B_UP + place // 8, 1)]
    narrow[pl.ds(B_UP, 1)] = pltpu.roll(chosen, WID - 96 * (place % 8), 1)[:, :128]
    writes = [
        pltpu.make_async_copy(refs[name], ref, local_sems.at[2 + slot])
        for slot, (name, ref) in enumerate(
            (("square_sum", square_out), ("up_sum", up_out), ("down_sum", down_out), ("narrow", narrow_out))
        )
    ]
    for write in writes:
        write.start()
    net.settle()
    for write in [write_layer] + writes:
        write.wait()


def layer_call(*operands):
    bf, ff = jnp.bfloat16, jnp.float32
    scratch = list(LAYER_SCRATCH.values()) + list(COMM_SCRATCH.values())
    return pl.pallas_call(
        layer_kernel,
        out_shape=(
            jax.ShapeDtypeStruct((MOLS, ROWS, WID), bf),
            jax.ShapeDtypeStruct((MOLS, ROWS, WID), bf),
            jax.ShapeDtypeStruct((4, 24, WID), ff),
            jax.ShapeDtypeStruct((24, 4 * WID), ff),
            jax.ShapeDtypeStruct((2 * BLK, WID), ff),
            jax.ShapeDtypeStruct((16, 128), ff),
        ),
        in_specs=[SMEM] + [VMEM] * 10 + [ANY] * 2,
        out_specs=(ANY,) * 6,
        scratch_shapes=[pltpu.VMEM(shape, dtype) for shape, dtype in scratch]
        + [
            pltpu.SemaphoreType.DMA((SEMS,)),
            pltpu.SemaphoreType.DMA((SEMS,)),
            pltpu.SemaphoreType.DMA((6,)),
            pltpu.SemaphoreType.REGULAR,
            pltpu.SemaphoreType.REGULAR,
        ],
        compiler_params=pltpu.CompilerParams(
            collective_id=0, has_side_effects=True, vmem_limit_bytes=64 * 2**20 - 2**17
        ),
    )(*operands)


def angle_tables():
    positions = np.arange(PAD)[:, None]
    angles = positions * 10000.0 ** (-2.0 * (np.arange(128)[None, :] % 32) / 64)
    return np.cos(angles).astype(np.float32), np.sin(angles).astype(np.float32)


def body(
    tokens, lengths, feature_proj, ln1_gain, ln1_bias, w_query, b_query, w_key, b_key, w_value, b_value,
    w_out, b_out, ln2_gain, ln2_bias, w_up, b_up, w_down, b_down, cotangent,
):
    cosines, sines = angle_tables()
    packed = jnp.concatenate(
        [ln1_gain, ln1_bias, b_query, b_key, b_value, b_out, ln2_gain, ln2_bias, b_down, b_up]
        + [jnp.zeros((HALF - 312,), jnp.bfloat16)]
    ).reshape(1, HALF)
    layer_out, grad_tokens, square, up, down, narrow = layer_call(
        lengths, w_query, w_key, w_value, w_out, w_up, w_down, packed, feature_proj,
        jnp.asarray(cosines), jnp.asarray(sines), tokens, cotangent,
    )
    small = [narrow[index, :24] for index in range(9)]
    return (
        layer_out, grad_tokens, small[0], small[1], square[0], small[2], square[1], small[3], square[2], small[4],
        square[3], small[5], small[6], small[7], up, narrow[9, :96], down, small[8],
    )


def solution(mesh):
    rows, flat = P("fsdp", None), P("fsdp")
    mols = P(("fsdp", "dp"), None, None)
    pairs = (flat, flat, rows, flat, rows, flat, rows, flat, rows, flat, flat, flat, rows, flat, rows, flat)
    return jax.shard_map(
        body,
        mesh=mesh,
        in_specs=(mols, P(("fsdp", "dp")), P()) + pairs + (mols,),
        out_specs=(mols, mols) + pairs,
        check_vma=False,
    )
```

```python
import jax
import jax.numpy as jnp
import numpy as np
from jax import lax
from jax.experimental import pallas as pl
from jax.experimental.pallas import tpu as pltpu
from jax.sharding import PartitionSpec as P


MESH = pl.DeviceIdType.MESH
RING = 4
BLK = 48
WID = 768
HALF = 384
ALL = pl.ds(0, RING)
STEPS = (1, 2, 3)
WAYS = (0, 1)


def rounded(value):
    return value.astype(jnp.bfloat16)


def wide(value):
    return value.astype(jnp.float32)


class Net:
    def __init__(self, send_sems, recv_sems):
        self.send_sems, self.recv_sems, self.count = send_sems, recv_sems, 0
        index = lax.axis_index("fsdp")
        self.x = lax.axis_index("dp")
        self.y = index // (2 * RING)
        self.z = (index // 2) % RING
        self.c = index % 2

    def at(self, y, z, c):
        return {"fsdp": ((y + RING) % RING) * (2 * RING) + ((z + RING) % RING) * 2 + c}

    def sibling(self):
        return self.at(self.y, self.z, 1 - self.c)

    def along(self, axis, step):
        if axis == "y":
            return self.at(self.y + step, self.z, self.c)
        if axis == "z":
            return self.at(self.y, self.z + step, self.c)
        return {"dp": (self.x + step) % RING}

    def peers(self):
        return [self.along(axis, step) for axis in ("x", "y", "z") for step in STEPS]

    def greet(self):
        barrier = pltpu.get_barrier_semaphore()
        peers = [self.sibling()] + self.peers()
        for peer in peers:
            pl.semaphore_signal(barrier, inc=1, device_id=peer, device_id_type=MESH)
        pl.semaphore_wait(barrier, len(peers))

    def send(self, src, dst, device):
        slot = self.count
        self.count += 1
        copy = pltpu.make_async_remote_copy(
            src_ref=src,
            dst_ref=dst,
            send_sem=self.send_sems.at[slot],
            recv_sem=self.recv_sems.at[slot],
            device_id=device,
            device_id_type=MESH,
        )
        copy.start()
        return slot

    def arrived(self, slot, land):
        pltpu.make_async_remote_copy(
            src_ref=land,
            dst_ref=land,
            send_sem=self.send_sems.at[slot],
            recv_sem=self.recv_sems.at[slot],
            device_id=self.sibling(),
            device_id_type=MESH,
        ).wait_recv()

    def left(self, slot, source):
        pltpu.make_async_remote_copy(
            src_ref=source,
            dst_ref=source,
            send_sem=self.send_sems.at[slot],
            recv_sem=self.recv_sems.at[slot],
            device_id=self.sibling(),
            device_id_type=MESH,
        ).wait_send()

    def axes(self, way):
        return ("y", "z") if way == 0 else ("z", "y")

    def place(self, way):
        return (self.y, self.z) if way == 0 else (self.z, self.y)


def wrap(index):
    return (index + RING) % RING


def base_of(ref, part):
    return 4 * part if ref.shape[0] == 12 else 4 * (part % 2)


def columns_of(side):
    return pl.ds(HALF * side, HALF)


def slot_of(ref, part, side, way, core, first, second):
    y, z = (first, second) if way == 0 else (second, first)
    base = base_of(ref, part)
    if part < 2:
        return ref.at[base + 2 * side + core, y, z, :, columns_of(way)]
    y = pl.ds(base, RING) if isinstance(y, pl.Slice) else base + y
    return ref.at[y, z, 2 * core + way, :, columns_of(side)]


class Traffic:
    def __init__(self, net):
        self.net, self.sent = net, []

    def send(self, src, dst, device):
        slot = self.net.send(src, dst, device)
        self.sent.append((slot, src))
        return slot

    def settle(self):
        for slot, src in self.sent:
            self.net.left(slot, src)
        self.sent = []


def gather_steps(net, weights, part, side):
    traffic, sent = Traffic(net), {}

    def slot(way, first, second, core=None):
        return slot_of(weights, part, side, way, net.c if core is None else core, first, second)

    for way in WAYS:
        own = slot(way, *net.place(way))
        for step in STEPS:
            sent[way, step] = traffic.send(own, own, net.along(net.axes(way)[0], step))
    yield
    for way in WAYS:
        p, q = net.place(way)
        for step in STEPS:
            net.arrived(sent[way, step], slot(way, wrap(p - step), q))
        row = slot(way, ALL, q)
        for step in STEPS:
            sent[way, step] = traffic.send(row, row, net.along(net.axes(way)[1], step))
        sent[way, "own"] = traffic.send(row, row, net.sibling())
    yield
    for step in STEPS:
        for way in WAYS:
            row = slot(way, ALL, wrap(net.place(way)[1] - step))
            net.arrived(sent[way, step], row)
            sent[way, "pair", step] = traffic.send(row, row, net.sibling())
    yield
    for way in WAYS:
        q = net.place(way)[1]
        net.arrived(sent[way, "own"], slot(way, ALL, q, 1 - net.c))
        for step in STEPS:
            net.arrived(sent[way, "pair", step], slot(way, ALL, wrap(q - step), 1 - net.c))
    traffic.settle()


def gather_small(net, small):
    traffic = Traffic(net)
    own = small.at[net.y, net.z]
    sent = [traffic.send(own, own, net.along("y", step)) for step in STEPS]
    yield
    for slot, step in zip(sent, STEPS):
        net.arrived(slot, small.at[wrap(net.y - step), net.z])
    row = small.at[ALL, net.z]
    sent = [traffic.send(row, row, net.along("z", step)) for step in STEPS]
    yield
    for slot, step in zip(sent, STEPS):
        net.arrived(slot, small.at[ALL, wrap(net.z - step)])
    traffic.settle()


def load_shards(net, weights, small, stage, small_mine, thin, shards):
    queries, keys, values, outs, ups, downs, vectors = shards
    first = net.c == 0
    traffic = Traffic(net)

    def rows(slot, core):
        return pl.ds(pl.multiple_of(BLK * slot + 24 * core, 8), 24)

    def lane(piece):
        return pl.ds(pl.multiple_of(WID * piece, WID), WID)

    def exchange(slot, mine, theirs):
        outgoing = pl.ds(4 * BLK + 24 * slot, 24)
        stage[rows(slot, net.c)] = mine
        stage[outgoing] = theirs
        return traffic.send(stage.at[outgoing], stage.at[rows(slot, net.c)], net.sibling())

    sent = []
    for early, late in ((queries, keys), (values, outs)):
        early, late = wide(early[...]), wide(late[...])
        slot = len(sent)
        sent.append(exchange(slot, jnp.where(first, early, late), jnp.where(first, late, early)))
    thin[...] = jnp.zeros_like(thin)
    for index in range(9):
        thin[index, 0:24] = wide(vectors[index][...])
    thin[9, 0:96] = wide(vectors[9][...])
    for index in range(1, 4):
        thin[pl.ds(9 + index, 1)] = pltpu.roll(thin[pl.ds(9, 1)], 128 - 24 * index, 1)
    pick = rounded(flag(iota((16, 128), 0) == iota((16, 128), 1)))
    small_mine[rows(0, net.c)] = dot_tn(rounded(thin[...]), pick)[0:24]
    sent_small = traffic.send(small_mine.at[rows(0, net.c)], small_mine.at[rows(0, net.c)], net.sibling())
    for side in (0, 1):
        near, away = 2 * side + net.c, 2 * side + 1 - net.c
        sent.append(exchange(2 + side, wide(ups[:, lane(near)]), wide(ups[:, lane(away)])))
    for way in WAYS:
        weights[8 + net.y, net.z, 2 * net.c + way] = downs[pl.ds(BLK * way, BLK)]
    yield
    for slot in (0, 1, 2, 3):
        net.arrived(sent[slot], stage.at[rows(slot, 1 - net.c)])
        piece = 4 * (slot // 2) + 2 * (slot % 2) + net.c
        weights[piece, net.y, net.z] = rounded(stage[pl.ds(BLK * slot, BLK)])
        if slot == 0:
            net.arrived(sent_small, small_mine.at[rows(0, 1 - net.c)])
            small[net.y, net.z] = rounded(small_mine[...])
        if slot < 2:
            yield
    traffic.settle()


def add_all(target, *sources):
    if len(target.shape) > 2:
        for index in range(target.shape[0]):
            add_all(target.at[index], *[source.at[index] for source in sources])
        return
    total = wide(target[...])
    for source in sources:
        total = total + wide(source[...])
    target[...] = rounded(total)


def together(*steps):
    steps = list(steps)
    while steps:
        steps = [step for step in steps if next(step, steps) is not steps]
        if steps:
            yield


def reduce_steps(net, grads, part, side, land, gates, total, result):
    pair, big, little, cross = land
    pair_ready, pair_done, land_ready, land_done = gates
    traffic, sent = Traffic(net), {}

    def slot(way, first, second):
        return slot_of(grads, part, side, way, net.c, first, second)

    def whole(way, core):
        base = base_of(grads, part)
        if part < 2:
            return grads.at[base + 2 * side + core, ALL, ALL, :, columns_of(way)]
        return grads.at[pl.ds(base, RING), ALL, 2 * core + way, :, columns_of(side)]

    if pair_ready is not None:
        pl.semaphore_wait(pair_ready, 1)
    for way in WAYS:
        sent[way] = traffic.send(whole(way, 1 - net.c), pair.at[way], net.sibling())
    yield
    for way in WAYS:
        net.arrived(sent[way], pair.at[way])
    if land_ready is not None:
        pl.semaphore_wait(land_ready, len(net.peers()))
    for step in (2, 1, 3, 0):
        for way in WAYS:
            q = wrap(net.place(way)[1] + step)
            group, other = slot(way, ALL, q), pair.at[way]
            other = other.at[ALL, q] if way == 0 else other.at[q]
            add_all(group, other)
            if step:
                land_at = big.at[way, step - 1]
                sent[way, step] = traffic.send(group, land_at, net.along(net.axes(way)[1], step))
    if pair_done is not None:
        pl.semaphore_signal(pair_done, inc=1, device_id=net.sibling(), device_id_type=MESH)
    yield
    for way in WAYS:
        p, q = net.place(way)
        for step in STEPS:
            net.arrived(sent[way, step], big.at[way, step - 1])
        for step in (2, 1, 3, 0):
            at = wrap(p + step)
            block = slot(way, at, q)
            add_all(block, *[big.at[way, index, at] for index in range(3)])
            if step:
                land_at = little.at[way, step - 1]
                sent[way, step] = traffic.send(block, land_at, net.along(net.axes(way)[0], step))
    yield
    for way in WAYS:
        for step in STEPS:
            net.arrived(sent[way, step], little.at[way, step - 1])
        block = slot(way, *net.place(way))
        add_all(block, *[little.at[way, index] for index in range(3)])
        mine = cross.at[way, net.x]
        mine[...] = block[...]
        for step in STEPS:
            sent[way, step] = traffic.send(mine, mine, net.along("x", step))
    yield
    for way in WAYS:
        for step in STEPS:
            net.arrived(sent[way, step], cross.at[way, wrap(net.x - step)])
        value = (wide(cross[way, 0]) + wide(cross[way, 1])) + (wide(cross[way, 2]) + wide(cross[way, 3]))
        if part == 2:
            result[pl.ds(BLK * way, BLK), columns_of(side)] = value
            continue
        total[way] = value
        mine = strip_of(result, part, side, way, net.c)
        mine[...] = total[way, pl.ds(pl.multiple_of(24 * net.c, 8), 24)]
        theirs = total.at[way, pl.ds(pl.multiple_of(24 - 24 * net.c, 8), 24)]
        sent[way] = traffic.send(theirs, mine, net.sibling())
    if land_done is not None:
        for device in net.peers():
            pl.semaphore_signal(land_done, inc=1, device_id=device, device_id_type=MESH)
    yield
    if part < 2:
        for way in WAYS:
            net.arrived(sent[way], strip_of(result, part, side, way, 1 - net.c))
    traffic.settle()


def strip_of(result, part, side, way, core):
    piece = 2 * side + core
    if part == 0:
        return result.at[piece, :, columns_of(way)]
    return result.at[:, pl.ds(pl.multiple_of(WID * piece + HALF * way, HALF), HALF)]


def vector_steps(net, vectors, land):
    traffic = Traffic(net)
    sent = traffic.send(vectors, land.at[0, 0], net.sibling())
    yield
    net.arrived(sent, land.at[0, 0])
    value = vectors[...] + land[0, 0]
    for stage, axis, me in ((1, "z", net.z), (2, "y", net.y), (3, "x", net.x)):
        land[stage, me] = value
        mine = land.at[stage, me]
        sent = [traffic.send(mine, mine, net.along(axis, step)) for step in STEPS]
        yield
        for step in STEPS:
            net.arrived(sent[step - 1], land.at[stage, wrap(me - step)])
        value = ((land[stage, 0] + land[stage, 1]) + land[stage, 2]) + land[stage, 3]
    land[0, 1] = value
    traffic.settle()


ROWS = 202
PAD = 208
MOLS = 4
TOTAL = MOLS * PAD
GROUPS = 3
LANES = 256
FEAT = 128
EPS_NORM = 1e-05
EPS_ATTN = 1e-06
GELU_SCALE = 0.7978845608028654
GELU_CUBIC = 0.044715


def dot(left, right):
    return jnp.dot(left, right, preferred_element_type=jnp.float32)


def dot_nt(left, right):
    return lax.dot_general(left, right, (((1,), (1,)), ((), ())), preferred_element_type=jnp.float32)


def dot_tn(left, right):
    return lax.dot_general(left, right, (((0,), (0,)), ((), ())), preferred_element_type=jnp.float32)


def square(ref, index):
    return ref[index].reshape(WID, WID)


def iota(shape, axis):
    return lax.broadcasted_iota(jnp.int32, shape, axis)


def flag(condition):
    return jnp.where(condition, 1.0, 0.0)


def softplus(value):
    small = jnp.exp(-jnp.abs(value))
    tail = jnp.where(small < 1e-3, small * (1.0 - 0.5 * small), jnp.log(1.0 + small))
    return jnp.maximum(value, 0.0) + tail


def softplus_slope(feature):
    return jnp.where(feature < 1e-3, feature * (1.0 - 0.5 * feature), 1.0 - jnp.exp(-feature))


def centred(value):
    centre = value - jnp.mean(value, axis=-1, keepdims=True)
    scale = lax.rsqrt(jnp.mean(centre * centre, axis=-1, keepdims=True) + EPS_NORM)
    return centre * scale, scale


def column_sum(value):
    return jnp.sum(value, axis=0, keepdims=True)


GAIN1, BIAS1, B_QUERY, B_KEY, B_VALUE, B_OUT, GAIN2, BIAS2, B_DOWN, B_UP = range(10)


class Layer:
    def __init__(self, **refs):
        self.__dict__.update(refs)

    def row(self, index):
        return self.params[pl.ds(index, 1)]

    def add_row(self, index, value):
        self.vectors[pl.ds(index, 1)] += value

    def block_mask(self):
        shape = (FEAT, LANES)
        return flag(iota(shape, 0) // 32 == iota(shape, 1) // 64)

    def prepare_features(self):
        proj = self.feature_ref[...]
        pick_rows = iota((LANES, 64), 0) % 64
        swap = iota((LANES, 64), 1)
        same = rounded(flag(pick_rows == swap))
        turned = rounded(flag(pick_rows + 32 == swap) - flag(pick_rows == swap + 32))
        spread = rounded(flag(iota((32, FEAT), 1) % 32 == iota((32, FEAT), 0)))
        mask = flag(iota((LANES, FEAT), 0) // 64 == iota((LANES, FEAT), 1) // 32)
        for index, pick in ((0, same), (1, turned)):
            tall = rounded(dot_nt(pick, proj))
            full = dot(tall, spread) * mask
            span = slice(index * LANES, (index + 1) * LANES)
            self.features[span] = rounded(full)
            self.features_back[:, span] = rounded(full.T)

    def prepare_tokens(self):
        zero = jnp.zeros((16, WID), jnp.bfloat16)
        for molecule in range(MOLS):
            start = molecule * PAD
            self.tokens[pl.ds(start + PAD - 16, 16)] = zero
            self.tokens[pl.ds(start, ROWS)] = self.raw[:, molecule, :]

    def prepare_cotangent(self):
        zero = jnp.zeros((16, WID), jnp.bfloat16)
        keep = iota((ROWS, WID), 0) < self.most()
        for molecule in range(MOLS):
            start = molecule * PAD
            self.grad_down[pl.ds(start + PAD - 16, 16)] = zero
            masked = jnp.where(keep, wide(self.raw[:, molecule, :]), 0.0)
            self.grad_down[pl.ds(start, ROWS)] = rounded(masked)
            self.add_row(B_DOWN, column_sum(masked))

    def prepare_params(self):
        columns = wide(self.small[...].reshape(WID, 128))
        rows = columns.T
        self.params[pl.ds(0, 16)] = rows[0:16]
        lanes = iota((8, WID), 1)
        owner = flag(lanes // 192 == iota((8, WID), 0))
        stacked = jnp.concatenate(
            [jnp.broadcast_to(rows[B_UP + k : B_UP + k + 1], (8, WID)) * owner for k in range(4)], axis=0
        )
        stacked = rounded(stacked)
        spread = jnp.zeros((32, WID), jnp.float32)
        for start in range(0, WID, 128):
            source = start + iota((128, WID), 0)
            pick = rounded(flag(96 * ((source // 24) % 8) + source % 24 == iota((128, WID), 1)))
            spread = spread + dot(stacked[:, start : start + 128], pick)
        total = spread[0:8]
        for k in range(1, 4):
            total = total + pltpu.roll(spread[8 * k : 8 * k + 8], 24 * k, 1)
        self.params[pl.ds(16, 8)] = total

    def norm_one(self):
        gain, bias = self.row(GAIN1), self.row(BIAS1)
        for molecule in range(MOLS):
            rows = pl.ds(molecule * PAD, PAD)
            normed, _ = centred(wide(self.tokens[rows]))
            self.normed_one[rows] = rounded(normed * gain + bias)

    def tables(self):
        return [
            jnp.concatenate([jnp.concatenate([table[...]] * 2, axis=1)] * MOLS, axis=0)
            for table in (self.cosines, self.sines)
        ]

    def feature_rows(self, piece, row):
        cosines, sines = self.tables()
        found = []
        for group in range(GROUPS):
            lanes = slice(group * LANES, (group + 1) * LANES)
            value = dot(self.normed_one[...], self.columns(piece, lanes)) + self.params[pl.ds(row, 1), lanes]
            turned = jnp.concatenate([rounded(value * cosines), rounded(value * sines)], axis=1)
            found.append(softplus(dot(turned, self.features[...])))
        return found

    def columns(self, piece, lanes):
        return self.weights[piece, :, :, :, lanes].reshape(WID, LANES)

    def query_rows(self):
        for group, feat in enumerate(self.feature_rows(0, B_QUERY)):
            self.feat_query[:, group * FEAT : (group + 1) * FEAT] = rounded(feat)

    def key_rows(self):
        keep = jnp.concatenate(
            [iota((PAD, FEAT), 0) < self.lengths[molecule] for molecule in range(MOLS)], axis=0
        )
        for group, feat in enumerate(self.feature_rows(1, B_KEY)):
            self.feat_key[:, group * FEAT : (group + 1) * FEAT] = rounded(jnp.where(keep, feat, 0.0))

    def attend(self):
        mask = self.block_mask()
        mask = jnp.concatenate([mask, mask], axis=1)
        ones = jnp.ones((PAD, LANES), jnp.bfloat16)
        for group in range(GROUPS):
            lanes = slice(group * LANES, (group + 1) * LANES)
            thin = slice(group * FEAT, (group + 1) * FEAT)
            value = dot(self.normed_one[...], self.columns(2, lanes)) + self.params[pl.ds(B_VALUE, 1), lanes]
            for molecule in range(MOLS):
                rows = slice(molecule * PAD, (molecule + 1) * PAD)
                length = self.lengths[molecule]
                valid = jnp.where(iota((PAD, LANES), 0) < length, value[rows], 0.0)
                level = column_sum(valid) / wide(jnp.maximum(length, 1))
                self.levels[pl.ds(8 * molecule, 1), lanes] = level
                low = rounded(value[rows] - level)
                self.values[rows, lanes] = low
                state = rounded(dot_tn(self.feat_key[rows, thin], jnp.concatenate([low, ones], axis=1)) * mask)
                self.states[molecule, group] = state
                both = dot(self.feat_query[rows, thin], state)
                mixed = level + (both[:, :LANES] - EPS_ATTN * level) / (both[:, LANES:] + EPS_ATTN)
                self.mixed[rows, lanes] = rounded(mixed)

    def middle_rows(self):
        whole = dot(self.mixed[...], square(self.weights, 3))
        for molecule in range(MOLS):
            rows = slice(molecule * PAD, (molecule + 1) * PAD)
            middle = wide(self.tokens[rows]) + whole[rows] + self.row(B_OUT)
            self.middle[rows] = middle
            normed, _ = centred(middle)
            self.normed_two[rows] = rounded(normed * self.row(GAIN2) + self.row(BIAS2))

    def up_rows(self, quarter):
        for group in range(GROUPS):
            lanes = slice(group * LANES, (group + 1) * LANES)
            pre = dot(self.normed_two[...], self.columns(4 + quarter, lanes))
            pre = pre + self.params[pl.ds(16 + quarter, 1), lanes]
            squared = pre * pre
            gate = 0.5 + 0.5 * jnp.tanh(pre * (GELU_SCALE + GELU_SCALE * GELU_CUBIC * squared))
            hidden = pre * gate
            slope = gate + (hidden - hidden * gate) * (
                2.0 * GELU_SCALE + 6.0 * GELU_SCALE * GELU_CUBIC * squared
            )
            self.hidden[quarter, :, lanes] = rounded(hidden)
            self.slope[quarter, :, lanes] = rounded(slope)

    def store_term(self, slot, value):
        self.grads[slot] = rounded(value).reshape(4, 4, BLK, WID)

    def term_down(self, quarter):
        self.store_term(quarter, dot_tn(self.hidden[quarter], self.grad_down[...]))

    def grad_pre_rows(self, quarter):
        grad_hidden = dot_nt(self.grad_down[...], square(self.weights, 8 + quarter))
        grad_pre = rounded(grad_hidden * wide(self.slope[quarter]))
        self.slope[quarter] = grad_pre
        self.add_row(B_UP + quarter, column_sum(wide(grad_pre)))

    def term_up(self, quarter):
        self.store_term(4 + quarter, dot_tn(self.normed_two[...], self.slope[quarter]))

    def norm_back(self, grad, inputs, gain, bias):
        normed, scale = centred(inputs)
        self.add_row(gain, column_sum(grad * normed))
        self.add_row(bias, column_sum(grad))
        scaled = grad * self.row(gain)
        first = jnp.mean(scaled, axis=-1, keepdims=True)
        second = jnp.mean(scaled * normed, axis=-1, keepdims=True)
        return scale * (scaled - first - normed * second)

    def grad_middle_rows(self):
        whole = dot_nt(self.slope[0], square(self.weights, 4))
        for quarter in range(1, 4):
            whole += dot_nt(self.slope[quarter], square(self.weights, 4 + quarter))
        for molecule in range(MOLS):
            rows = slice(molecule * PAD, (molecule + 1) * PAD)
            grad = wide(self.grad_down[rows]) + self.norm_back(whole[rows], self.middle[rows], GAIN2, BIAS2)
            self.grad_middle[rows] = grad
            low = rounded(grad)
            self.slope[3, rows] = low
            self.add_row(B_OUT, column_sum(wide(low)))

    def term_out(self):
        self.store_term(3, dot_tn(self.mixed[...], self.slope[3]))

    def attend_back(self, group):
        mask = self.block_mask()
        mask = jnp.concatenate([mask, mask], axis=1)
        ones = jnp.ones((PAD, LANES), jnp.bfloat16)
        cosines, sines = self.tables()
        thin = slice(group * FEAT, (group + 1) * FEAT)
        lanes = slice(group * LANES, (group + 1) * LANES)
        out_rows = self.weights[3].reshape(WID, WID)[lanes]
        grad_mixed = dot_nt(self.slope[3], out_rows)
        slopes_query, slopes_key = [], []
        for molecule in range(MOLS):
            rows = slice(molecule * PAD, (molecule + 1) * PAD)
            feat_query, feat_key = self.feat_query[rows, thin], self.feat_key[rows, thin]
            values, state = self.values[rows, lanes], self.states[molecule, group]
            both = dot(feat_query, state)
            inverse = 1.0 / (both[:, LANES:] + EPS_ATTN)
            grad_num = grad_mixed[rows] * inverse
            offset = EPS_ATTN * self.levels[pl.ds(8 * molecule, 1), lanes]
            grad_den = -grad_num * ((both[:, :LANES] - offset) * inverse)
            grad_both = jnp.concatenate([rounded(grad_num), rounded(grad_den)], axis=1)
            grad_state = rounded(dot_tn(feat_query, grad_both) * mask)
            self.slope[2, rows, lanes] = rounded(dot(feat_key, grad_state[:, :LANES]))
            grad_query = dot_nt(grad_both, state)
            grad_key = dot_nt(jnp.concatenate([values, ones], axis=1), grad_state)
            slopes_query.append(rounded(grad_query * softplus_slope(wide(feat_query))))
            slopes_key.append(rounded(grad_key * softplus_slope(wide(feat_key))))
        for slot, slopes in ((0, slopes_query), (1, slopes_key)):
            turned = dot(jnp.concatenate(slopes, axis=0), self.features_back[...])
            self.slope[slot, :, lanes] = rounded(cosines * turned[:, :LANES] + sines * turned[:, LANES:])
        for slot, row in ((0, B_QUERY), (1, B_KEY), (2, B_VALUE)):
            self.vectors[pl.ds(row, 1), lanes] += column_sum(wide(self.slope[slot, :, lanes]))

    def term_square(self, index):
        self.store_term(index, dot_tn(self.normed_one[...], self.slope[index]))

    def grad_token_rows(self):
        whole = dot_nt(self.slope[0], square(self.weights, 0))
        for index in (1, 2):
            whole += dot_nt(self.slope[index], square(self.weights, index))
        for molecule in range(MOLS):
            rows = slice(molecule * PAD, (molecule + 1) * PAD)
            back = self.norm_back(whole[rows], wide(self.tokens[rows]), GAIN1, BIAS1)
            grad = self.grad_middle[rows] + back
            self.raw[:, molecule, :] = rounded(grad[:ROWS])

    def most(self):
        lengths = self.lengths
        return jnp.maximum(jnp.maximum(lengths[0], lengths[1]), jnp.maximum(lengths[2], lengths[3]))

    def layer_out_rows(self):
        whole = dot(self.hidden[0], square(self.weights, 8))
        for quarter in range(1, 4):
            whole += dot(self.hidden[quarter], square(self.weights, 8 + quarter))
        keep = iota((ROWS, WID), 0) < self.most()
        for molecule in range(MOLS):
            rows = slice(molecule * PAD, molecule * PAD + ROWS)
            result = self.middle[rows] + whole[rows] + self.row(B_DOWN)
            self.raw[:, molecule, :] = rounded(jnp.where(keep, result, 0.0))

LAYER_SCRATCH = dict(
    raw=((ROWS, MOLS, WID), jnp.bfloat16),
    tokens=((TOTAL, WID), jnp.bfloat16),
    grad_down=((TOTAL, WID), jnp.bfloat16),
    normed_one=((TOTAL, WID), jnp.bfloat16),
    values=((TOTAL, WID), jnp.bfloat16),
    mixed=((TOTAL, WID), jnp.bfloat16),
    normed_two=((TOTAL, WID), jnp.bfloat16),
    feat_query=((TOTAL, HALF), jnp.bfloat16),
    feat_key=((TOTAL, HALF), jnp.bfloat16),
    levels=((8 * MOLS, WID), jnp.float32),
    states=((MOLS, GROUPS, FEAT, 2 * LANES), jnp.bfloat16),
    middle=((TOTAL, WID), jnp.float32),
    grad_middle=((TOTAL, WID), jnp.float32),
    hidden=((4, TOTAL, WID), jnp.bfloat16),
    slope=((4, TOTAL, WID), jnp.bfloat16),
    features=((2 * LANES, FEAT), jnp.bfloat16),
    features_back=((FEAT, 2 * LANES), jnp.bfloat16),
    params=((24, WID), jnp.float32),
    vectors=((16, WID), jnp.float32),
    grads=((8, 4, 4, BLK, WID), jnp.bfloat16),
    weights=((12, 4, 4, BLK, WID), jnp.bfloat16),
    small=((4, 4, BLK, 128), jnp.bfloat16),
)


VMEM = pl.BlockSpec(memory_space=pltpu.VMEM)
SMEM = pl.BlockSpec(memory_space=pltpu.SMEM)
ANY = pl.BlockSpec(memory_space=pl.ANY)
SEMS = 288


COMM_SCRATCH = dict(
    pair=((2, 2, 4, 4, BLK, HALF), jnp.bfloat16),
    big=((3, 2, 3, 4, BLK, HALF), jnp.bfloat16),
    little=((3, 2, 3, BLK, HALF), jnp.bfloat16),
    cross=((3, 2, 4, BLK, HALF), jnp.bfloat16),
    total=((4, 2, BLK, HALF), jnp.float32),
    square_sum=((4, 24, WID), jnp.float32),
    up_sum=((24, 4 * WID), jnp.float32),
    down_sum=((2 * BLK, WID), jnp.float32),
    vector_land=((4, 4, 16, WID), jnp.float32),
    narrow=((16, 128), jnp.float32),
    small_mine=((BLK, 128), jnp.float32),
)
def layer_kernel(
    lengths, queries, keys, values, outs, ups, downs, feature_ref, cosines, sines, *rest,
):
    vectors_in, rest = rest[:10], rest[10:]
    tokens_in, cot_in, layer_out, tokens_out, square_out, up_out, down_out, narrow_out = rest[:8]
    scratch = rest[8:]
    names = list(LAYER_SCRATCH) + list(COMM_SCRATCH)
    refs = dict(zip(names, scratch))
    send_sems, recv_sems, local_sems, pair_gates, land_gates = scratch[len(names):]
    net = Net(send_sems, recv_sems)
    work = Layer(
        lengths=lengths, feature_ref=feature_ref, cosines=cosines, sines=sines,
        **{name: refs[name] for name in LAYER_SCRATCH},
    )
    load_tokens = pltpu.make_async_copy(tokens_in, work.raw, local_sems.at[0])
    load_cot = pltpu.make_async_copy(cot_in, work.raw, local_sems.at[1])
    load_tokens.start()
    net.greet()

    shards = (queries, keys, values, outs, ups, downs, vectors_in)
    load = load_shards(
        net, work.weights, work.small, work.grad_middle, refs["small_mine"], refs["narrow"], shards
    )
    small = gather_small(net, work.small)
    get = [gather_steps(net, work.weights, part, side) for part in (0, 1, 2) for side in (0, 1)]

    def go(*steps):
        for step in steps:
            next(step, None)

    def reduce(order, part, side, result):
        land = [refs["pair"].at[order % 2]] + [
            refs[name].at[order % 3] for name in ("big", "little", "cross")
        ]
        gates = (
            pair_gates.at[order - 2] if order >= 2 else None,
            pair_gates.at[order] if order < 4 else None,
            land_gates.at[order - 3] if order >= 3 else None,
            land_gates.at[order] if order < 3 else None,
        )
        total = refs["total"].at[order - 2] if order >= 2 else None
        return reduce_steps(net, work.grads, part, side, land, gates, total, refs[result])

    down = [reduce(0, 2, 0, "down_sum"), reduce(1, 2, 1, "down_sum")]
    up = [reduce(2, 1, 0, "up_sum"), reduce(3, 1, 1, "up_sum")]
    value, query = reduce(4, 0, 1, "square_sum"), reduce(5, 0, 0, "square_sum")
    vectors = vector_steps(net, work.vectors, refs["vector_land"])

    go(load)
    work.vectors[...] = jnp.zeros_like(work.vectors)
    work.prepare_features()
    go(load, get[0], small, load, get[1])
    load_tokens.wait()
    work.prepare_tokens()
    load_cot.start()
    go(get[0], small, get[1], load, get[2], get[3])
    load_cot.wait()
    work.prepare_cotangent()
    go(small)
    work.prepare_params()
    work.norm_one()
    go(get[0], get[2], get[0])
    work.query_rows()
    go(get[1], get[3])
    work.key_rows()
    go(get[1], get[4], get[5])
    work.attend()
    go(get[2])
    work.middle_rows()
    go(get[3], get[2], get[4])
    work.up_rows(0)
    work.up_rows(1)
    go(get[3], get[5])
    work.up_rows(2)
    work.up_rows(3)
    go(get[4])
    work.term_down(0)
    work.term_down(1)
    go(get[5], get[4])
    work.term_down(2)
    work.term_down(3)
    go(*down)
    go(get[5])
    work.grad_pre_rows(0)
    work.grad_pre_rows(1)
    go(down[0])
    work.grad_pre_rows(2)
    work.grad_pre_rows(3)
    go(down[1])
    work.term_up(0)
    work.term_up(1)
    go(up[0], down[0])
    work.term_up(2)
    work.term_up(3)
    go(up[1], down[1], up[0])
    work.grad_middle_rows()
    go(*down)
    work.attend_back(0)
    go(*down)
    go(up[0], up[1])
    work.attend_back(1)
    go(*down)
    go(up[0], up[1])
    work.attend_back(2)
    go(up[0], up[1])
    work.term_square(2)
    work.term_out()
    go(value)
    work.term_square(0)
    work.term_square(1)
    go(query, up[0], up[1], value, query)
    work.grad_token_rows()
    write_tokens = pltpu.make_async_copy(work.raw, tokens_out, local_sems.at[0])
    write_tokens.start()
    go(vectors, value, up[1], query, vectors)
    write_tokens.wait()
    work.layer_out_rows()
    write_layer = pltpu.make_async_copy(work.raw, layer_out, local_sems.at[1])
    write_layer.start()
    for _ in together(value, query, vectors, up[0], up[1]):
        pass
    total = refs["vector_land"][0, 1]
    place = net.y * 8 + net.z * 2 + net.c
    narrow = refs["narrow"]
    turned = pltpu.roll(total, WID - 24 * place, 1)
    narrow[...] = turned[:, :128]
    chosen = refs["vector_land"][0, 1, pl.ds(B_UP + place // 8, 1)]
    narrow[pl.ds(B_UP, 1)] = pltpu.roll(chosen, WID - 96 * (place % 8), 1)[:, :128]
    writes = [
        pltpu.make_async_copy(refs[name], ref, local_sems.at[2 + slot])
        for slot, (name, ref) in enumerate(
            (("square_sum", square_out), ("up_sum", up_out), ("down_sum", down_out), ("narrow", narrow_out))
        )
    ]
    for write in writes:
        write.start()
    for write in [write_layer] + writes:
        write.wait()


def layer_call(*operands):
    bf, ff = jnp.bfloat16, jnp.float32
    scratch = list(LAYER_SCRATCH.values()) + list(COMM_SCRATCH.values())
    return pl.pallas_call(
        layer_kernel,
        out_shape=(
            jax.ShapeDtypeStruct((ROWS, MOLS, WID), bf),
            jax.ShapeDtypeStruct((ROWS, MOLS, WID), bf),
            jax.ShapeDtypeStruct((4, 24, WID), ff),
            jax.ShapeDtypeStruct((24, 4 * WID), ff),
            jax.ShapeDtypeStruct((2 * BLK, WID), ff),
            jax.ShapeDtypeStruct((16, 128), ff),
        ),
        in_specs=[SMEM] + [VMEM] * 19 + [ANY] * 2,
        out_specs=(ANY,) * 6,
        scratch_shapes=[pltpu.VMEM(shape, dtype) for shape, dtype in scratch]
        + [
            pltpu.SemaphoreType.DMA((SEMS,)),
            pltpu.SemaphoreType.DMA((SEMS,)),
            pltpu.SemaphoreType.DMA((6,)),
            pltpu.SemaphoreType.REGULAR((4,)),
            pltpu.SemaphoreType.REGULAR((3,)),
        ],
        compiler_params=pltpu.CompilerParams(
            collective_id=0, has_side_effects=True, vmem_limit_bytes=64 * 2**20 - 2**17
        ),
    )(*operands)


def finish_kernel(layer, tokens, square, up, down, narrow, *rest):
    outs, sems = rest[:18], rest[18]
    squares = (4, 6, 8, 10)
    pairs = [(layer, outs[0]), (tokens, outs[1]), (up, outs[14]), (down, outs[16])]
    pairs += [(square.at[index], outs[slot]) for index, slot in enumerate(squares)]
    copies = [pltpu.make_async_copy(src, dst, sems.at[slot]) for slot, (src, dst) in enumerate(pairs)]
    for copy in copies:
        copy.start()
    for index, slot in enumerate((2, 3, 5, 7, 9, 11, 12, 13, 17)):
        outs[slot][...] = narrow[index, 0:24]
    outs[15][...] = narrow[9, 0:96]
    for copy in copies:
        copy.wait()


def finish_call(*sums):
    bf, ff = jnp.bfloat16, jnp.float32
    tokens, thin, wide_one = ((ROWS, MOLS, WID), bf), ((24,), ff), ((24, WID), ff)
    shapes = [tokens, tokens, thin, thin] + [wide_one, thin] * 4 + [thin, thin]
    shapes += [((24, 4 * WID), ff), ((96,), ff), ((96, WID), ff), thin]
    return pl.pallas_call(
        finish_kernel,
        out_shape=[jax.ShapeDtypeStruct(shape, dtype) for shape, dtype in shapes],
        in_specs=[ANY] * 5 + [VMEM],
        out_specs=[VMEM if len(shape) == 1 else ANY for shape, dtype in shapes],
        scratch_shapes=[pltpu.SemaphoreType.DMA((8,))],
    )(*sums)


def angle_tables():
    positions = np.arange(PAD)[:, None]
    angles = positions * 10000.0 ** (-2.0 * (np.arange(128)[None, :] % 32) / 64)
    return np.cos(angles).astype(np.float32), np.sin(angles).astype(np.float32)


def body(
    tokens, lengths, feature_proj, ln1_gain, ln1_bias, w_query, b_query, w_key, b_key, w_value, b_value,
    w_out, b_out, ln2_gain, ln2_bias, w_up, b_up, w_down, b_down, cotangent,
):
    cosines, sines = angle_tables()
    sums = layer_call(
        lengths, w_query, w_key, w_value, w_out, w_up, w_down, feature_proj.T, jnp.asarray(cosines), jnp.asarray(sines),
        ln1_gain, ln1_bias, b_query, b_key, b_value, b_out, ln2_gain, ln2_bias, b_down, b_up,
        tokens.transpose(1, 0, 2), cotangent.transpose(1, 0, 2),
    )
    done = finish_call(*sums)
    return (done[0].transpose(1, 0, 2), done[1].transpose(1, 0, 2)) + tuple(done[2:])


def solution(mesh):
    rows, flat = P("fsdp", None), P("fsdp")
    mols = P(("fsdp", "dp"), None, None)
    pairs = (flat, flat, rows, flat, rows, flat, rows, flat, rows, flat, flat, flat, rows, flat, rows, flat)
    return jax.shard_map(
        body,
        mesh=mesh,
        in_specs=(mols, P(("fsdp", "dp")), P()) + pairs + (mols,),
        out_specs=(mols, mols) + pairs,
        check_vma=False,
    )
```

```python
import jax
import jax.numpy as jnp
import numpy as np
from jax import lax
from jax.experimental import pallas as pl
from jax.experimental.pallas import tpu as pltpu
from jax.sharding import PartitionSpec as P


MESH = pl.DeviceIdType.MESH
RING = 4
BLK = 48
WID = 768
HALF = 384
ALL = pl.ds(0, RING)
STEPS = (1, 2, 3)
WAYS = (0, 1)


def rounded(value):
    return value.astype(jnp.bfloat16)


def wide(value):
    return value.astype(jnp.float32)


class Net:
    def __init__(self, send_sems, recv_sems):
        self.send_sems, self.recv_sems, self.count = send_sems, recv_sems, 0
        index = lax.axis_index("fsdp")
        self.x = lax.axis_index("dp")
        self.y = index // (2 * RING)
        self.z = (index // 2) % RING
        self.c = index % 2

    def at(self, y, z, c):
        return {"fsdp": ((y + RING) % RING) * (2 * RING) + ((z + RING) % RING) * 2 + c}

    def sibling(self):
        return self.at(self.y, self.z, 1 - self.c)

    def along(self, axis, step):
        if axis == "y":
            return self.at(self.y + step, self.z, self.c)
        if axis == "z":
            return self.at(self.y, self.z + step, self.c)
        return {"dp": (self.x + step) % RING}

    def peers(self):
        return [self.along(axis, step) for axis in ("x", "y", "z") for step in STEPS]

    def greet(self):
        barrier = pltpu.get_barrier_semaphore()
        peers = [self.sibling()] + self.peers()
        for peer in peers:
            pl.semaphore_signal(barrier, inc=1, device_id=peer, device_id_type=MESH)
        pl.semaphore_wait(barrier, len(peers))

    def send(self, src, dst, device, when=None):
        slot = self.count
        self.count += 1
        copy = pltpu.make_async_remote_copy(
            src_ref=src,
            dst_ref=dst,
            send_sem=self.send_sems.at[slot],
            recv_sem=self.recv_sems.at[slot],
            device_id=device,
            device_id_type=MESH,
        )
        if when is None:
            copy.start()
        else:
            pl.when(when)(copy.start)
        return slot

    def arrived(self, slot, land):
        pltpu.make_async_remote_copy(
            src_ref=land,
            dst_ref=land,
            send_sem=self.send_sems.at[slot],
            recv_sem=self.recv_sems.at[slot],
            device_id=self.sibling(),
            device_id_type=MESH,
        ).wait_recv()

    def left(self, slot, source):
        pltpu.make_async_remote_copy(
            src_ref=source,
            dst_ref=source,
            send_sem=self.send_sems.at[slot],
            recv_sem=self.recv_sems.at[slot],
            device_id=self.sibling(),
            device_id_type=MESH,
        ).wait_send()

    def axes(self, way):
        return ("y", "z") if way == 0 else ("z", "y")

    def place(self, way):
        return (self.y, self.z) if way == 0 else (self.z, self.y)


def wrap(index):
    return (index + RING) % RING


def columns_of(side):
    return pl.ds(HALF * side, HALF)


def slot_of(ref, base, part, side, way, core, y, z):
    if part < 2:
        return ref.at[base + 2 * side + core, y, z, :, columns_of(way)]
    y = pl.ds(base, RING) if isinstance(y, pl.Slice) else base + y
    return ref.at[y, z, 2 * core + way, :, columns_of(side)]


class Traffic:
    def __init__(self, net):
        self.net, self.sent = net, []

    def send(self, src, dst, device, when=None):
        slot = self.net.send(src, dst, device, when)
        self.sent.append((slot, src, when))
        return slot

    def settle(self):
        for slot, src, when in self.sent:
            guarded(when, lambda: self.net.left(slot, src))
        self.sent = []


def guarded(when, work):
    if when is None:
        work()
    else:
        pl.when(when)(work)


Y_FIRST, Z_FIRST, X_LAST = 0, 1, 2


def gather_lane(net, traffic, order, slot):
    mine, theirs = net.c, 1 - net.c
    if order == X_LAST:
        root, others = net.z == net.x, net.z != net.x
        own = slot(mine, net.y, net.z)
        sent = {step: traffic.send(own, own, net.along("y", step), root) for step in STEPS}
        yield
        row = slot(mine, ALL, net.x)

        def take():
            for step in STEPS:
                net.arrived(sent[step], slot(mine, wrap(net.y - step), net.z))

        pl.when(root)(take)
        down = {step: traffic.send(row, row, net.along("z", step), root) for step in STEPS}
        yield
        for step in STEPS:
            pl.when(net.z == wrap(net.x + step))(lambda: net.arrived(down[step], row))
        across = {step: traffic.send(row, row, net.along("x", step)) for step in STEPS}
        pairs = {0: traffic.send(row, row, net.sibling())}
        yield
        for step in STEPS:
            far = slot(mine, ALL, wrap(net.x - step))
            net.arrived(across[step], far)
            pairs[step] = traffic.send(far, far, net.sibling())
        yield
        for step in (0,) + STEPS:
            net.arrived(pairs[step], slot(theirs, ALL, wrap(net.x - step)))
        return

    def at(core, first, second):
        return slot(core, first, second) if order == Y_FIRST else slot(core, second, first)

    p, q = net.place(order)
    first, second = net.axes(order)
    own = at(mine, p, q)
    sent = {step: traffic.send(own, own, net.along(first, step)) for step in STEPS}
    yield
    for step in STEPS:
        net.arrived(sent[step], at(mine, wrap(p - step), q))
    row = at(mine, ALL, q)
    sent = {step: traffic.send(row, row, net.along(second, step)) for step in STEPS}
    pairs = {0: traffic.send(row, row, net.sibling())}
    yield
    for step in STEPS:
        far = at(mine, ALL, wrap(q - step))
        net.arrived(sent[step], far)
        pairs[step] = traffic.send(far, far, net.sibling())
    yield
    for step in (0,) + STEPS:
        net.arrived(pairs[step], at(theirs, ALL, wrap(q - step)))


def gather_steps(net, weights, part, side, orders):
    traffic = Traffic(net)

    def lane(way):
        def slot(core, y, z):
            return slot_of(weights, 4 * part, part, side, way, core, y, z)

        return gather_lane(net, traffic, orders[way], slot)

    yield from together(*[lane(way) for way in WAYS])
    traffic.settle()


def gather_small(net, small):
    traffic = Traffic(net)
    own = small.at[net.y, net.z]
    sent = [traffic.send(own, own, net.along("y", step)) for step in STEPS]
    yield
    for slot, step in zip(sent, STEPS):
        net.arrived(slot, small.at[wrap(net.y - step), net.z])
    row = small.at[ALL, net.z]
    sent = [traffic.send(row, row, net.along("z", step)) for step in STEPS]
    yield
    for slot, step in zip(sent, STEPS):
        net.arrived(slot, small.at[ALL, wrap(net.z - step)])
    traffic.settle()


def load_shards(net, weights, small, stage, small_mine, thin, shards, orders):
    queries, keys, values, outs, ups, downs, vectors = shards
    first = net.c == 0
    traffic = Traffic(net)

    def rows(slot, core):
        return pl.ds(pl.multiple_of(BLK * slot + 24 * core, 8), 24)

    def lane(piece):
        return pl.ds(pl.multiple_of(WID * piece, WID), WID)

    def exchange(slot, mine, theirs):
        outgoing = pl.ds(4 * BLK + 24 * slot, 24)
        stage[rows(slot, net.c)] = mine
        stage[outgoing] = theirs
        return traffic.send(stage.at[outgoing], stage.at[rows(slot, net.c)], net.sibling())


    def heads(group):
        lanes = slice(256 * group, 256 * group + 256)
        return jnp.concatenate([wide(ref[:, lanes]) for ref in (queries, keys, values)], axis=1)

    sent = []
    for early, late in ((heads(0), heads(1)), (heads(2), wide(outs[...]))):
        slot = len(sent)
        sent.append(exchange(slot, jnp.where(first, early, late), jnp.where(first, late, early)))
    thin[...] = jnp.zeros_like(thin)
    for index in range(9):
        thin[index, 0:24] = wide(vectors[index][...])
    thin[9, 0:96] = wide(vectors[9][...])
    for index in range(1, 4):
        thin[pl.ds(9 + index, 1)] = pltpu.roll(thin[pl.ds(9, 1)], 128 - 24 * index, 1)
    pick = rounded(flag(iota((16, 128), 0) == iota((16, 128), 1)))
    small_mine[rows(0, net.c)] = dot_tn(rounded(thin[...]), pick)[0:24]
    sent_small = traffic.send(small_mine.at[rows(0, net.c)], small_mine.at[rows(0, net.c)], net.sibling())
    for side in (0, 1):
        near, away = 2 * side + net.c, 2 * side + 1 - net.c
        sent.append(exchange(2 + side, wide(ups[:, lane(near)]), wide(ups[:, lane(away)])))


    def place(part, side, way, value):
        target = slot_of(weights, 4 * part, part, side, way, net.c, net.y, net.z)

        def put():
            target[...] = value()

        guarded(net.z == net.x if orders[part, side][way] == X_LAST else None, put)

    for side in (0, 1):
        for way in WAYS:
            place(2, side, way, lambda: downs[pl.ds(BLK * way, BLK), columns_of(side)])
    yield
    for slot in (0, 1, 2, 3):
        net.arrived(sent[slot], stage.at[rows(slot, 1 - net.c)])
        for way in WAYS:
            place(slot // 2, slot % 2, way, lambda: rounded(stage[pl.ds(BLK * slot, BLK), columns_of(way)]))
        if slot == 0:
            net.arrived(sent_small, small_mine.at[rows(0, 1 - net.c)])
            small[net.y, net.z] = rounded(small_mine[...])
        if slot < 2:
            yield
    traffic.settle()


def add_all(target, *sources):
    if len(target.shape) > 2:
        for index in range(target.shape[0]):
            add_all(target.at[index], *[source.at[index] for source in sources])
        return
    total = wide(target[...])
    for source in sources:
        total = total + wide(source[...])
    target[...] = rounded(total)


def together(*steps):
    steps = list(steps)
    while steps:
        steps = [step for step in steps if next(step, steps) is not steps]
        if steps:
            yield


def reduce_lane(net, traffic, order, slot, pair, land, total):
    big, mid, little, cross = land

    def group(at):
        return slot(ALL, at) if order != Z_FIRST else slot(at, ALL)

    def pair_group(at):
        return pair.at[ALL, at] if order != Z_FIRST else pair.at[at]

    axis = ("z", "y", "x")[order]
    me = (net.z, net.y, net.x)[order]
    sent = {}
    for step in (2, 1, 3, 0):
        at = wrap(me + step)
        add_all(group(at), pair_group(at))
        if step:
            sent[step] = traffic.send(group(at), big.at[step - 1], net.along(axis, step))
    yield
    for step in STEPS:
        net.arrived(sent[step], big.at[step - 1])
    if order == X_LAST:
        root, row = net.z == net.x, group(me)
        add_all(row, *[big.at[index] for index in range(3)])
        up = {}
        for step in STEPS:
            up[step] = traffic.send(row, mid.at[step - 1], net.along("z", step), net.x == wrap(net.z + step))
        yield

        def spread():
            for step in STEPS:
                net.arrived(up[step], mid.at[step - 1])
            for step in (2, 1, 3, 0):
                at = wrap(net.y + step)
                add_all(slot(at, net.z), *[mid.at[index, at] for index in range(3)])

        pl.when(root)(spread)
        out = {}
        for step in STEPS:
            block = slot(wrap(net.y + step), net.z)
            out[step] = traffic.send(block, little.at[step - 1], net.along("y", step), root)
        yield

        def finish():
            for step in STEPS:
                net.arrived(out[step], little.at[step - 1])
            value = wide(slot(net.y, net.z)[...])
            for index in range(3):
                value = value + wide(little[index])
            total[...] = value

        pl.when(root)(finish)
        back = {step: traffic.send(total, total, net.along("x", step), root) for step in STEPS}
        yield
        for step in STEPS:
            pl.when(net.x == wrap(net.z + step))(lambda: net.arrived(back[step], total))
        return
    p, q = net.place(order)
    first = net.axes(order)[0]

    def block(at):
        return slot(at, q) if order == Y_FIRST else slot(q, at)

    for step in (2, 1, 3, 0):
        at = wrap(p + step)
        add_all(block(at), *[big.at[index, at] for index in range(3)])
        if step:
            sent[step] = traffic.send(block(at), little.at[step - 1], net.along(first, step))
    yield
    for step in STEPS:
        net.arrived(sent[step], little.at[step - 1])
    add_all(block(p), *[little.at[index] for index in range(3)])
    mine = cross.at[net.x]
    mine[...] = block(p)[...]
    sent = {step: traffic.send(mine, mine, net.along("x", step)) for step in STEPS}
    yield
    for step in STEPS:
        net.arrived(sent[step], cross.at[wrap(net.x - step)])
    total[...] = (wide(cross[0]) + wide(cross[1])) + (wide(cross[2]) + wide(cross[3]))


def reduce_steps(net, grads, base, part, side, orders, pair, lands, gates, total, result):
    pair_ready, pair_done, land_ready, land_done = gates
    traffic, sent = Traffic(net), {}

    def whole(way, core):
        if part < 2:
            return grads.at[base + 2 * side + core, ALL, ALL, :, columns_of(way)]
        return grads.at[pl.ds(base, RING), ALL, 2 * core + way, :, columns_of(side)]

    def lane(way):
        def slot(y, z):
            return slot_of(grads, base, part, side, way, net.c, y, z)

        return reduce_lane(net, traffic, orders[way], slot, pair.at[way], lands[way], sum_of(way))

    def sum_of(way):
        if part == 2:
            return result.at[pl.ds(BLK * way, BLK), columns_of(side)]
        return total.at[way]

    if pair_ready is not None:
        pl.semaphore_wait(pair_ready, 1)
    for way in WAYS:
        sent[way] = traffic.send(whole(way, 1 - net.c), pair.at[way], net.sibling())
    yield
    for way in WAYS:
        net.arrived(sent[way], pair.at[way])
    if land_ready is not None:
        pl.semaphore_wait(land_ready, len(net.peers()))
    lanes = together(*[lane(way) for way in WAYS])
    next(lanes)
    if pair_done is not None:
        pl.semaphore_signal(pair_done, inc=1, device_id=net.sibling(), device_id_type=MESH)
    yield
    yield from lanes
    traffic.settle()
    for way in WAYS:
        if part == 2:
            continue
        mine = strip_of(result, part, side, way, net.c)
        mine[...] = total[way, pl.ds(pl.multiple_of(24 * net.c, 8), 24)]
        theirs = total.at[way, pl.ds(pl.multiple_of(24 - 24 * net.c, 8), 24)]
        sent[way] = traffic.send(theirs, mine, net.sibling())
    if land_done is not None:
        for device in net.peers():
            pl.semaphore_signal(land_done, inc=1, device_id=device, device_id_type=MESH)
    yield
    if part < 2:
        for way in WAYS:
            net.arrived(sent[way], strip_of(result, part, side, way, 1 - net.c))
    traffic.settle()


def strip_of(result, part, side, way, core):
    piece = 2 * side + core
    if part == 0:
        return result.at[piece, :, columns_of(way)]
    return result.at[:, pl.ds(pl.multiple_of(WID * piece + HALF * way, HALF), HALF)]


def vector_steps(net, vectors, land):
    traffic = Traffic(net)
    sent = traffic.send(vectors, land.at[0, 0], net.sibling())
    yield
    net.arrived(sent, land.at[0, 0])
    value = vectors[...] + land[0, 0]
    for stage, axis, me in ((1, "z", net.z), (2, "y", net.y), (3, "x", net.x)):
        land[stage, me] = value
        mine = land.at[stage, me]
        sent = [traffic.send(mine, mine, net.along(axis, step)) for step in STEPS]
        yield
        for step in STEPS:
            net.arrived(sent[step - 1], land.at[stage, wrap(me - step)])
        value = ((land[stage, 0] + land[stage, 1]) + land[stage, 2]) + land[stage, 3]
    land[0, 1] = value
    traffic.settle()


ROWS = 202
PAD = 208
MOLS = 4
TOTAL = MOLS * PAD
GROUPS = 3
LANES = 256
FEAT = 128
EPS_NORM = 1e-05
EPS_ATTN = 1e-06
GELU_SCALE = 0.7978845608028654
GELU_CUBIC = 0.044715


def dot(left, right):
    return jnp.dot(left, right, preferred_element_type=jnp.float32)


def dot_nt(left, right):
    return lax.dot_general(left, right, (((1,), (1,)), ((), ())), preferred_element_type=jnp.float32)


def dot_tn(left, right):
    return lax.dot_general(left, right, (((0,), (0,)), ((), ())), preferred_element_type=jnp.float32)


def square(ref, index):
    return ref[index].reshape(WID, WID)


def iota(shape, axis):
    return lax.broadcasted_iota(jnp.int32, shape, axis)


def flag(condition):
    return jnp.where(condition, 1.0, 0.0)


def softplus(value):
    small = jnp.exp(-jnp.abs(value))
    tail = jnp.where(small < 1e-3, small * (1.0 - 0.5 * small), jnp.log(1.0 + small))
    return jnp.maximum(value, 0.0) + tail


def softplus_slope(feature):
    return jnp.where(feature < 1e-3, feature * (1.0 - 0.5 * feature), 1.0 - jnp.exp(-feature))


def centred(value):
    centre = value - jnp.mean(value, axis=-1, keepdims=True)
    scale = lax.rsqrt(jnp.mean(centre * centre, axis=-1, keepdims=True) + EPS_NORM)
    return centre * scale, scale


def column_sum(value):
    return jnp.sum(value, axis=0, keepdims=True)


GAIN1, BIAS1, B_QUERY, B_KEY, B_VALUE, B_OUT, GAIN2, BIAS2, B_DOWN, B_UP = range(10)


class Layer:
    def __init__(self, **refs):
        self.__dict__.update(refs)

    origin = 0

    def row(self, index):
        return self.params[pl.ds(index, 1)]

    def add_row(self, index, value):
        self.vectors[pl.ds(index, 1)] += value

    def block_mask(self):
        shape = (FEAT, LANES)
        return flag(iota(shape, 0) // 32 == iota(shape, 1) // 64)

    def prepare_features(self):
        proj = self.feature_ref[...]
        pick_rows = iota((LANES, 64), 0) % 64
        swap = iota((LANES, 64), 1)
        same = rounded(flag(pick_rows == swap))
        turned = rounded(flag(pick_rows + 32 == swap) - flag(pick_rows == swap + 32))
        spread = rounded(flag(iota((32, FEAT), 1) % 32 == iota((32, FEAT), 0)))
        mask = flag(iota((LANES, FEAT), 0) // 64 == iota((LANES, FEAT), 1) // 32)
        for index, pick in ((0, same), (1, turned)):
            tall = rounded(dot_nt(pick, proj))
            full = dot(tall, spread) * mask
            span = slice(index * LANES, (index + 1) * LANES)
            self.features[span] = rounded(full)
            self.features_back[:, span] = rounded(full.T)

    def prepare_tokens(self):
        zero = jnp.zeros((16, WID), jnp.bfloat16)
        for molecule in range(MOLS):
            start = molecule * PAD
            self.tokens[pl.ds(start + PAD - 16, 16)] = zero
            self.tokens[pl.ds(start, ROWS)] = self.raw[:, molecule, :]

    def prepare_cotangent(self):
        zero = jnp.zeros((16, WID), jnp.bfloat16)
        keep = iota((ROWS, WID), 0) < self.most()
        for molecule in range(MOLS):
            start = molecule * PAD
            self.grad_down[pl.ds(start + PAD - 16, 16)] = zero
            masked = jnp.where(keep, wide(self.raw[:, molecule, :]), 0.0)
            self.grad_down[pl.ds(start, ROWS)] = rounded(masked)
            self.add_row(B_DOWN, column_sum(masked))

    def prepare_params(self):
        columns = wide(self.small[...].reshape(WID, 128))
        rows = columns.T
        self.params[pl.ds(0, 16)] = rows[0:16]
        lanes = iota((8, WID), 1)
        owner = flag(lanes // 192 == iota((8, WID), 0))
        stacked = jnp.concatenate(
            [jnp.broadcast_to(rows[B_UP + k : B_UP + k + 1], (8, WID)) * owner for k in range(4)], axis=0
        )
        stacked = rounded(stacked)
        spread = jnp.zeros((32, WID), jnp.float32)
        for start in range(0, WID, 128):
            source = start + iota((128, WID), 0)
            pick = rounded(flag(96 * ((source // 24) % 8) + source % 24 == iota((128, WID), 1)))
            spread = spread + dot(stacked[:, start : start + 128], pick)
        total = spread[0:8]
        for k in range(1, 4):
            total = total + pltpu.roll(spread[8 * k : 8 * k + 8], 24 * k, 1)
        self.params[pl.ds(16, 8)] = total

    def norm_one(self):
        gain, bias = self.row(GAIN1), self.row(BIAS1)
        for molecule in range(MOLS):
            rows = pl.ds(molecule * PAD, PAD)
            normed, _ = centred(wide(self.tokens[rows]))
            self.normed_one[rows] = rounded(normed * gain + bias)

    def tables(self):
        return [
            jnp.concatenate([jnp.concatenate([table[...]] * 2, axis=1)] * MOLS, axis=0)
            for table in (self.cosines, self.sines)
        ]

    def project(self, group, kind, row):
        lanes = slice(kind * LANES, (kind + 1) * LANES)
        bias = self.params[pl.ds(row, 1), group * LANES : (group + 1) * LANES]
        return dot(self.normed_one[...], self.columns(group, lanes)) + bias

    def feature_rows(self, value):
        cosines, sines = self.tables()
        turned = jnp.concatenate([rounded(value * cosines), rounded(value * sines)], axis=1)
        return softplus(dot(turned, self.features[...]))

    def columns(self, piece, lanes):
        return self.weights[piece, :, :, :, lanes].reshape(WID, LANES)

    def attend(self, group):
        lanes = slice(group * LANES, (group + 1) * LANES)
        thin = slice(group * FEAT, (group + 1) * FEAT)
        keep = jnp.concatenate(
            [iota((PAD, FEAT), 0) < self.lengths[molecule] for molecule in range(MOLS)], axis=0
        )
        self.feat_query[:, thin] = rounded(self.feature_rows(self.project(group, 0, B_QUERY)))
        feat = self.feature_rows(self.project(group, 1, B_KEY))
        self.feat_key[:, thin] = rounded(jnp.where(keep, feat, 0.0))
        mask = self.block_mask()
        mask = jnp.concatenate([mask, mask], axis=1)
        ones = jnp.ones((PAD, LANES), jnp.bfloat16)
        value = self.project(group, 2, B_VALUE)
        for molecule in range(MOLS):
            rows = slice(molecule * PAD, (molecule + 1) * PAD)
            length = self.lengths[molecule]
            valid = jnp.where(iota((PAD, LANES), 0) < length, value[rows], 0.0)
            level = column_sum(valid) / wide(jnp.maximum(length, 1))
            self.levels[pl.ds(8 * molecule, 1), lanes] = level
            low = rounded(value[rows] - level)
            self.values[rows, lanes] = low
            state = rounded(dot_tn(self.feat_key[rows, thin], jnp.concatenate([low, ones], axis=1)) * mask)
            both = dot(self.feat_query[rows, thin], state)
            mixed = level + (both[:, :LANES] - EPS_ATTN * level) / (both[:, LANES:] + EPS_ATTN)
            self.mixed[rows, lanes] = rounded(mixed)

    def middle_rows(self):
        for molecule in range(MOLS):
            rows = slice(molecule * PAD, (molecule + 1) * PAD)
            middle = wide(self.tokens[rows]) + self.row(B_OUT) + dot(self.mixed[rows], square(self.weights, 3))
            self.middle[rows] = middle
            normed, _ = centred(middle)
            self.normed_two[rows] = rounded(normed * self.row(GAIN2) + self.row(BIAS2))

    def up_rows(self, quarter):
        for group in range(GROUPS):
            lanes = slice(group * LANES, (group + 1) * LANES)
            pre = dot(self.normed_two[...], self.columns(4 + quarter, lanes))
            pre = pre + self.params[pl.ds(16 + quarter, 1), lanes]
            squared = pre * pre
            gate = 0.5 + 0.5 * jnp.tanh(pre * (GELU_SCALE + GELU_SCALE * GELU_CUBIC * squared))
            hidden = pre * gate
            slope = gate + (hidden - hidden * gate) * (
                2.0 * GELU_SCALE + 6.0 * GELU_SCALE * GELU_CUBIC * squared
            )
            self.hidden[self.origin + quarter, :, lanes] = rounded(hidden)
            self.slope[self.origin + quarter, :, lanes] = rounded(slope)

    def blocks(self, value):
        return rounded(value).reshape(4, 4, BLK, WID)

    def store_term(self, slot, value):
        self.grads[slot] = self.blocks(value)

    def term_down(self, quarter):
        self.store_term(quarter, dot_tn(self.hidden[self.origin + quarter], self.grad_down[...]))

    def grad_pre_rows(self, quarter):
        for group in range(GROUPS):
            lanes = slice(group * LANES, (group + 1) * LANES)
            grad_hidden = dot_nt(self.grad_down[...], self.weights[8 + quarter].reshape(WID, WID)[lanes])
            grad_pre = rounded(grad_hidden * wide(self.slope[self.origin + quarter, :, lanes]))
            self.slope[self.origin + quarter, :, lanes] = grad_pre
            self.vectors[pl.ds(B_UP + quarter, 1), lanes] += column_sum(wide(grad_pre))

    def term_up(self, quarter):
        self.store_term(4 + quarter, dot_tn(self.normed_two[...], self.slope[self.origin + quarter]))

    def norm_back(self, grad, inputs, gain, bias):
        normed, scale = centred(inputs)
        self.add_row(gain, column_sum(grad * normed))
        self.add_row(bias, column_sum(grad))
        scaled = grad * self.row(gain)
        first = jnp.mean(scaled, axis=-1, keepdims=True)
        second = jnp.mean(scaled * normed, axis=-1, keepdims=True)
        return scale * (scaled - first - normed * second)

    def grad_two_columns(self, group):
        lanes = slice(group * LANES, (group + 1) * LANES)
        whole = dot_nt(self.slope[self.origin + 0], self.weights[4].reshape(WID, WID)[lanes])
        for quarter in range(1, 4):
            whole += dot_nt(self.slope[self.origin + quarter], self.weights[4 + quarter].reshape(WID, WID)[lanes])
        self.grad_middle[:, lanes] = whole

    def grad_middle_rows(self):
        for molecule in range(MOLS):
            rows = slice(molecule * PAD, (molecule + 1) * PAD)
            back = self.norm_back(self.grad_middle[rows], self.middle[rows], GAIN2, BIAS2)
            grad = wide(self.grad_down[rows]) + back
            self.grad_middle[rows] = grad
            low = rounded(grad)
            self.slope[self.origin + 3, rows] = low
            self.add_row(B_OUT, column_sum(wide(low)))

    def term_out(self):
        self.weights[7] = self.blocks(dot_tn(self.mixed[...], self.slope[self.origin + 3]))

    def attend_back(self, group):
        mask = self.block_mask()
        mask = jnp.concatenate([mask, mask], axis=1)
        ones = jnp.ones((PAD, LANES), jnp.bfloat16)
        cosines, sines = [jnp.concatenate([table[...]] * 2, axis=1) for table in (self.cosines, self.sines)]
        thin = slice(group * FEAT, (group + 1) * FEAT)
        lanes = slice(group * LANES, (group + 1) * LANES)
        grad_mixed, feat_queries, feat_keys = self.normed_two, self.feat_query, self.feat_key
        grad_mixed[:, lanes] = rounded(dot_nt(self.slope[self.origin + 3], self.weights[3].reshape(WID, WID)[lanes]))

        for molecule in range(MOLS):
            rows = slice(molecule * PAD, (molecule + 1) * PAD)
            feat_query, feat_key = feat_queries[rows, thin], feat_keys[rows, thin]
            values = jnp.concatenate([self.values[rows, lanes], ones], axis=1)
            state = rounded(dot_tn(feat_key, values) * mask)
            both = dot(feat_query, state)
            inverse = 1.0 / (both[:, LANES:] + EPS_ATTN)
            grad_num = wide(grad_mixed[rows, lanes]) * inverse
            offset = EPS_ATTN * self.levels[pl.ds(8 * molecule, 1), lanes]
            grad_den = -grad_num * ((both[:, :LANES] - offset) * inverse)
            grad_both = jnp.concatenate([rounded(grad_num), rounded(grad_den)], axis=1)
            grad_state = rounded(dot_tn(feat_query, grad_both) * mask)
            grad_query = dot_nt(grad_both, state)
            grad_key = dot_nt(values, grad_state)
            grad_value = rounded(dot(feat_key, grad_state[:, :LANES]))
            self.slope[self.origin + group, rows, 2 * LANES : 3 * LANES] = grad_value
            self.vectors[pl.ds(B_VALUE, 1), lanes] += column_sum(wide(grad_value))
            for slot, row, feat, grad in (
                (0, B_QUERY, feat_query, grad_query),
                (1, B_KEY, feat_key, grad_key),
            ):
                turned = dot(rounded(grad * softplus_slope(wide(feat))), self.features_back[...])
                low = rounded(cosines * turned[:, :LANES] + sines * turned[:, LANES:])
                self.slope[self.origin + group, rows, slot * LANES : (slot + 1) * LANES] = low
                self.vectors[pl.ds(row, 1), lanes] += column_sum(wide(low))
    def term_square(self, group):
        self.weights[4 + (2, 0, 1)[group]] = self.blocks(dot_tn(self.normed_one[...], self.slope[self.origin + group]))

    def grad_token_rows(self, first):
        pair = pl.ds(first * PAD, 2 * PAD)
        whole = dot_nt(self.slope[self.origin + 0, pair], square(self.weights, 0))
        for index in (1, 2):
            whole += dot_nt(self.slope[self.origin + index, pair], square(self.weights, index))
        for molecule in (first, first + 1):
            rows = slice(molecule * PAD, (molecule + 1) * PAD)
            own = whole[(molecule - first) * PAD : (molecule - first + 1) * PAD]
            grad = self.grad_middle[rows] + self.norm_back(own, wide(self.tokens[rows]), GAIN1, BIAS1)
            self.raw[:, molecule, :] = rounded(grad[:ROWS])

    def most(self):
        lengths = self.lengths
        return jnp.maximum(jnp.maximum(lengths[0], lengths[1]), jnp.maximum(lengths[2], lengths[3]))

    def layer_out_rows(self, molecule):
        rows = pl.ds(molecule * PAD, PAD)
        result = self.middle[rows] + self.row(B_DOWN)
        for quarter in range(4):
            result += dot(self.hidden[self.origin + quarter, rows], square(self.weights, 8 + quarter))
        keep = iota((ROWS, WID), 0) < self.most()
        self.raw[:, molecule, :] = rounded(jnp.where(keep, result[:ROWS], 0.0))


LAYER_SCRATCH = dict(
    raw=((ROWS, MOLS, WID), jnp.bfloat16),
    tokens=((TOTAL, WID), jnp.bfloat16),
    grad_down=((TOTAL, WID), jnp.bfloat16),
    normed_one=((TOTAL, WID), jnp.bfloat16),
    values=((TOTAL, WID), jnp.bfloat16),
    mixed=((TOTAL, WID), jnp.bfloat16),
    normed_two=((TOTAL, WID), jnp.bfloat16),
    feat_query=((TOTAL, HALF), jnp.bfloat16),
    feat_key=((TOTAL, HALF), jnp.bfloat16),
    levels=((8 * MOLS, WID), jnp.float32),
    middle=((TOTAL, WID), jnp.float32),
    grad_middle=((TOTAL, WID), jnp.float32),
    hidden=((4, TOTAL, WID), jnp.bfloat16),
    slope=((4, TOTAL, WID), jnp.bfloat16),
    features=((2 * LANES, FEAT), jnp.bfloat16),
    features_back=((FEAT, 2 * LANES), jnp.bfloat16),
    params=((24, WID), jnp.float32),
    vectors=((16, WID), jnp.float32),
    grads=((8, 4, 4, BLK, WID), jnp.bfloat16),
    weights=((12, 4, 4, BLK, WID), jnp.bfloat16),
    small=((4, 4, BLK, 128), jnp.bfloat16),
)


VMEM = pl.BlockSpec(memory_space=pltpu.VMEM)
SMEM = pl.BlockSpec(memory_space=pltpu.SMEM)
ANY = pl.BlockSpec(memory_space=pl.ANY)
SEMS = 320


PLAIN = (Y_FIRST, Z_FIRST)
ROUTES = {(part, side): PLAIN for part in (0, 1, 2) for side in (0, 1)}
RETURNS = {(part, side): PLAIN for part in (0, 1, 2) for side in (0, 1)}
COMM_SCRATCH = dict(
    pair=((2, 4, 4, BLK, HALF), jnp.bfloat16),
    big=((3, 2, 3, 4, BLK, HALF), jnp.bfloat16),
    little=((3, 2, 3, BLK, HALF), jnp.bfloat16),
    cross=((3, 2, 4, BLK, HALF), jnp.bfloat16),
    total=((4, 2, BLK, HALF), jnp.float32),
    square_sum=((4, 24, WID), jnp.float32),
    up_sum=((24, 4 * WID), jnp.float32),
    down_sum=((2 * BLK, WID), jnp.float32),
    vector_land=((4, 4, 16, WID), jnp.float32),
    narrow=((16, 128), jnp.float32),
    small_mine=((BLK, 128), jnp.float32),
)
def layer_kernel(
    lengths, queries, keys, values, outs, ups, downs, feature_ref, cosines, sines, *rest,
):
    vectors_in, rest = rest[:10], rest[10:]
    tokens_in, cot_in, layer_out, tokens_out, square_out, up_out, down_out, narrow_out = rest[:8]
    scratch = rest[8:]
    names = list(LAYER_SCRATCH) + list(COMM_SCRATCH)
    refs = dict(zip(names, scratch))
    send_sems, recv_sems, local_sems, pair_gates, land_gates = scratch[len(names):]
    net = Net(send_sems, recv_sems)
    work = Layer(
        lengths=lengths, feature_ref=feature_ref, cosines=cosines, sines=sines,
        **{name: refs[name] for name in LAYER_SCRATCH},
    )
    work.origin = net.x // RING
    load_tokens = pltpu.make_async_copy(tokens_in, work.raw, local_sems.at[0])
    load_cot = pltpu.make_async_copy(cot_in, work.raw, local_sems.at[1])
    load_tokens.start()
    net.greet()

    shards = (queries, keys, values, outs, ups, downs, vectors_in)
    load = load_shards(
        net, work.weights, work.small, work.grad_middle, refs["small_mine"], refs["narrow"], shards, ROUTES
    )
    small = gather_small(net, work.small)
    get = [
        gather_steps(net, work.weights, part, side, ROUTES[part, side])
        for part in (0, 1, 2)
        for side in (0, 1)
    ]

    def go(*steps):
        for step in steps:
            next(step, None)

    def reduce(order, part, side, result):
        lands = [
            (
                refs["big"].at[order % 3, way],
                None,
                refs["little"].at[order % 3, way],
                refs["cross"].at[order % 3, way],
            )
            for way in WAYS
        ]
        gates = (
            pair_gates.at[order - 1] if order >= 1 else None,
            pair_gates.at[order] if order < 5 else None,
            land_gates.at[order - 3] if order >= 3 else None,
            land_gates.at[order] if order < 3 else None,
        )
        return reduce_steps(
            net, work.weights if part == 0 else work.grads, 4 * (part < 2), part, side, RETURNS[part, side], refs["pair"], lands, gates,
            refs["total"].at[order - 2] if order >= 2 else None, refs[result],
        )

    down = [reduce(0, 2, 0, "down_sum"), reduce(1, 2, 1, "down_sum")]
    up = [reduce(2, 1, 0, "up_sum"), reduce(3, 1, 1, "up_sum")]
    value, query = reduce(4, 0, 1, "square_sum"), reduce(5, 0, 0, "square_sum")
    vectors = vector_steps(net, work.vectors, refs["vector_land"])

    write_tokens = pltpu.make_async_copy(work.raw, tokens_out, local_sems.at[0])
    write_layer = pltpu.make_async_copy(work.raw, layer_out, local_sems.at[1])
    go(load)
    work.vectors[...] = jnp.zeros_like(work.vectors)
    work.prepare_features()
    go(load, get[0], small, load, get[1])
    load_tokens.wait()
    work.prepare_tokens()
    load_cot.start()
    go(get[0], small, get[1], load, get[2], get[3], get[4], get[5])
    load_cot.wait()
    work.prepare_cotangent()
    go(small)
    work.prepare_params()
    work.norm_one()
    go(get[0], get[0])
    work.attend(1)
    go(get[1], get[2], get[3])
    work.attend(0)
    go(get[5], get[4], get[1])
    work.attend(2)
    go(get[2])
    work.middle_rows()
    go(get[2])
    work.up_rows(1)
    work.up_rows(0)
    go(get[3])
    work.term_down(1)
    work.term_down(0)
    go(get[3])
    work.up_rows(3)
    work.up_rows(2)
    work.term_down(2)
    go(get[5])
    work.term_down(3)
    go(down[0], get[4], down[0], get[5], down[1], get[4])
    work.grad_pre_rows(0)
    work.term_up(0)
    work.grad_pre_rows(3)
    go(down[1])
    work.grad_pre_rows(1)
    work.term_up(1)
    go(up[0])
    work.grad_pre_rows(2)
    work.grad_two_columns(0)
    go(down[0])
    work.term_up(3)
    work.grad_two_columns(2)
    go(up[0])
    work.term_up(2)
    work.grad_two_columns(1)
    go(down[1])
    work.grad_middle_rows()
    go(down[0])
    work.attend_back(0)
    work.term_out()
    go(up[1], up[0], down[1], down[0])
    work.attend_back(2)
    go(up[1])
    work.term_square(0)
    go(up[0], down[1], value)
    work.attend_back(1)
    go(value)
    work.term_square(1)
    work.term_square(2)
    go(query, up[0], up[1], query)
    work.grad_token_rows(0)
    go(value)
    work.grad_token_rows(2)
    write_tokens.start()
    go(vectors, up[1], vectors, query, value)
    write_tokens.wait()
    work.layer_out_rows(2)
    go(up[0], vectors)
    work.layer_out_rows(1)
    go(down[1], query)
    work.layer_out_rows(0)
    go(value, down[0], vectors, up[1], value, up[1], query)
    work.layer_out_rows(3)
    write_layer.start()
    go(vectors, query)
    total = refs["vector_land"][0, 1]
    place = net.y * 8 + net.z * 2 + net.c
    narrow = refs["narrow"]
    turned = pltpu.roll(total, WID - 24 * place, 1)
    narrow[...] = turned[:, :128]
    chosen = refs["vector_land"][0, 1, pl.ds(B_UP + place // 8, 1)]
    narrow[pl.ds(B_UP, 1)] = pltpu.roll(chosen, WID - 96 * (place % 8), 1)[:, :128]
    writes = [
        pltpu.make_async_copy(refs[name], ref, local_sems.at[2 + slot])
        for slot, (name, ref) in enumerate(
            (("square_sum", square_out), ("up_sum", up_out), ("down_sum", down_out), ("narrow", narrow_out))
        )
    ]
    for write in writes:
        write.start()
    for write in [write_layer] + writes:
        write.wait()


def layer_call(*operands):
    bf, ff = jnp.bfloat16, jnp.float32
    scratch = list(LAYER_SCRATCH.values()) + list(COMM_SCRATCH.values())
    return pl.pallas_call(
        layer_kernel,
        out_shape=(
            jax.ShapeDtypeStruct((ROWS, MOLS, WID), bf),
            jax.ShapeDtypeStruct((ROWS, MOLS, WID), bf),
            jax.ShapeDtypeStruct((4, 24, WID), ff),
            jax.ShapeDtypeStruct((24, 4 * WID), ff),
            jax.ShapeDtypeStruct((2 * BLK, WID), ff),
            jax.ShapeDtypeStruct((16, 128), ff),
        ),
        in_specs=[SMEM] + [VMEM] * 19 + [ANY] * 2,
        out_specs=(ANY,) * 6,
        scratch_shapes=[pltpu.VMEM(shape, dtype) for shape, dtype in scratch]
        + [
            pltpu.SemaphoreType.DMA((SEMS,)),
            pltpu.SemaphoreType.DMA((SEMS,)),
            pltpu.SemaphoreType.DMA((6,)),
            pltpu.SemaphoreType.REGULAR((5,)),
            pltpu.SemaphoreType.REGULAR((3,)),
        ],
        compiler_params=pltpu.CompilerParams(
            collective_id=0, has_side_effects=True, vmem_limit_bytes=64 * 2**20 - 2**17
        ),
    )(*operands)


def finish_kernel(layer, tokens, square, up, down, narrow, *outs):
    outs[0][...] = layer[...]
    outs[1][...] = tokens[...]
    for group, index in ((0, 2), (1, 0), (2, 1)):
        for kind, slot in enumerate((4, 6, 8)):
            outs[slot][:, group * LANES : (group + 1) * LANES] = square[index, :, kind * LANES : (kind + 1) * LANES]
    outs[10][...] = square[3]
    outs[14][...] = up[...]
    outs[16][...] = down[...]
    for index, slot in enumerate((2, 3, 5, 7, 9, 11, 12, 13, 17)):
        outs[slot][...] = narrow[index, 0:24]
    outs[15][...] = narrow[9, 0:96]


def finish_call(*sums):
    bf, ff = jnp.bfloat16, jnp.float32
    tokens, thin, wide_one = ((ROWS, MOLS, WID), bf), ((24,), ff), ((24, WID), ff)
    shapes = [tokens, tokens, thin, thin] + [wide_one, thin] * 4 + [thin, thin]
    shapes += [((24, 4 * WID), ff), ((96,), ff), ((96, WID), ff), thin]
    return pl.pallas_call(
        finish_kernel,
        out_shape=[jax.ShapeDtypeStruct(shape, dtype) for shape, dtype in shapes],
        in_specs=[VMEM] * 6,
        out_specs=[VMEM] * 18,
    )(*sums)


def angle_tables():
    positions = np.arange(PAD)[:, None]
    angles = positions * 10000.0 ** (-2.0 * (np.arange(128)[None, :] % 32) / 64)
    return np.cos(angles).astype(np.float32), np.sin(angles).astype(np.float32)


def body(
    tokens, lengths, feature_proj, ln1_gain, ln1_bias, w_query, b_query, w_key, b_key, w_value, b_value,
    w_out, b_out, ln2_gain, ln2_bias, w_up, b_up, w_down, b_down, cotangent,
):
    cosines, sines = angle_tables()
    sums = layer_call(
        lengths, w_query, w_key, w_value, w_out, w_up, w_down, feature_proj.T, jnp.asarray(cosines), jnp.asarray(sines),
        ln1_gain, ln1_bias, b_query, b_key, b_value, b_out, ln2_gain, ln2_bias, b_down, b_up,
        tokens.transpose(1, 0, 2), cotangent.transpose(1, 0, 2),
    )
    done = finish_call(*sums)
    return (done[0].transpose(1, 0, 2), done[1].transpose(1, 0, 2)) + tuple(done[2:])


def solution(mesh):
    rows, flat = P("fsdp", None), P("fsdp")
    mols = P(("fsdp", "dp"), None, None)
    pairs = (flat, flat, rows, flat, rows, flat, rows, flat, rows, flat, flat, flat, rows, flat, rows, flat)
    return jax.shard_map(
        body,
        mesh=mesh,
        in_specs=(mols, P(("fsdp", "dp")), P()) + pairs + (mols,),
        out_specs=(mols, mols) + pairs,
        check_vma=False,
    )
```

```python
import jax
import jax.numpy as jnp
import numpy as np
from jax import lax
from jax.experimental import pallas as pl
from jax.experimental.pallas import tpu as pltpu
from jax.sharding import PartitionSpec as P


MESH = pl.DeviceIdType.MESH
RING = 4
BLK = 48
WID = 768
HALF = 384
ALL = pl.ds(0, RING)
STEPS = (1, 2, 3)
WAYS = (0, 1)


def rounded(value):
    return value.astype(jnp.bfloat16)


def wide(value):
    return value.astype(jnp.float32)


class Net:
    def __init__(self, send_sems, recv_sems):
        self.send_sems, self.recv_sems, self.count = send_sems, recv_sems, 0
        index = lax.axis_index("fsdp")
        self.x = lax.axis_index("dp")
        self.y = index // (2 * RING)
        self.z = (index // 2) % RING
        self.c = index % 2

    def at(self, y, z, c):
        return {"fsdp": ((y + RING) % RING) * (2 * RING) + ((z + RING) % RING) * 2 + c}

    def sibling(self):
        return self.at(self.y, self.z, 1 - self.c)

    def along(self, axis, step):
        if axis == "y":
            return self.at(self.y + step, self.z, self.c)
        if axis == "z":
            return self.at(self.y, self.z + step, self.c)
        return {"dp": (self.x + step) % RING}

    def peers(self):
        return [self.along(axis, step) for axis in ("x", "y", "z") for step in STEPS]

    def greet(self):
        barrier = pltpu.get_barrier_semaphore()
        peers = [self.sibling()] + self.peers()
        for peer in peers:
            pl.semaphore_signal(barrier, inc=1, device_id=peer, device_id_type=MESH)
        pl.semaphore_wait(barrier, len(peers))

    def send(self, src, dst, device):
        slot = self.count
        self.count += 1
        copy = pltpu.make_async_remote_copy(
            src_ref=src,
            dst_ref=dst,
            send_sem=self.send_sems.at[slot],
            recv_sem=self.recv_sems.at[slot],
            device_id=device,
            device_id_type=MESH,
        )
        copy.start()
        return slot

    def arrived(self, slot, land):
        pltpu.make_async_remote_copy(
            src_ref=land,
            dst_ref=land,
            send_sem=self.send_sems.at[slot],
            recv_sem=self.recv_sems.at[slot],
            device_id=self.sibling(),
            device_id_type=MESH,
        ).wait_recv()

    def left(self, slot, source):
        pltpu.make_async_remote_copy(
            src_ref=source,
            dst_ref=source,
            send_sem=self.send_sems.at[slot],
            recv_sem=self.recv_sems.at[slot],
            device_id=self.sibling(),
            device_id_type=MESH,
        ).wait_send()

    def axes(self, way):
        return ("y", "z") if way == 0 else ("z", "y")

    def place(self, way):
        return (self.y, self.z) if way == 0 else (self.z, self.y)


def wrap(index):
    return (index + RING) % RING


def columns_of(side):
    return pl.ds(HALF * side, HALF)


def slot_of(ref, base, part, side, way, core, y, z):
    if part < 2:
        return ref.at[base + 2 * side + core, y, z, :, columns_of(way)]
    y = pl.ds(base, RING) if isinstance(y, pl.Slice) else base + y
    return ref.at[y, z, 2 * core + way, :, columns_of(side)]


class Traffic:
    def __init__(self, net):
        self.net, self.sent = net, []

    def send(self, src, dst, device):
        slot = self.net.send(src, dst, device)
        self.sent.append((slot, src))
        return slot

    def settle(self):
        for slot, src in self.sent:
            self.net.left(slot, src)
        self.sent = []


Y_FIRST, Z_FIRST = 0, 1


def gather_lane(net, traffic, order, slot):
    mine, theirs = net.c, 1 - net.c
    def at(core, first, second):
        return slot(core, first, second) if order == Y_FIRST else slot(core, second, first)

    p, q = net.place(order)
    first, second = net.axes(order)
    own = at(mine, p, q)
    sent = {step: traffic.send(own, own, net.along(first, step)) for step in STEPS}
    yield
    for step in STEPS:
        net.arrived(sent[step], at(mine, wrap(p - step), q))
    row = at(mine, ALL, q)
    sent = {step: traffic.send(row, row, net.along(second, step)) for step in STEPS}
    pairs = {0: traffic.send(row, row, net.sibling())}
    yield
    for step in STEPS:
        far = at(mine, ALL, wrap(q - step))
        net.arrived(sent[step], far)
        pairs[step] = traffic.send(far, far, net.sibling())
    yield
    for step in (0,) + STEPS:
        net.arrived(pairs[step], at(theirs, ALL, wrap(q - step)))


def gather_steps(net, weights, part, side):
    traffic = Traffic(net)

    def lane(way):
        def slot(core, y, z):
            return slot_of(weights, 4 * part, part, side, way, core, y, z)

        return gather_lane(net, traffic, way, slot)

    yield from together(*[lane(way) for way in WAYS])
    traffic.settle()


def gather_small(net, small):
    traffic = Traffic(net)
    own = small.at[net.y, net.z]
    sent = [traffic.send(own, own, net.along("y", step)) for step in STEPS]
    yield
    for slot, step in zip(sent, STEPS):
        net.arrived(slot, small.at[wrap(net.y - step), net.z])
    row = small.at[ALL, net.z]
    sent = [traffic.send(row, row, net.along("z", step)) for step in STEPS]
    yield
    for slot, step in zip(sent, STEPS):
        net.arrived(slot, small.at[ALL, wrap(net.z - step)])
    traffic.settle()


def load_shards(net, weights, small, stage, small_mine, thin, shards):
    queries, keys, values, outs, ups, downs, vectors = shards
    first = net.c == 0
    traffic, sent = Traffic(net), []

    def rows(slot, core):
        return pl.ds(pl.multiple_of(BLK * slot + 24 * core, 8), 24)

    def lane(piece):
        return pl.ds(pl.multiple_of(WID * piece, WID), WID)

    def exchange(mine, theirs):
        slot = len(sent)
        outgoing = pl.ds(4 * BLK + 24 * slot, 24)
        stage[rows(slot, net.c)] = mine
        stage[outgoing] = theirs
        sent.append(traffic.send(stage.at[outgoing], stage.at[rows(slot, net.c)], net.sibling()))

    def heads(group):
        lanes = slice(256 * group, 256 * group + 256)
        return jnp.concatenate([wide(ref[:, lanes]) for ref in (queries, keys, values)], axis=1)

    def either(early, late):
        exchange(jnp.where(first, early, late), jnp.where(first, late, early))

    def place(slot):
        net.arrived(sent[slot], stage.at[rows(slot, 1 - net.c)])
        piece = 4 * (slot // 2) + 2 * (slot % 2) + net.c
        weights[piece, net.y, net.z] = rounded(stage[pl.ds(BLK * slot, BLK)])

    either(heads(0), heads(1))
    thin[...] = jnp.zeros_like(thin)
    for index in range(9):
        thin[index, 0:24] = wide(vectors[index][...])
    thin[9, 0:96] = wide(vectors[9][...])
    for index in range(1, 4):
        thin[pl.ds(9 + index, 1)] = pltpu.roll(thin[pl.ds(9, 1)], 128 - 24 * index, 1)
    pick = rounded(flag(iota((16, 128), 0) == iota((16, 128), 1)))
    small_mine[rows(0, net.c)] = dot_tn(rounded(thin[...]), pick)[0:24]
    sent_small = traffic.send(small_mine.at[rows(0, net.c)], small_mine.at[rows(0, net.c)], net.sibling())
    yield
    place(0)
    net.arrived(sent_small, small_mine.at[rows(0, 1 - net.c)])
    small[net.y, net.z] = rounded(small_mine[...])
    yield
    either(heads(2), wide(outs[...]))
    for side in (0, 1):
        exchange(wide(ups[:, lane(2 * side + net.c)]), wide(ups[:, lane(2 * side + 1 - net.c)]))
    for way in WAYS:
        weights[8 + net.y, net.z, 2 * net.c + way] = downs[pl.ds(BLK * way, BLK)]
    yield
    place(1)
    yield
    place(2)
    place(3)
    traffic.settle()


def add_all(target, *sources):
    if len(target.shape) > 2:
        for index in range(target.shape[0]):
            add_all(target.at[index], *[source.at[index] for source in sources])
        return
    total = wide(target[...])
    for source in sources:
        total = total + wide(source[...])
    target[...] = rounded(total)


def together(*steps):
    steps = list(steps)
    while steps:
        steps = [step for step in steps if next(step, steps) is not steps]
        if steps:
            yield


def reduce_lane(net, traffic, order, slot, pair, land, total):
    big, little, cross = land

    def group(at):
        return slot(ALL, at) if order != Z_FIRST else slot(at, ALL)

    def pair_group(at):
        return pair.at[ALL, at] if order != Z_FIRST else pair.at[at]

    axis = net.axes(order)[1]
    me = net.place(order)[1]
    sent = {}
    for step in (2, 1, 3, 0):
        at = wrap(me + step)
        add_all(group(at), pair_group(at))
        if step:
            sent[step] = traffic.send(group(at), big.at[step - 1], net.along(axis, step))
    yield
    for step in STEPS:
        net.arrived(sent[step], big.at[step - 1])
    p, q = net.place(order)
    first = net.axes(order)[0]

    def block(at):
        return slot(at, q) if order == Y_FIRST else slot(q, at)

    for step in (2, 1, 3, 0):
        at = wrap(p + step)
        add_all(block(at), *[big.at[index, at] for index in range(3)])
        if step:
            sent[step] = traffic.send(block(at), little.at[step - 1], net.along(first, step))
    yield
    for step in STEPS:
        net.arrived(sent[step], little.at[step - 1])
    add_all(block(p), *[little.at[index] for index in range(3)])
    mine = cross.at[net.x]
    mine[...] = block(p)[...]
    sent = {step: traffic.send(mine, mine, net.along("x", step)) for step in STEPS}
    yield
    for step in STEPS:
        net.arrived(sent[step], cross.at[wrap(net.x - step)])
    total[...] = (wide(cross[0]) + wide(cross[1])) + (wide(cross[2]) + wide(cross[3]))


def reduce_steps(net, grads, base, part, side, pair, lands, gates, total, result):
    pair_ready, pair_done, land_ready, land_done = gates
    traffic, sent = Traffic(net), {}

    def whole(way, core):
        if part < 2:
            return grads.at[base + 2 * side + core, ALL, ALL, :, columns_of(way)]
        return grads.at[pl.ds(base, RING), ALL, 2 * core + way, :, columns_of(side)]

    def lane(way):
        def slot(y, z):
            return slot_of(grads, base, part, side, way, net.c, y, z)

        return reduce_lane(net, traffic, way, slot, pair.at[way], lands[way], sum_of(way))

    def sum_of(way):
        if part == 2:
            return result.at[pl.ds(BLK * way, BLK), columns_of(side)]
        return total.at[way]

    if pair_ready is not None:
        pl.semaphore_wait(pair_ready, 1)
    for way in WAYS:
        sent[way] = traffic.send(whole(way, 1 - net.c), pair.at[way], net.sibling())
    yield
    for way in WAYS:
        net.arrived(sent[way], pair.at[way])
    if land_ready is not None:
        pl.semaphore_wait(land_ready, len(net.peers()))
    lanes = together(*[lane(way) for way in WAYS])
    next(lanes)
    if pair_done is not None:
        pl.semaphore_signal(pair_done, inc=1, device_id=net.sibling(), device_id_type=MESH)
    yield
    yield from lanes
    traffic.settle()
    for way in WAYS:
        if part == 2:
            continue
        mine = strip_of(result, part, side, way, net.c)
        mine[...] = total[way, pl.ds(pl.multiple_of(24 * net.c, 8), 24)]
        theirs = total.at[way, pl.ds(pl.multiple_of(24 - 24 * net.c, 8), 24)]
        sent[way] = traffic.send(theirs, mine, net.sibling())
    if land_done is not None:
        for device in net.peers():
            pl.semaphore_signal(land_done, inc=1, device_id=device, device_id_type=MESH)
    yield
    if part < 2:
        for way in WAYS:
            net.arrived(sent[way], strip_of(result, part, side, way, 1 - net.c))
    traffic.settle()


def strip_of(result, part, side, way, core):
    piece = 2 * side + core
    if part == 0:
        return result.at[piece, :, columns_of(way)]
    return result.at[:, pl.ds(pl.multiple_of(WID * piece + HALF * way, HALF), HALF)]


def vector_steps(net, vectors, land):
    traffic = Traffic(net)
    sent = traffic.send(vectors, land.at[0, 0], net.sibling())
    yield
    net.arrived(sent, land.at[0, 0])
    value = vectors[...] + land[0, 0]
    for stage, axis, me in ((1, "z", net.z), (2, "y", net.y), (3, "x", net.x)):
        land[stage, me] = value
        mine = land.at[stage, me]
        sent = [traffic.send(mine, mine, net.along(axis, step)) for step in STEPS]
        yield
        for step in STEPS:
            net.arrived(sent[step - 1], land.at[stage, wrap(me - step)])
        value = ((land[stage, 0] + land[stage, 1]) + land[stage, 2]) + land[stage, 3]
    land[0, 1] = value
    traffic.settle()


ROWS = 202
PAD = 208
MOLS = 4
TOTAL = MOLS * PAD
GROUPS = 3
LANES = 256
FEAT = 128
EPS_NORM = 1e-05
EPS_ATTN = 1e-06
GELU_SCALE = 0.7978845608028654
GELU_CUBIC = 0.044715


def dot(left, right):
    return jnp.dot(left, right, preferred_element_type=jnp.float32)


def dot_nt(left, right):
    return lax.dot_general(left, right, (((1,), (1,)), ((), ())), preferred_element_type=jnp.float32)


def dot_tn(left, right):
    return lax.dot_general(left, right, (((0,), (0,)), ((), ())), preferred_element_type=jnp.float32)


def square(ref, index):
    return ref[index].reshape(WID, WID)


def iota(shape, axis):
    return lax.broadcasted_iota(jnp.int32, shape, axis)


def flag(condition):
    return jnp.where(condition, 1.0, 0.0)


def softplus(value):
    small = jnp.exp(-jnp.abs(value))
    tail = jnp.where(small < 1e-3, small * (1.0 - 0.5 * small), jnp.log(1.0 + small))
    return jnp.maximum(value, 0.0) + tail


def softplus_slope(feature):
    return jnp.where(feature < 1e-3, feature * (1.0 - 0.5 * feature), 1.0 - jnp.exp(-feature))


def centred(value):
    centre = value - jnp.mean(value, axis=-1, keepdims=True)
    scale = lax.rsqrt(jnp.mean(centre * centre, axis=-1, keepdims=True) + EPS_NORM)
    return centre * scale, scale


def column_sum(value):
    return jnp.sum(value, axis=0, keepdims=True)


GAIN1, BIAS1, B_QUERY, B_KEY, B_VALUE, B_OUT, GAIN2, BIAS2, B_DOWN, B_UP = range(10)


class Layer:
    def __init__(self, **refs):
        self.__dict__.update(refs)

    origin = 0

    def row(self, index):
        return self.params[pl.ds(index, 1)]

    def add_row(self, index, value):
        self.vectors[pl.ds(index, 1)] += value

    def block_mask(self):
        shape = (FEAT, LANES)
        return flag(iota(shape, 0) // 32 == iota(shape, 1) // 64)

    def prepare_features(self):
        proj = self.feature_ref[...]
        pick_rows = iota((LANES, 64), 0) % 64
        swap = iota((LANES, 64), 1)
        same = rounded(flag(pick_rows == swap))
        turned = rounded(flag(pick_rows + 32 == swap) - flag(pick_rows == swap + 32))
        spread = rounded(flag(iota((32, FEAT), 1) % 32 == iota((32, FEAT), 0)))
        mask = flag(iota((LANES, FEAT), 0) // 64 == iota((LANES, FEAT), 1) // 32)
        for index, pick in ((0, same), (1, turned)):
            tall = rounded(dot_nt(pick, proj))
            full = dot(tall, spread) * mask
            span = slice(index * LANES, (index + 1) * LANES)
            self.features[span] = rounded(full)
            self.features_back[:, span] = rounded(full.T)

    def prepare_tokens(self):
        zero = jnp.zeros((16, WID), jnp.bfloat16)
        for molecule in range(MOLS):
            start = molecule * PAD
            self.tokens[pl.ds(start + PAD - 16, 16)] = zero
            self.tokens[pl.ds(start, ROWS)] = self.raw[:, molecule, :]

    def prepare_cotangent(self):
        zero = jnp.zeros((16, WID), jnp.bfloat16)
        keep = iota((ROWS, WID), 0) < self.most()
        for molecule in range(MOLS):
            start = molecule * PAD
            self.grad_down[pl.ds(start + PAD - 16, 16)] = zero
            masked = jnp.where(keep, wide(self.raw[:, molecule, :]), 0.0)
            self.grad_down[pl.ds(start, ROWS)] = rounded(masked)
            self.add_row(B_DOWN, column_sum(masked))

    def prepare_params(self):
        columns = wide(self.small[...].reshape(WID, 128))
        rows = columns.T
        self.params[pl.ds(0, 16)] = rows[0:16]
        lanes = iota((8, WID), 1)
        owner = flag(lanes // 192 == iota((8, WID), 0))
        stacked = jnp.concatenate(
            [jnp.broadcast_to(rows[B_UP + k : B_UP + k + 1], (8, WID)) * owner for k in range(4)], axis=0
        )
        stacked = rounded(stacked)
        spread = jnp.zeros((32, WID), jnp.float32)
        for start in range(0, WID, 128):
            source = start + iota((128, WID), 0)
            pick = rounded(flag(96 * ((source // 24) % 8) + source % 24 == iota((128, WID), 1)))
            spread = spread + dot(stacked[:, start : start + 128], pick)
        total = spread[0:8]
        for k in range(1, 4):
            total = total + pltpu.roll(spread[8 * k : 8 * k + 8], 24 * k, 1)
        self.params[pl.ds(16, 8)] = total

    def norm_one(self):
        gain, bias = self.row(GAIN1), self.row(BIAS1)
        for molecule in range(MOLS):
            rows = pl.ds(molecule * PAD, PAD)
            normed, _ = centred(wide(self.tokens[rows]))
            self.normed_one[rows] = rounded(normed * gain + bias)

    def columns(self, piece, lanes):
        return self.weights[piece, :, :, :, lanes].reshape(WID, LANES)

    def molecules(self):
        return [slice(molecule * PAD, (molecule + 1) * PAD) for molecule in range(MOLS)]

    def attend(self, group):
        lanes = slice(group * LANES, (group + 1) * LANES)
        thin = slice(group * FEAT, (group + 1) * FEAT)
        bias = [self.params[pl.ds(row, 1), lanes] for row in (B_QUERY, B_KEY, B_VALUE)]
        cosines, sines = [jnp.concatenate([table[...]] * 2, axis=1) for table in (self.cosines, self.sines)]
        mask = self.block_mask()
        mask = jnp.concatenate([mask, mask], axis=1)
        ones = jnp.ones((PAD, LANES), jnp.bfloat16)
        weights = square(self.weights, group)
        every = list(enumerate(self.molecules()))
        whole = [dot(self.normed_one[rows], weights) for _, rows in every]
        turned = []
        for index, _ in every:
            for kind in (0, 1):
                value = whole[index][:, kind * LANES : (kind + 1) * LANES] + bias[kind]
                turned.append(jnp.concatenate([rounded(value * cosines), rounded(value * sines)], axis=1))
        lows, levels = [], []
        for index, _ in every:
            value = whole[index][:, 2 * LANES :] + bias[2]
            length = self.lengths[index]
            valid = jnp.where(iota((PAD, LANES), 0) < length, value, 0.0)
            level = column_sum(valid) / wide(jnp.maximum(length, 1))
            levels.append(level)
            lows.append(rounded(value - level))
        feats = [softplus(dot(one, self.features[...])) for one in turned]
        queries = [rounded(feats[2 * index]) for index, _ in every]
        keys = [
            rounded(jnp.where(iota((PAD, FEAT), 0) < self.lengths[index], feats[2 * index + 1], 0.0))
            for index, _ in every
        ]
        states = [
            rounded(dot_tn(keys[index], jnp.concatenate([lows[index], ones], axis=1)) * mask) for index, _ in every
        ]
        both = [dot(queries[index], states[index]) for index, _ in every]
        for index, rows in every:
            level = levels[index]
            mixed = level + (both[index][:, :LANES] - EPS_ATTN * level) / (both[index][:, LANES:] + EPS_ATTN)
            self.mixed[rows, lanes] = rounded(mixed)
            self.feat_query[rows, thin] = queries[index]
            self.feat_key[rows, thin] = keys[index]
            self.values[rows, lanes] = lows[index]
            self.levels[pl.ds(8 * index, 1), lanes] = level

    def middle_rows(self):
        for molecule in range(MOLS):
            rows = slice(molecule * PAD, (molecule + 1) * PAD)
            middle = wide(self.tokens[rows]) + self.row(B_OUT) + dot(self.mixed[rows], square(self.weights, 3))
            self.middle[rows] = middle
            normed, _ = centred(middle)
            self.normed_two[rows] = rounded(normed * self.row(GAIN2) + self.row(BIAS2))

    def up_rows(self, quarter):
        for group in range(GROUPS):
            lanes = slice(group * LANES, (group + 1) * LANES)
            pre = dot(self.normed_two[...], self.columns(4 + quarter, lanes))
            pre = pre + self.params[pl.ds(16 + quarter, 1), lanes]
            squared = pre * pre
            gate = 0.5 + 0.5 * jnp.tanh(pre * (GELU_SCALE + GELU_SCALE * GELU_CUBIC * squared))
            hidden = pre * gate
            slope = gate + (hidden - hidden * gate) * (
                2.0 * GELU_SCALE + 6.0 * GELU_SCALE * GELU_CUBIC * squared
            )
            self.hidden[self.origin + quarter, :, lanes] = rounded(hidden)
            self.slope[self.origin + quarter, :, lanes] = rounded(slope)

    def blocks(self, value):
        return rounded(value).reshape(4, 4, BLK, WID)

    def store_term(self, slot, value):
        self.grads[slot] = self.blocks(value)

    def term_down(self, quarter):
        self.store_term(quarter, dot_tn(self.hidden[self.origin + quarter], self.grad_down[...]))

    def grad_pre_rows(self, quarter):
        for group in range(GROUPS):
            lanes = slice(group * LANES, (group + 1) * LANES)
            grad_hidden = dot_nt(self.grad_down[...], self.weights[8 + quarter].reshape(WID, WID)[lanes])
            grad_pre = rounded(grad_hidden * wide(self.slope[self.origin + quarter, :, lanes]))
            self.slope[self.origin + quarter, :, lanes] = grad_pre
            self.vectors[pl.ds(B_UP + quarter, 1), lanes] += column_sum(wide(grad_pre))

    def term_up(self, quarter):
        self.store_term(4 + quarter, dot_tn(self.normed_two[...], self.slope[self.origin + quarter]))

    def norm_back(self, grad, inputs, gain, bias):
        normed, scale = centred(inputs)
        self.add_row(gain, column_sum(grad * normed))
        self.add_row(bias, column_sum(grad))
        scaled = grad * self.row(gain)
        first = jnp.mean(scaled, axis=-1, keepdims=True)
        second = jnp.mean(scaled * normed, axis=-1, keepdims=True)
        return scale * (scaled - first - normed * second)

    def grad_two_columns(self, group):
        lanes = slice(group * LANES, (group + 1) * LANES)
        whole = dot_nt(self.slope[self.origin + 0], self.weights[4].reshape(WID, WID)[lanes])
        for quarter in range(1, 4):
            whole += dot_nt(self.slope[self.origin + quarter], self.weights[4 + quarter].reshape(WID, WID)[lanes])
        self.grad_middle[:, lanes] = whole

    def grad_middle_rows(self):
        for molecule in range(MOLS):
            rows = slice(molecule * PAD, (molecule + 1) * PAD)
            back = self.norm_back(self.grad_middle[rows], self.middle[rows], GAIN2, BIAS2)
            grad = wide(self.grad_down[rows]) + back
            self.grad_middle[rows] = grad
            low = rounded(grad)
            self.slope[self.origin + 3, rows] = low
            self.add_row(B_OUT, column_sum(wide(low)))

    def term_out(self):
        self.weights[7] = self.blocks(dot_tn(self.mixed[...], self.slope[self.origin + 3]))

    def attend_back(self, group):
        mask = self.block_mask()
        mask = jnp.concatenate([mask, mask], axis=1)
        ones = jnp.ones((PAD, LANES), jnp.bfloat16)
        cosines, sines = [jnp.concatenate([table[...]] * 2, axis=1) for table in (self.cosines, self.sines)]
        thin = slice(group * FEAT, (group + 1) * FEAT)
        lanes = slice(group * LANES, (group + 1) * LANES)
        every = list(enumerate(self.molecules()))
        queries = [self.feat_query[rows, thin] for _, rows in every]
        keys = [self.feat_key[rows, thin] for _, rows in every]
        values = [jnp.concatenate([self.values[rows, lanes], ones], axis=1) for _, rows in every]
        grad_mixed = dot_nt(self.slope[self.origin + 3], self.weights[3].reshape(WID, WID)[lanes])
        states = [rounded(dot_tn(keys[index], values[index]) * mask) for index, _ in every]
        both = [dot(queries[index], states[index]) for index, _ in every]
        grads = []
        for index, rows in every:
            inverse = 1.0 / (both[index][:, LANES:] + EPS_ATTN)
            grad_num = grad_mixed[rows] * inverse
            offset = EPS_ATTN * self.levels[pl.ds(8 * index, 1), lanes]
            grad_den = -grad_num * ((both[index][:, :LANES] - offset) * inverse)
            grads.append(jnp.concatenate([rounded(grad_num), rounded(grad_den)], axis=1))
        grad_states = [rounded(dot_tn(queries[index], grads[index]) * mask) for index, _ in every]
        grad_queries = [dot_nt(grads[index], states[index]) for index, _ in every]
        grad_keys = [dot_nt(values[index], grad_states[index]) for index, _ in every]
        grad_values = [rounded(dot(keys[index], grad_states[index][:, :LANES])) for index, _ in every]
        for index, rows in every:
            self.slope[self.origin + group, rows, 2 * LANES : 3 * LANES] = grad_values[index]
        self.vectors[pl.ds(B_VALUE, 1), lanes] += sum(column_sum(wide(value)) for value in grad_values)
        for slot, row, feats, grads in ((0, B_QUERY, queries, grad_queries), (1, B_KEY, keys, grad_keys)):
            turned = [
                dot(rounded(grads[index] * softplus_slope(wide(feats[index]))), self.features_back[...])
                for index, _ in every
            ]
            lows = [rounded(cosines * one[:, :LANES] + sines * one[:, LANES:]) for one in turned]
            for index, rows in every:
                self.slope[self.origin + group, rows, slot * LANES : (slot + 1) * LANES] = lows[index]
            self.vectors[pl.ds(row, 1), lanes] += sum(column_sum(wide(low)) for low in lows)

    def term_square(self, group):
        self.weights[4 + (2, 0, 1)[group]] = self.blocks(dot_tn(self.normed_one[...], self.slope[self.origin + group]))

    def grad_token_rows(self, first):
        pair = pl.ds(first * PAD, 2 * PAD)
        whole = dot_nt(self.slope[self.origin + 0, pair], square(self.weights, 0))
        for index in (1, 2):
            whole += dot_nt(self.slope[self.origin + index, pair], square(self.weights, index))
        for molecule in (first, first + 1):
            rows = slice(molecule * PAD, (molecule + 1) * PAD)
            own = whole[(molecule - first) * PAD : (molecule - first + 1) * PAD]
            grad = self.grad_middle[rows] + self.norm_back(own, wide(self.tokens[rows]), GAIN1, BIAS1)
            self.raw[:, molecule, :] = rounded(grad[:ROWS])

    def most(self):
        lengths = self.lengths
        return jnp.maximum(jnp.maximum(lengths[0], lengths[1]), jnp.maximum(lengths[2], lengths[3]))

    def layer_out_rows(self, molecule):
        rows = pl.ds(molecule * PAD, PAD)
        result = self.middle[rows] + self.row(B_DOWN)
        for quarter in range(4):
            result += dot(self.hidden[self.origin + quarter, rows], square(self.weights, 8 + quarter))
        keep = iota((ROWS, WID), 0) < self.most()
        self.raw[:, molecule, :] = rounded(jnp.where(keep, result[:ROWS], 0.0))


LAYER_SCRATCH = dict(
    raw=((ROWS, MOLS, WID), jnp.bfloat16),
    tokens=((TOTAL, WID), jnp.bfloat16),
    grad_down=((TOTAL, WID), jnp.bfloat16),
    normed_one=((TOTAL, WID), jnp.bfloat16),
    values=((TOTAL, WID), jnp.bfloat16),
    mixed=((TOTAL, WID), jnp.bfloat16),
    normed_two=((TOTAL, WID), jnp.bfloat16),
    feat_query=((TOTAL, HALF), jnp.bfloat16),
    feat_key=((TOTAL, HALF), jnp.bfloat16),
    levels=((8 * MOLS, WID), jnp.float32),
    middle=((TOTAL, WID), jnp.float32),
    grad_middle=((TOTAL, WID), jnp.float32),
    hidden=((4, TOTAL, WID), jnp.bfloat16),
    slope=((4, TOTAL, WID), jnp.bfloat16),
    features=((2 * LANES, FEAT), jnp.bfloat16),
    features_back=((FEAT, 2 * LANES), jnp.bfloat16),
    params=((24, WID), jnp.float32),
    vectors=((16, WID), jnp.float32),
    grads=((8, 4, 4, BLK, WID), jnp.bfloat16),
    weights=((12, 4, 4, BLK, WID), jnp.bfloat16),
    small=((4, 4, BLK, 128), jnp.bfloat16),
)


VMEM = pl.BlockSpec(memory_space=pltpu.VMEM)
SMEM = pl.BlockSpec(memory_space=pltpu.SMEM)
ANY = pl.BlockSpec(memory_space=pl.ANY)
SEMS = 320


COMM_SCRATCH = dict(
    pair=((2, 4, 4, BLK, HALF), jnp.bfloat16),
    big=((3, 2, 3, 4, BLK, HALF), jnp.bfloat16),
    little=((3, 2, 3, BLK, HALF), jnp.bfloat16),
    cross=((3, 2, 4, BLK, HALF), jnp.bfloat16),
    total=((4, 2, BLK, HALF), jnp.float32),
    square_sum=((4, 24, WID), jnp.float32),
    up_sum=((24, 4 * WID), jnp.float32),
    down_sum=((2 * BLK, WID), jnp.float32),
    vector_land=((4, 4, 16, WID), jnp.float32),
    narrow=((16, 128), jnp.float32),
    small_mine=((BLK, 128), jnp.float32),
)
def layer_kernel(
    lengths, queries, keys, values, outs, ups, downs, feature_ref, cosines, sines, *rest,
):
    vectors_in, rest = rest[:10], rest[10:]
    tokens_in, cot_in, layer_out, tokens_out, square_out, up_out, down_out, narrow_out = rest[:8]
    scratch = rest[8:]
    names = list(LAYER_SCRATCH) + list(COMM_SCRATCH)
    refs = dict(zip(names, scratch))
    send_sems, recv_sems, local_sems, pair_gates, land_gates = scratch[len(names):]
    net = Net(send_sems, recv_sems)
    work = Layer(
        lengths=lengths, feature_ref=feature_ref, cosines=cosines, sines=sines,
        **{name: refs[name] for name in LAYER_SCRATCH},
    )
    work.origin = net.x // RING
    load_tokens = pltpu.make_async_copy(tokens_in, work.raw, local_sems.at[0])
    load_cot = pltpu.make_async_copy(cot_in, work.raw, local_sems.at[1])
    load_tokens.start()
    net.greet()

    shards = (queries, keys, values, outs, ups, downs, vectors_in)
    load = load_shards(
        net, work.weights, work.small, work.grad_middle, refs["small_mine"], refs["narrow"], shards
    )
    small = gather_small(net, work.small)
    get = [gather_steps(net, work.weights, part, side) for part in (0, 1, 2) for side in (0, 1)]

    def go(*steps):
        for step in steps:
            next(step, None)

    def reduce(order, part, side, result):
        lands = [
            (
                refs["big"].at[order % 3, way],
                refs["little"].at[order % 3, way],
                refs["cross"].at[order % 3, way],
            )
            for way in WAYS
        ]
        gates = (
            pair_gates.at[order - 1] if order >= 1 else None,
            pair_gates.at[order] if order < 5 else None,
            land_gates.at[order - 3] if order >= 3 else None,
            land_gates.at[order] if order < 3 else None,
        )
        return reduce_steps(
            net, work.weights if part == 0 else work.grads, 4 * (part < 2), part, side, refs["pair"], lands, gates,
            refs["total"].at[order - 2] if order >= 2 else None, refs[result],
        )

    down = [reduce(0, 2, 0, "down_sum"), reduce(1, 2, 1, "down_sum")]
    up = [reduce(2, 1, 0, "up_sum"), reduce(3, 1, 1, "up_sum")]
    value, query = reduce(4, 0, 1, "square_sum"), reduce(5, 0, 0, "square_sum")
    vectors = vector_steps(net, work.vectors, refs["vector_land"])

    work.vectors[...] = jnp.zeros_like(work.vectors)
    write_tokens = pltpu.make_async_copy(work.raw, tokens_out, local_sems.at[0])
    write_layer = pltpu.make_async_copy(work.raw, layer_out, local_sems.at[1])
    go(load)
    load_tokens.wait()
    work.prepare_tokens()
    load_cot.start()
    go(load, get[0], load, small, get[5], load, get[1], load, get[2], get[3], small, get[0], get[1], get[3], small, get[2], get[4])
    work.prepare_params()
    go(get[0])
    work.norm_one()
    work.prepare_features()
    go(get[0])
    load_cot.wait()
    work.prepare_cotangent()
    work.attend(0)
    go(get[1])
    work.attend(1)
    go(get[1])
    work.attend(2)
    go(get[3], get[5])
    work.middle_rows()
    go(get[3])
    work.up_rows(3)
    work.term_down(3)
    go(get[2])
    work.up_rows(2)
    work.term_down(2)
    go(get[4], get[2])
    work.up_rows(0)
    work.term_down(0)
    work.up_rows(1)
    work.term_down(1)
    go(down[0], get[5], down[0], get[4], down[1], get[5], get[4])
    work.grad_pre_rows(0)
    work.term_up(0)
    go(down[1])
    work.grad_pre_rows(1)
    work.term_up(1)
    go(up[0])
    work.grad_pre_rows(3)
    go(down[0])
    work.grad_pre_rows(2)
    work.grad_two_columns(2)
    go(up[0])
    work.grad_two_columns(1)
    work.term_up(3)
    go(down[0])
    work.term_up(2)
    go(up[1], down[1])
    work.grad_two_columns(0)
    work.grad_middle_rows()
    work.attend_back(2)
    go(down[0], up[0], down[1])
    work.attend_back(0)
    go(up[1])
    work.term_out()
    work.term_square(0)
    go(value, down[1], up[0])
    work.attend_back(1)
    go(value)
    work.term_square(1)
    work.term_square(2)
    go(query, up[0], up[1], query)
    work.grad_token_rows(0)
    work.grad_token_rows(2)
    write_tokens.start()
    go(vectors, value, vectors, up[0], up[1], query, value, vectors)
    write_tokens.wait()
    work.layer_out_rows(0)
    go(query, down[0])
    work.layer_out_rows(1)
    go(vectors)
    work.layer_out_rows(2)
    work.layer_out_rows(3)
    write_layer.start()
    go(value, up[1], query, vectors, value, up[1], down[1], query)
    total = refs["vector_land"][0, 1]
    place = net.y * 8 + net.z * 2 + net.c
    narrow = refs["narrow"]
    turned = pltpu.roll(total, WID - 24 * place, 1)
    narrow[...] = turned[:, :128]
    chosen = refs["vector_land"][0, 1, pl.ds(B_UP + place // 8, 1)]
    narrow[pl.ds(B_UP, 1)] = pltpu.roll(chosen, WID - 96 * (place % 8), 1)[:, :128]
    writes = [
        pltpu.make_async_copy(refs[name], ref, local_sems.at[2 + slot])
        for slot, (name, ref) in enumerate(
            (("square_sum", square_out), ("up_sum", up_out), ("down_sum", down_out), ("narrow", narrow_out))
        )
    ]
    for write in writes:
        write.start()
    for write in [write_layer] + writes:
        write.wait()


def layer_call(*operands):
    bf, ff = jnp.bfloat16, jnp.float32
    scratch = list(LAYER_SCRATCH.values()) + list(COMM_SCRATCH.values())
    return pl.pallas_call(
        layer_kernel,
        out_shape=(
            jax.ShapeDtypeStruct((ROWS, MOLS, WID), bf),
            jax.ShapeDtypeStruct((ROWS, MOLS, WID), bf),
            jax.ShapeDtypeStruct((4, 24, WID), ff),
            jax.ShapeDtypeStruct((24, 4 * WID), ff),
            jax.ShapeDtypeStruct((2 * BLK, WID), ff),
            jax.ShapeDtypeStruct((16, 128), ff),
        ),
        in_specs=[SMEM] + [VMEM] * 19 + [ANY] * 2,
        out_specs=(ANY,) * 6,
        scratch_shapes=[pltpu.VMEM(shape, dtype) for shape, dtype in scratch]
        + [
            pltpu.SemaphoreType.DMA((SEMS,)),
            pltpu.SemaphoreType.DMA((SEMS,)),
            pltpu.SemaphoreType.DMA((6,)),
            pltpu.SemaphoreType.REGULAR((5,)),
            pltpu.SemaphoreType.REGULAR((3,)),
        ],
        compiler_params=pltpu.CompilerParams(
            collective_id=0, has_side_effects=True, vmem_limit_bytes=64 * 2**20 - 2**17
        ),
    )(*operands)


def finish_kernel(layer, tokens, square, up, down, narrow, *rest):
    outs, held, (sems_in, sems_out) = rest[:18], rest[18:23], rest[23:]
    fetch = [
        pltpu.make_async_copy(src, dst, sems_in.at[slot])
        for slot, (src, dst) in enumerate(zip((square, layer, tokens, up, down), held))
    ]
    for copy in fetch:
        copy.start()
    for index, slot in enumerate((2, 3, 5, 7, 9, 11, 12, 13, 17)):
        outs[slot][...] = narrow[index, 0:24]
    outs[15][...] = narrow[9, 0:96]
    fetch[0].wait()
    for group, index in ((0, 2), (1, 0), (2, 1)):
        for kind, slot in enumerate((4, 6, 8)):
            outs[slot][:, group * LANES : (group + 1) * LANES] = held[0][index, :, kind * LANES : (kind + 1) * LANES]
    outs[10][...] = held[0][3]
    stores = []
    for index, slot in ((1, 0), (2, 1), (3, 14), (4, 16)):
        fetch[index].wait()
        stores.append(pltpu.make_async_copy(held[index], outs[slot], sems_out.at[index]))
        stores[-1].start()
    for copy in stores:
        copy.wait()


def finish_call(*sums):
    bf, ff = jnp.bfloat16, jnp.float32
    tokens, thin, wide_one = ((ROWS, MOLS, WID), bf), ((24,), ff), ((24, WID), ff)
    up, down = ((24, 4 * WID), ff), ((96, WID), ff)
    shapes = [tokens, tokens, thin, thin] + [wide_one, thin] * 4 + [thin, thin, up, thin, down, thin]
    shapes[15] = ((96,), ff)
    direct = (0, 1, 14, 16)
    return pl.pallas_call(
        finish_kernel,
        out_shape=[jax.ShapeDtypeStruct(shape, dtype) for shape, dtype in shapes],
        in_specs=[ANY] * 5 + [VMEM],
        out_specs=[ANY if slot in direct else VMEM for slot in range(18)],
        scratch_shapes=[pltpu.VMEM((4, 24, WID), ff)]
        + [pltpu.VMEM(shapes[slot][0], shapes[slot][1]) for slot in direct]
        + [pltpu.SemaphoreType.DMA((5,)), pltpu.SemaphoreType.DMA((5,))],
    )(*sums)


def angle_tables():
    positions = np.arange(PAD)[:, None]
    angles = positions * 10000.0 ** (-2.0 * (np.arange(128)[None, :] % 32) / 64)
    return np.cos(angles).astype(np.float32), np.sin(angles).astype(np.float32)


def body(
    tokens, lengths, feature_proj, ln1_gain, ln1_bias, w_query, b_query, w_key, b_key, w_value, b_value,
    w_out, b_out, ln2_gain, ln2_bias, w_up, b_up, w_down, b_down, cotangent,
):
    cosines, sines = angle_tables()
    sums = layer_call(
        lengths, w_query, w_key, w_value, w_out, w_up, w_down, feature_proj.T, jnp.asarray(cosines), jnp.asarray(sines),
        ln1_gain, ln1_bias, b_query, b_key, b_value, b_out, ln2_gain, ln2_bias, b_down, b_up,
        tokens.transpose(1, 0, 2), cotangent.transpose(1, 0, 2),
    )
    done = finish_call(*sums)
    return (done[0].transpose(1, 0, 2), done[1].transpose(1, 0, 2)) + tuple(done[2:])


def solution(mesh):
    rows, flat = P("fsdp", None), P("fsdp")
    mols = P(("fsdp", "dp"), None, None)
    pairs = (flat, flat, rows, flat, rows, flat, rows, flat, rows, flat, flat, flat, rows, flat, rows, flat)
    return jax.shard_map(
        body,
        mesh=mesh,
        in_specs=(mols, P(("fsdp", "dp")), P()) + pairs + (mols,),
        out_specs=(mols, mols) + pairs,
        check_vma=False,
    )
```

```python
import jax
import jax.numpy as jnp
import numpy as np
from jax import lax
from jax.experimental import pallas as pl
from jax.experimental.pallas import tpu as pltpu
from jax.sharding import PartitionSpec as P


MESH = pl.DeviceIdType.MESH
RING = 4
BLK = 48
WID = 768
HALF = 384
ALL = pl.ds(0, RING)
STEPS = (1, 2, 3)
WAYS = (0, 1)


def rounded(value):
    return value.astype(jnp.bfloat16)


def wide(value):
    return value.astype(jnp.float32)


class Net:
    def __init__(self, send_sems, recv_sems):
        self.send_sems, self.recv_sems, self.count = send_sems, recv_sems, 0
        index = lax.axis_index("fsdp")
        self.x = lax.axis_index("dp")
        self.y = index // (2 * RING)
        self.z = (index // 2) % RING
        self.c = index % 2

    def at(self, y, z, c):
        return {"fsdp": ((y + RING) % RING) * (2 * RING) + ((z + RING) % RING) * 2 + c}

    def sibling(self):
        return self.at(self.y, self.z, 1 - self.c)

    def along(self, axis, step):
        if axis == "y":
            return self.at(self.y + step, self.z, self.c)
        if axis == "z":
            return self.at(self.y, self.z + step, self.c)
        return {"dp": (self.x + step) % RING}

    def peers(self):
        return [self.along(axis, step) for axis in ("x", "y", "z") for step in STEPS]

    def greet(self):
        barrier = pltpu.get_barrier_semaphore()
        peers = [self.sibling()] + self.peers()
        for peer in peers:
            pl.semaphore_signal(barrier, inc=1, device_id=peer, device_id_type=MESH)
        pl.semaphore_wait(barrier, len(peers))

    def send(self, src, dst, device):
        slot = self.count
        self.count += 1
        copy = pltpu.make_async_remote_copy(
            src_ref=src,
            dst_ref=dst,
            send_sem=self.send_sems.at[slot],
            recv_sem=self.recv_sems.at[slot],
            device_id=device,
            device_id_type=MESH,
        )
        copy.start()
        return slot

    def arrived(self, slot, land):
        pltpu.make_async_remote_copy(
            src_ref=land,
            dst_ref=land,
            send_sem=self.send_sems.at[slot],
            recv_sem=self.recv_sems.at[slot],
            device_id=self.sibling(),
            device_id_type=MESH,
        ).wait_recv()

    def left(self, slot, source):
        pltpu.make_async_remote_copy(
            src_ref=source,
            dst_ref=source,
            send_sem=self.send_sems.at[slot],
            recv_sem=self.recv_sems.at[slot],
            device_id=self.sibling(),
            device_id_type=MESH,
        ).wait_send()

    def axes(self, way):
        return ("y", "z") if way == 0 else ("z", "y")

    def place(self, way):
        return (self.y, self.z) if way == 0 else (self.z, self.y)


def wrap(index):
    return (index + RING) % RING


def columns_of(side):
    return pl.ds(HALF * side, HALF)


def slot_of(ref, base, part, side, way, core, y, z):
    if part < 2:
        return ref.at[base + 2 * side + core, y, z, :, columns_of(way)]
    y = pl.ds(base, RING) if isinstance(y, pl.Slice) else base + y
    return ref.at[y, z, 2 * core + way, :, columns_of(side)]


class Traffic:
    def __init__(self, net):
        self.net, self.sent = net, []

    def send(self, src, dst, device):
        slot = self.net.send(src, dst, device)
        self.sent.append((slot, src))
        return slot

    def settle(self):
        for slot, src in self.sent:
            self.net.left(slot, src)
        self.sent = []


Y_FIRST, Z_FIRST = 0, 1


def gather_lane(net, traffic, order, slot):
    mine, theirs = net.c, 1 - net.c
    def at(core, first, second):
        return slot(core, first, second) if order == Y_FIRST else slot(core, second, first)

    p, q = net.place(order)
    first, second = net.axes(order)
    own = at(mine, p, q)
    sent = {step: traffic.send(own, own, net.along(first, step)) for step in STEPS}
    yield
    for step in STEPS:
        net.arrived(sent[step], at(mine, wrap(p - step), q))
    row = at(mine, ALL, q)
    sent = {step: traffic.send(row, row, net.along(second, step)) for step in STEPS}
    pairs = {0: traffic.send(row, row, net.sibling())}
    yield
    for step in (1, 3, 2):
        far = at(mine, ALL, wrap(q - step))
        net.arrived(sent[step], far)
        pairs[step] = traffic.send(far, far, net.sibling())
    yield
    for step in (0,) + STEPS:
        net.arrived(pairs[step], at(theirs, ALL, wrap(q - step)))


def gather_steps(net, weights, part, side):
    traffic = Traffic(net)

    def lane(way):
        def slot(core, y, z):
            return slot_of(weights, 4 * part, part, side, way, core, y, z)

        return gather_lane(net, traffic, way, slot)

    yield from together(*[lane(way) for way in WAYS])
    traffic.settle()


def gather_small(net, small):
    traffic = Traffic(net)
    own = small.at[net.y, net.z]
    sent = [traffic.send(own, own, net.along("y", step)) for step in STEPS]
    yield
    for slot, step in zip(sent, STEPS):
        net.arrived(slot, small.at[wrap(net.y - step), net.z])
    row = small.at[ALL, net.z]
    sent = [traffic.send(row, row, net.along("z", step)) for step in STEPS]
    yield
    for slot, step in zip(sent, STEPS):
        net.arrived(slot, small.at[ALL, wrap(net.z - step)])
    traffic.settle()


def load_shards(net, weights, small, stage, small_mine, thin, shards):
    queries, keys, values, outs, ups, downs, vectors = shards
    first = net.c == 0
    traffic, sent = Traffic(net), []

    def rows(slot, core):
        return pl.ds(pl.multiple_of(BLK * slot + 24 * core, 8), 24)

    def lane(piece):
        return pl.ds(pl.multiple_of(WID * piece, WID), WID)

    def exchange(mine, theirs):
        slot = len(sent)
        outgoing = pl.ds(4 * BLK + 24 * slot, 24)
        stage[rows(slot, net.c)] = mine
        stage[outgoing] = theirs
        sent.append(traffic.send(stage.at[outgoing], stage.at[rows(slot, net.c)], net.sibling()))

    def heads(group):
        lanes = slice(256 * group, 256 * group + 256)
        return jnp.concatenate([wide(ref[:, lanes]) for ref in (queries, keys, values)], axis=1)

    def either(early, late):
        exchange(jnp.where(first, early, late), jnp.where(first, late, early))

    def place(slot):
        net.arrived(sent[slot], stage.at[rows(slot, 1 - net.c)])
        piece = 4 * (slot // 2) + 2 * (slot % 2) + net.c
        weights[piece, net.y, net.z] = rounded(stage[pl.ds(BLK * slot, BLK)])

    either(heads(0), heads(1))
    thin[...] = jnp.zeros_like(thin)
    for index in range(9):
        thin[index, 0:24] = wide(vectors[index][...])
    thin[9, 0:96] = wide(vectors[9][...])
    for index in range(1, 4):
        thin[pl.ds(9 + index, 1)] = pltpu.roll(thin[pl.ds(9, 1)], 128 - 24 * index, 1)
    pick = rounded(flag(iota((16, 128), 0) == iota((16, 128), 1)))
    small_mine[rows(0, net.c)] = dot_tn(rounded(thin[...]), pick)[0:24]
    sent_small = traffic.send(small_mine.at[rows(0, net.c)], small_mine.at[rows(0, net.c)], net.sibling())
    yield
    place(0)
    net.arrived(sent_small, small_mine.at[rows(0, 1 - net.c)])
    small[net.y, net.z] = rounded(small_mine[...])
    yield
    either(heads(2), wide(outs[...]))
    for side in (0, 1):
        exchange(wide(ups[:, lane(2 * side + net.c)]), wide(ups[:, lane(2 * side + 1 - net.c)]))
    for way in WAYS:
        weights[8 + net.y, net.z, 2 * net.c + way] = downs[pl.ds(BLK * way, BLK)]
    yield
    place(1)
    yield
    place(2)
    place(3)
    traffic.settle()


def add_all(target, *sources):
    if len(target.shape) > 2:
        for index in range(target.shape[0]):
            add_all(target.at[index], *[source.at[index] for source in sources])
        return
    total = wide(target[...])
    for source in sources:
        total = total + wide(source[...])
    target[...] = rounded(total)


def together(*steps):
    steps = list(steps)
    while steps:
        steps = [step for step in steps if next(step, steps) is not steps]
        if steps:
            yield


def reduce_lane(net, traffic, order, slot, pair, land, total):
    big, little, cross = land

    def group(at):
        return slot(ALL, at) if order != Z_FIRST else slot(at, ALL)

    def pair_group(at):
        return pair.at[ALL, at] if order != Z_FIRST else pair.at[at]

    axis = net.axes(order)[1]
    me = net.place(order)[1]
    sent = {}
    for step in (2, 1, 3, 0):
        at = wrap(me + step)
        add_all(group(at), pair_group(at))
        if step:
            sent[step] = traffic.send(group(at), big.at[step - 1], net.along(axis, step))
    yield
    for step in STEPS:
        net.arrived(sent[step], big.at[step - 1])
    p, q = net.place(order)
    first = net.axes(order)[0]

    def block(at):
        return slot(at, q) if order == Y_FIRST else slot(q, at)

    for step in (2, 1, 3, 0):
        at = wrap(p + step)
        add_all(block(at), *[big.at[index, at] for index in range(3)])
        if step:
            sent[step] = traffic.send(block(at), little.at[step - 1], net.along(first, step))
    yield
    for step in STEPS:
        net.arrived(sent[step], little.at[step - 1])
    add_all(block(p), *[little.at[index] for index in range(3)])
    mine = cross.at[net.x]
    mine[...] = block(p)[...]
    sent = {step: traffic.send(mine, mine, net.along("x", step)) for step in STEPS}
    yield
    for step in STEPS:
        net.arrived(sent[step], cross.at[wrap(net.x - step)])
    total[...] = (wide(cross[0]) + wide(cross[1])) + (wide(cross[2]) + wide(cross[3]))


def reduce_steps(net, grads, base, part, side, pair, lands, gates, total, result):
    pair_ready, pair_done, land_ready, land_done = gates
    traffic, sent = Traffic(net), {}

    def whole(way, core):
        if part < 2:
            return grads.at[base + 2 * side + core, ALL, ALL, :, columns_of(way)]
        return grads.at[pl.ds(base, RING), ALL, 2 * core + way, :, columns_of(side)]

    def lane(way):
        def slot(y, z):
            return slot_of(grads, base, part, side, way, net.c, y, z)

        return reduce_lane(net, traffic, way, slot, pair.at[way], lands[way], sum_of(way))

    def sum_of(way):
        if part == 2:
            return result.at[pl.ds(BLK * way, BLK), columns_of(side)]
        return total.at[way]

    if pair_ready is not None:
        pl.semaphore_wait(pair_ready, 1)
    for way in WAYS:
        sent[way] = traffic.send(whole(way, 1 - net.c), pair.at[way], net.sibling())
    yield
    for way in WAYS:
        net.arrived(sent[way], pair.at[way])
    if land_ready is not None:
        pl.semaphore_wait(land_ready, len(net.peers()))
    lanes = together(*[lane(way) for way in WAYS])
    next(lanes)
    if pair_done is not None:
        pl.semaphore_signal(pair_done, inc=1, device_id=net.sibling(), device_id_type=MESH)
    yield
    yield from lanes
    traffic.settle()
    for way in WAYS:
        if part == 2:
            continue
        mine = strip_of(result, part, side, way, net.c)
        mine[...] = total[way, pl.ds(pl.multiple_of(24 * net.c, 8), 24)]
        theirs = total.at[way, pl.ds(pl.multiple_of(24 - 24 * net.c, 8), 24)]
        sent[way] = traffic.send(theirs, mine, net.sibling())
    if land_done is not None:
        for device in net.peers():
            pl.semaphore_signal(land_done, inc=1, device_id=device, device_id_type=MESH)
    yield
    if part < 2:
        for way in WAYS:
            net.arrived(sent[way], strip_of(result, part, side, way, 1 - net.c))
    traffic.settle()


def strip_of(result, part, side, way, core):
    piece = 2 * side + core
    if part == 0:
        return result.at[piece, :, columns_of(way)]
    return result.at[:, pl.ds(pl.multiple_of(WID * piece + HALF * way, HALF), HALF)]


def vector_steps(net, vectors, land):
    traffic = Traffic(net)
    sent = traffic.send(vectors, land.at[0, 0], net.sibling())
    yield
    net.arrived(sent, land.at[0, 0])
    value = vectors[...] + land[0, 0]
    for stage, axis, me in ((1, "z", net.z), (2, "y", net.y), (3, "x", net.x)):
        land[stage, me] = value
        mine = land.at[stage, me]
        sent = [traffic.send(mine, mine, net.along(axis, step)) for step in STEPS]
        yield
        for step in STEPS:
            net.arrived(sent[step - 1], land.at[stage, wrap(me - step)])
        value = ((land[stage, 0] + land[stage, 1]) + land[stage, 2]) + land[stage, 3]
    land[0, 1] = value
    traffic.settle()


ROWS = 202
PAD = 208
MOLS = 4
TOTAL = MOLS * PAD
GROUPS = 3
LANES = 256
FEAT = 128
EPS_NORM = 1e-05
EPS_ATTN = 1e-06
GELU_SCALE = 0.7978845608028654
GELU_CUBIC = 0.044715


def dot(left, right):
    return jnp.dot(left, right, preferred_element_type=jnp.float32)


def dot_nt(left, right):
    return lax.dot_general(left, right, (((1,), (1,)), ((), ())), preferred_element_type=jnp.float32)


def dot_tn(left, right):
    return lax.dot_general(left, right, (((0,), (0,)), ((), ())), preferred_element_type=jnp.float32)


def square(ref, index):
    return ref[index].reshape(WID, WID)


def iota(shape, axis):
    return lax.broadcasted_iota(jnp.int32, shape, axis)


def flag(condition):
    return jnp.where(condition, 1.0, 0.0)


def softplus(value):
    small = jnp.exp(-jnp.abs(value))
    tail = jnp.where(small < 1e-3, small * (1.0 - 0.5 * small), jnp.log(1.0 + small))
    return jnp.maximum(value, 0.0) + tail


def softplus_slope(feature):
    return jnp.where(feature < 1e-3, feature * (1.0 - 0.5 * feature), 1.0 - jnp.exp(-feature))


def centred(value):
    centre = value - jnp.mean(value, axis=-1, keepdims=True)
    scale = lax.rsqrt(jnp.mean(centre * centre, axis=-1, keepdims=True) + EPS_NORM)
    return centre * scale, scale


def column_sum(value):
    return jnp.sum(value, axis=0, keepdims=True)


GAIN1, BIAS1, B_QUERY, B_KEY, B_VALUE, B_OUT, GAIN2, BIAS2, B_DOWN, B_UP = range(10)


class Layer:
    def __init__(self, **refs):
        self.__dict__.update(refs)

    origin = 0

    def row(self, index):
        return self.params[pl.ds(index, 1)]

    def add_row(self, index, value):
        self.vectors[pl.ds(index, 1)] += value

    def block_mask(self):
        shape = (FEAT, LANES)
        return flag(iota(shape, 0) // 32 == iota(shape, 1) // 64)

    def prepare_features(self):
        proj = self.feature_ref[...]
        pick_rows = iota((LANES, 64), 0) % 64
        swap = iota((LANES, 64), 1)
        same = rounded(flag(pick_rows == swap))
        turned = rounded(flag(pick_rows + 32 == swap) - flag(pick_rows == swap + 32))
        spread = rounded(flag(iota((32, FEAT), 1) % 32 == iota((32, FEAT), 0)))
        mask = flag(iota((LANES, FEAT), 0) // 64 == iota((LANES, FEAT), 1) // 32)
        for index, pick in ((0, same), (1, turned)):
            tall = rounded(dot_nt(pick, proj))
            full = dot(tall, spread) * mask
            span = slice(index * LANES, (index + 1) * LANES)
            self.features[span] = rounded(full)
            self.features_back[:, span] = rounded(full.T)

    def prepare_tokens(self):
        zero = jnp.zeros((16, WID), jnp.bfloat16)
        for molecule in range(MOLS):
            start = molecule * PAD
            self.tokens[pl.ds(start + PAD - 16, 16)] = zero
            self.tokens[pl.ds(start, ROWS)] = self.raw[:, molecule, :]

    def prepare_cotangent(self):
        zero = jnp.zeros((16, WID), jnp.bfloat16)
        keep = iota((ROWS, WID), 0) < self.most()
        for molecule in range(MOLS):
            start = molecule * PAD
            self.grad_down[pl.ds(start + PAD - 16, 16)] = zero
            masked = jnp.where(keep, wide(self.raw[:, molecule, :]), 0.0)
            self.grad_down[pl.ds(start, ROWS)] = rounded(masked)
            self.add_row(B_DOWN, column_sum(masked))

    def prepare_params(self):
        columns = wide(self.small[...].reshape(WID, 128))
        rows = columns.T
        self.params[pl.ds(0, 16)] = rows[0:16]
        lanes = iota((8, WID), 1)
        owner = flag(lanes // 192 == iota((8, WID), 0))
        stacked = jnp.concatenate(
            [jnp.broadcast_to(rows[B_UP + k : B_UP + k + 1], (8, WID)) * owner for k in range(4)], axis=0
        )
        stacked = rounded(stacked)
        spread = jnp.zeros((32, WID), jnp.float32)
        for start in range(0, WID, 128):
            source = start + iota((128, WID), 0)
            pick = rounded(flag(96 * ((source // 24) % 8) + source % 24 == iota((128, WID), 1)))
            spread = spread + dot(stacked[:, start : start + 128], pick)
        total = spread[0:8]
        for k in range(1, 4):
            total = total + pltpu.roll(spread[8 * k : 8 * k + 8], 24 * k, 1)
        self.params[pl.ds(16, 8)] = total

    def norm_one(self):
        gain, bias = self.row(GAIN1), self.row(BIAS1)
        for molecule in range(MOLS):
            rows = pl.ds(molecule * PAD, PAD)
            normed, _ = centred(wide(self.tokens[rows]))
            self.normed_one[rows] = rounded(normed * gain + bias)

    def columns(self, piece, lanes):
        return self.weights[piece, :, :, :, lanes].reshape(WID, LANES)

    def molecules(self):
        return [slice(molecule * PAD, (molecule + 1) * PAD) for molecule in range(MOLS)]

    def attend(self, group):
        lanes = slice(group * LANES, (group + 1) * LANES)
        thin = slice(group * FEAT, (group + 1) * FEAT)
        bias = [self.params[pl.ds(row, 1), lanes] for row in (B_QUERY, B_KEY, B_VALUE)]
        cosines, sines = [jnp.concatenate([table[...]] * 2, axis=1) for table in (self.cosines, self.sines)]
        mask = self.block_mask()
        mask = jnp.concatenate([mask, mask], axis=1)
        ones = jnp.ones((PAD, LANES), jnp.bfloat16)
        weights = square(self.weights, group)
        every = list(enumerate(self.molecules()))
        whole = [dot(self.normed_one[rows], weights) for _, rows in every]
        turned = []
        for index, _ in every:
            for kind in (0, 1):
                value = whole[index][:, kind * LANES : (kind + 1) * LANES] + bias[kind]
                turned.append(jnp.concatenate([rounded(value * cosines), rounded(value * sines)], axis=1))
        lows, levels = [], []
        for index, _ in every:
            value = whole[index][:, 2 * LANES :] + bias[2]
            length = self.lengths[index]
            valid = jnp.where(iota((PAD, LANES), 0) < length, value, 0.0)
            level = column_sum(valid) / wide(jnp.maximum(length, 1))
            levels.append(level)
            lows.append(rounded(value - level))
        feats = [softplus(dot(one, self.features[...])) for one in turned]
        queries = [rounded(feats[2 * index]) for index, _ in every]
        keys = [
            rounded(jnp.where(iota((PAD, FEAT), 0) < self.lengths[index], feats[2 * index + 1], 0.0))
            for index, _ in every
        ]
        states = [
            rounded(dot_tn(keys[index], jnp.concatenate([lows[index], ones], axis=1)) * mask) for index, _ in every
        ]
        both = [dot(queries[index], states[index]) for index, _ in every]
        for index, rows in every:
            level = levels[index]
            mixed = level + (both[index][:, :LANES] - EPS_ATTN * level) / (both[index][:, LANES:] + EPS_ATTN)
            self.mixed[rows, lanes] = rounded(mixed)
            self.feat_query[rows, thin] = queries[index]
            self.feat_key[rows, thin] = keys[index]
            self.values[rows, lanes] = lows[index]
            self.levels[pl.ds(8 * index, 1), lanes] = level

    def middle_rows(self):
        for molecule in range(MOLS):
            rows = slice(molecule * PAD, (molecule + 1) * PAD)
            middle = wide(self.tokens[rows]) + self.row(B_OUT) + dot(self.mixed[rows], square(self.weights, 3))
            self.middle[rows] = middle
            normed, _ = centred(middle)
            self.normed_two[rows] = rounded(normed * self.row(GAIN2) + self.row(BIAS2))

    def up_rows(self, quarter):
        for group in range(GROUPS):
            lanes = slice(group * LANES, (group + 1) * LANES)
            pre = dot(self.normed_two[...], self.columns(4 + quarter, lanes))
            pre = pre + self.params[pl.ds(16 + quarter, 1), lanes]
            squared = pre * pre
            gate = 0.5 + 0.5 * jnp.tanh(pre * (GELU_SCALE + GELU_SCALE * GELU_CUBIC * squared))
            hidden = pre * gate
            slope = gate + (hidden - hidden * gate) * (
                2.0 * GELU_SCALE + 6.0 * GELU_SCALE * GELU_CUBIC * squared
            )
            self.hidden[self.origin + quarter, :, lanes] = rounded(hidden)
            self.slope[self.origin + quarter, :, lanes] = rounded(slope)

    def blocks(self, value):
        return rounded(value).reshape(4, 4, BLK, WID)

    def store_term(self, slot, value):
        self.grads[slot] = self.blocks(value)

    def term_down(self, quarter):
        self.store_term(quarter, dot_tn(self.hidden[self.origin + quarter], self.grad_down[...]))

    def grad_pre_rows(self, quarter):
        for group in range(GROUPS):
            lanes = slice(group * LANES, (group + 1) * LANES)
            grad_hidden = dot_nt(self.grad_down[...], self.weights[8 + quarter].reshape(WID, WID)[lanes])
            grad_pre = rounded(grad_hidden * wide(self.slope[self.origin + quarter, :, lanes]))
            self.slope[self.origin + quarter, :, lanes] = grad_pre
            self.vectors[pl.ds(B_UP + quarter, 1), lanes] += column_sum(wide(grad_pre))

    def term_up(self, quarter):
        self.store_term(4 + quarter, dot_tn(self.normed_two[...], self.slope[self.origin + quarter]))

    def norm_back(self, grad, inputs, gain, bias):
        normed, scale = centred(inputs)
        self.add_row(gain, column_sum(grad * normed))
        self.add_row(bias, column_sum(grad))
        scaled = grad * self.row(gain)
        first = jnp.mean(scaled, axis=-1, keepdims=True)
        second = jnp.mean(scaled * normed, axis=-1, keepdims=True)
        return scale * (scaled - first - normed * second)

    def grad_two_columns(self, group):
        lanes = slice(group * LANES, (group + 1) * LANES)
        whole = dot_nt(self.slope[self.origin + 0], self.weights[4].reshape(WID, WID)[lanes])
        for quarter in range(1, 4):
            whole += dot_nt(self.slope[self.origin + quarter], self.weights[4 + quarter].reshape(WID, WID)[lanes])
        self.grad_middle[:, lanes] = whole

    def grad_middle_rows(self):
        for molecule in range(MOLS):
            rows = slice(molecule * PAD, (molecule + 1) * PAD)
            back = self.norm_back(self.grad_middle[rows], self.middle[rows], GAIN2, BIAS2)
            grad = wide(self.grad_down[rows]) + back
            self.grad_middle[rows] = grad
            low = rounded(grad)
            self.slope[self.origin + 3, rows] = low
            self.add_row(B_OUT, column_sum(wide(low)))

    def term_out(self):
        self.weights[7] = self.blocks(dot_tn(self.mixed[...], self.slope[self.origin + 3]))

    def attend_back(self, group):
        mask = self.block_mask()
        mask = jnp.concatenate([mask, mask], axis=1)
        ones = jnp.ones((PAD, LANES), jnp.bfloat16)
        cosines, sines = [jnp.concatenate([table[...]] * 2, axis=1) for table in (self.cosines, self.sines)]
        thin = slice(group * FEAT, (group + 1) * FEAT)
        lanes = slice(group * LANES, (group + 1) * LANES)
        every = list(enumerate(self.molecules()))
        queries = [self.feat_query[rows, thin] for _, rows in every]
        keys = [self.feat_key[rows, thin] for _, rows in every]
        values = [jnp.concatenate([self.values[rows, lanes], ones], axis=1) for _, rows in every]
        grad_mixed = dot_nt(self.slope[self.origin + 3], self.weights[3].reshape(WID, WID)[lanes])
        states = [rounded(dot_tn(keys[index], values[index]) * mask) for index, _ in every]
        both = [dot(queries[index], states[index]) for index, _ in every]
        grads = []
        for index, rows in every:
            inverse = 1.0 / (both[index][:, LANES:] + EPS_ATTN)
            grad_num = grad_mixed[rows] * inverse
            offset = EPS_ATTN * self.levels[pl.ds(8 * index, 1), lanes]
            grad_den = -grad_num * ((both[index][:, :LANES] - offset) * inverse)
            grads.append(jnp.concatenate([rounded(grad_num), rounded(grad_den)], axis=1))
        grad_states = [rounded(dot_tn(queries[index], grads[index]) * mask) for index, _ in every]
        grad_queries = [dot_nt(grads[index], states[index]) for index, _ in every]
        grad_keys = [dot_nt(values[index], grad_states[index]) for index, _ in every]
        grad_values = [rounded(dot(keys[index], grad_states[index][:, :LANES])) for index, _ in every]
        for index, rows in every:
            self.slope[self.origin + group, rows, 2 * LANES : 3 * LANES] = grad_values[index]
        self.vectors[pl.ds(B_VALUE, 1), lanes] += sum(column_sum(wide(value)) for value in grad_values)
        for slot, row, feats, grads in ((0, B_QUERY, queries, grad_queries), (1, B_KEY, keys, grad_keys)):
            turned = [
                dot(rounded(grads[index] * softplus_slope(wide(feats[index]))), self.features_back[...])
                for index, _ in every
            ]
            lows = [rounded(cosines * one[:, :LANES] + sines * one[:, LANES:]) for one in turned]
            for index, rows in every:
                self.slope[self.origin + group, rows, slot * LANES : (slot + 1) * LANES] = lows[index]
            self.vectors[pl.ds(row, 1), lanes] += sum(column_sum(wide(low)) for low in lows)

    def term_square(self, group):
        self.weights[4 + (2, 0, 1)[group]] = self.blocks(dot_tn(self.normed_one[...], self.slope[self.origin + group]))

    def grad_token_rows(self, first):
        pair = pl.ds(first * PAD, 2 * PAD)
        whole = dot_nt(self.slope[self.origin + 0, pair], square(self.weights, 0))
        for index in (1, 2):
            whole += dot_nt(self.slope[self.origin + index, pair], square(self.weights, index))
        for molecule in (first, first + 1):
            rows = slice(molecule * PAD, (molecule + 1) * PAD)
            own = whole[(molecule - first) * PAD : (molecule - first + 1) * PAD]
            grad = self.grad_middle[rows] + self.norm_back(own, wide(self.tokens[rows]), GAIN1, BIAS1)
            self.raw[:, molecule, :] = rounded(grad[:ROWS])

    def most(self):
        lengths = self.lengths
        return jnp.maximum(jnp.maximum(lengths[0], lengths[1]), jnp.maximum(lengths[2], lengths[3]))

    def layer_out_rows(self, molecule):
        rows = pl.ds(molecule * PAD, PAD)
        result = self.middle[rows] + self.row(B_DOWN)
        for quarter in range(4):
            result += dot(self.hidden[self.origin + quarter, rows], square(self.weights, 8 + quarter))
        keep = iota((ROWS, WID), 0) < self.most()
        self.raw[:, molecule, :] = rounded(jnp.where(keep, result[:ROWS], 0.0))


LAYER_SCRATCH = dict(
    raw=((ROWS, MOLS, WID), jnp.bfloat16),
    tokens=((TOTAL, WID), jnp.bfloat16),
    grad_down=((TOTAL, WID), jnp.bfloat16),
    normed_one=((TOTAL, WID), jnp.bfloat16),
    values=((TOTAL, WID), jnp.bfloat16),
    mixed=((TOTAL, WID), jnp.bfloat16),
    normed_two=((TOTAL, WID), jnp.bfloat16),
    feat_query=((TOTAL, HALF), jnp.bfloat16),
    feat_key=((TOTAL, HALF), jnp.bfloat16),
    levels=((8 * MOLS, WID), jnp.float32),
    middle=((TOTAL, WID), jnp.float32),
    grad_middle=((TOTAL, WID), jnp.float32),
    hidden=((4, TOTAL, WID), jnp.bfloat16),
    slope=((4, TOTAL, WID), jnp.bfloat16),
    features=((2 * LANES, FEAT), jnp.bfloat16),
    features_back=((FEAT, 2 * LANES), jnp.bfloat16),
    params=((24, WID), jnp.float32),
    vectors=((16, WID), jnp.float32),
    grads=((8, 4, 4, BLK, WID), jnp.bfloat16),
    weights=((12, 4, 4, BLK, WID), jnp.bfloat16),
    small=((4, 4, BLK, 128), jnp.bfloat16),
)


VMEM = pl.BlockSpec(memory_space=pltpu.VMEM)
SMEM = pl.BlockSpec(memory_space=pltpu.SMEM)
ANY = pl.BlockSpec(memory_space=pl.ANY)
SEMS = 320


COMM_SCRATCH = dict(
    pair=((2, 4, 4, BLK, HALF), jnp.bfloat16),
    big=((3, 2, 3, 4, BLK, HALF), jnp.bfloat16),
    little=((3, 2, 3, BLK, HALF), jnp.bfloat16),
    cross=((3, 2, 4, BLK, HALF), jnp.bfloat16),
    total=((4, 2, BLK, HALF), jnp.float32),
    square_sum=((4, 24, WID), jnp.float32),
    up_sum=((24, 4 * WID), jnp.float32),
    down_sum=((2 * BLK, WID), jnp.float32),
    vector_land=((4, 4, 16, WID), jnp.float32),
    narrow=((16, 128), jnp.float32),
    small_mine=((BLK, 128), jnp.float32),
)
def layer_kernel(
    lengths, queries, keys, values, outs, ups, downs, feature_ref, cosines, sines, *rest,
):
    vectors_in, rest = rest[:10], rest[10:]
    tokens_in, cot_in, layer_out, tokens_out, square_out, up_out, down_out, narrow_out = rest[:8]
    scratch = rest[8:]
    names = list(LAYER_SCRATCH) + list(COMM_SCRATCH)
    refs = dict(zip(names, scratch))
    send_sems, recv_sems, local_sems, pair_gates, land_gates = scratch[len(names):]
    net = Net(send_sems, recv_sems)
    work = Layer(
        lengths=lengths, feature_ref=feature_ref, cosines=cosines, sines=sines,
        **{name: refs[name] for name in LAYER_SCRATCH},
    )
    work.origin = net.x // RING
    load_tokens = pltpu.make_async_copy(tokens_in, work.raw, local_sems.at[0])
    load_cot = pltpu.make_async_copy(cot_in, work.raw, local_sems.at[1])
    load_tokens.start()
    net.greet()

    shards = (queries, keys, values, outs, ups, downs, vectors_in)
    load = load_shards(
        net, work.weights, work.small, work.grad_middle, refs["small_mine"], refs["narrow"], shards
    )
    small = gather_small(net, work.small)
    get = [gather_steps(net, work.weights, part, side) for part in (0, 1, 2) for side in (0, 1)]

    def go(*steps):
        for step in steps:
            next(step, None)

    def reduce(order, part, side, result):
        lands = [
            (
                refs["big"].at[order % 3, way],
                refs["little"].at[order % 3, way],
                refs["cross"].at[order % 3, way],
            )
            for way in WAYS
        ]
        gates = (
            pair_gates.at[order - 1] if order >= 1 else None,
            pair_gates.at[order] if order < 5 else None,
            land_gates.at[order - 3] if order >= 3 else None,
            land_gates.at[order] if order < 3 else None,
        )
        return reduce_steps(
            net, work.weights if part == 0 else work.grads, 4 * (part < 2), part, side, refs["pair"], lands, gates,
            refs["total"].at[order - 2] if order >= 2 else None, refs[result],
        )

    down = [reduce(0, 2, 0, "down_sum"), reduce(1, 2, 1, "down_sum")]
    up = [reduce(2, 1, 0, "up_sum"), reduce(3, 1, 1, "up_sum")]
    value, query = reduce(4, 0, 1, "square_sum"), reduce(5, 0, 0, "square_sum")
    vectors = vector_steps(net, work.vectors, refs["vector_land"])

    work.vectors[...] = jnp.zeros_like(work.vectors)
    write_tokens = pltpu.make_async_copy(work.raw, tokens_out, local_sems.at[0])
    write_layer = pltpu.make_async_copy(work.raw, layer_out, local_sems.at[1])
    go(load)
    load_tokens.wait()
    work.prepare_tokens()
    load_cot.start()
    go(load, get[0], load, small, get[5], load, get[1], load, get[2], get[3], small, get[0], get[1], get[3], small, get[2], get[4])
    work.prepare_params()
    go(get[0])
    work.norm_one()
    work.prepare_features()
    go(get[0])
    load_cot.wait()
    work.prepare_cotangent()
    work.attend(0)
    go(get[1])
    work.attend(1)
    go(get[1])
    work.attend(2)
    go(get[3], get[5])
    work.middle_rows()
    go(get[3])
    work.up_rows(3)
    work.term_down(3)
    go(get[2])
    work.up_rows(2)
    work.term_down(2)
    go(get[4], get[2])
    work.up_rows(0)
    work.term_down(0)
    work.up_rows(1)
    work.term_down(1)
    go(down[0], get[5], down[0], get[4], down[1], get[5], get[4])
    work.grad_pre_rows(0)
    work.term_up(0)
    go(down[1])
    work.grad_pre_rows(1)
    work.term_up(1)
    go(up[0])
    work.grad_pre_rows(3)
    go(down[0])
    work.grad_pre_rows(2)
    work.grad_two_columns(2)
    go(up[0])
    work.grad_two_columns(1)
    work.term_up(3)
    go(down[0])
    work.term_up(2)
    go(up[1], down[1])
    work.grad_two_columns(0)
    work.grad_middle_rows()
    work.attend_back(2)
    go(down[0], up[0], down[1])
    work.attend_back(0)
    go(up[1])
    work.term_out()
    work.term_square(0)
    go(value, down[1], up[0])
    work.attend_back(1)
    go(value)
    work.term_square(1)
    work.term_square(2)
    go(query, up[0], up[1], query)
    work.grad_token_rows(0)
    work.grad_token_rows(2)
    write_tokens.start()
    go(vectors, value, vectors, up[0], up[1], query, value, vectors)
    write_tokens.wait()
    work.layer_out_rows(0)
    go(query, down[0])
    work.layer_out_rows(1)
    go(vectors)
    work.layer_out_rows(2)
    work.layer_out_rows(3)
    write_layer.start()
    go(value, up[1], query, vectors, value, up[1], down[1], query)
    total = refs["vector_land"][0, 1]
    place = net.y * 8 + net.z * 2 + net.c
    narrow = refs["narrow"]
    turned = pltpu.roll(total, WID - 24 * place, 1)
    narrow[...] = turned[:, :128]
    chosen = refs["vector_land"][0, 1, pl.ds(B_UP + place // 8, 1)]
    narrow[pl.ds(B_UP, 1)] = pltpu.roll(chosen, WID - 96 * (place % 8), 1)[:, :128]
    writes = [
        pltpu.make_async_copy(refs[name], ref, local_sems.at[2 + slot])
        for slot, (name, ref) in enumerate(
            (("square_sum", square_out), ("up_sum", up_out), ("down_sum", down_out), ("narrow", narrow_out))
        )
    ]
    for write in writes:
        write.start()
    for write in [write_layer] + writes:
        write.wait()


def layer_call(*operands):
    bf, ff = jnp.bfloat16, jnp.float32
    scratch = list(LAYER_SCRATCH.values()) + list(COMM_SCRATCH.values())
    return pl.pallas_call(
        layer_kernel,
        out_shape=(
            jax.ShapeDtypeStruct((ROWS, MOLS, WID), bf),
            jax.ShapeDtypeStruct((ROWS, MOLS, WID), bf),
            jax.ShapeDtypeStruct((4, 24, WID), ff),
            jax.ShapeDtypeStruct((24, 4 * WID), ff),
            jax.ShapeDtypeStruct((2 * BLK, WID), ff),
            jax.ShapeDtypeStruct((16, 128), ff),
        ),
        in_specs=[SMEM] + [VMEM] * 19 + [ANY] * 2,
        out_specs=(ANY,) * 6,
        scratch_shapes=[pltpu.VMEM(shape, dtype) for shape, dtype in scratch]
        + [
            pltpu.SemaphoreType.DMA((SEMS,)),
            pltpu.SemaphoreType.DMA((SEMS,)),
            pltpu.SemaphoreType.DMA((6,)),
            pltpu.SemaphoreType.REGULAR((5,)),
            pltpu.SemaphoreType.REGULAR((3,)),
        ],
        compiler_params=pltpu.CompilerParams(
            collective_id=0, has_side_effects=True, vmem_limit_bytes=64 * 2**20 - 2**17
        ),
    )(*operands)


def finish_kernel(layer, tokens, square, up, down, narrow, *outs):
    outs[0][...] = layer[...]
    outs[1][...] = tokens[...]
    for group, index in ((0, 2), (1, 0), (2, 1)):
        for kind, slot in enumerate((4, 6, 8)):
            outs[slot][:, group * LANES : (group + 1) * LANES] = square[index, :, kind * LANES : (kind + 1) * LANES]
    outs[10][...] = square[3]
    outs[14][...] = up[...]
    outs[16][...] = down[...]
    for index, slot in enumerate((2, 3, 5, 7, 9, 11, 12, 13, 17)):
        outs[slot][...] = narrow[index, 0:24]
    outs[15][...] = narrow[9, 0:96]


def finish_call(*sums):
    bf, ff = jnp.bfloat16, jnp.float32
    tokens, thin, wide_one = ((ROWS, MOLS, WID), bf), ((24,), ff), ((24, WID), ff)
    shapes = [tokens, tokens, thin, thin] + [wide_one, thin] * 4 + [thin, thin]
    shapes += [((24, 4 * WID), ff), ((96,), ff), ((96, WID), ff), thin]
    return pl.pallas_call(
        finish_kernel,
        out_shape=[jax.ShapeDtypeStruct(shape, dtype) for shape, dtype in shapes],
        in_specs=[VMEM] * 6,
        out_specs=[VMEM] * 18,
    )(*sums)


def angle_tables():
    positions = np.arange(PAD)[:, None]
    angles = positions * 10000.0 ** (-2.0 * (np.arange(128)[None, :] % 32) / 64)
    return np.cos(angles).astype(np.float32), np.sin(angles).astype(np.float32)


def body(
    tokens, lengths, feature_proj, ln1_gain, ln1_bias, w_query, b_query, w_key, b_key, w_value, b_value,
    w_out, b_out, ln2_gain, ln2_bias, w_up, b_up, w_down, b_down, cotangent,
):
    cosines, sines = angle_tables()
    sums = layer_call(
        lengths, w_query, w_key, w_value, w_out, w_up, w_down, feature_proj.T, jnp.asarray(cosines), jnp.asarray(sines),
        ln1_gain, ln1_bias, b_query, b_key, b_value, b_out, ln2_gain, ln2_bias, b_down, b_up,
        tokens.transpose(1, 0, 2), cotangent.transpose(1, 0, 2),
    )
    done = finish_call(*sums)
    return (done[0].transpose(1, 0, 2), done[1].transpose(1, 0, 2)) + tuple(done[2:])


def solution(mesh):
    rows, flat = P("fsdp", None), P("fsdp")
    mols = P(("fsdp", "dp"), None, None)
    pairs = (flat, flat, rows, flat, rows, flat, rows, flat, rows, flat, flat, flat, rows, flat, rows, flat)
    return jax.shard_map(
        body,
        mesh=mesh,
        in_specs=(mols, P(("fsdp", "dp")), P()) + pairs + (mols,),
        out_specs=(mols, mols) + pairs,
        check_vma=False,
    )
```
